32 devices in a mesh: batch: 16 (over z, y, x), seq: 2 (over core).
Axes of the slice: x: 2, y: 2, z: 4, core: 2. Of those that a mesh axis runs over, the one named last changes fastest.
Arguments:
- cls_input: bfloat16 [64, 768], P('batch'), may hold values from -6 to 6
- patch_input: bfloat16 [64, 196, 768], P('batch', 'seq'), may hold values from -6 to 6
- task_ids: int32 [64], P('batch'), may hold values from 0 to 15
- prompts: bfloat16 [16, 2, 50, 768], replicated, may hold values from -6 to 6
- attn_weight: bfloat16 [2, 768, 2304], replicated, may hold values from -0.21875 to 0.21875
- attn_bias: bfloat16 [2, 2304], replicated, may hold values from -3 to 3
- out_weight: bfloat16 [2, 768, 768], replicated, may hold values from -0.625 to 0.625
- out_bias: bfloat16 [2, 768], replicated, may hold values from -3 to 3
- up_weight: bfloat16 [2, 768, 3072], replicated, may hold values from -0.21875 to 0.21875
- up_bias: bfloat16 [2, 3072], replicated, may hold values from -3 to 3
- down_weight: bfloat16 [2, 3072, 768], replicated, may hold values from -0.15625 to 0.15625
- down_bias: bfloat16 [2, 768], replicated, may hold values from -3 to 3
- norm_gain: float32 [2, 2, 768], replicated, may hold values from 0.1 to 1.9
- norm_bias: float32 [2, 2, 768], replicated, may hold values from -3 to 3
- final_gain: float32 [768], replicated, may hold values from 0.1 to 1.9
- final_bias: float32 [768], replicated, may hold values from -3 to 3
- head_weight: bfloat16 [768, 16, 100], replicated, may hold values from -0.21875 to 0.21875
- head_bias: bfloat16 [16, 100], replicated, may hold values from -4 to 4
- cls_cotangent: bfloat16 [64, 768], P('batch'), may hold values from -6 to 6
- patch_cotangent: bfloat16 [64, 196, 768], P('batch', 'seq'), may hold values from -6 to 6
- logit_cotangent: bfloat16 [64, 100], P('batch'), may hold values from -6 to 6
Outputs:
- cls_output: bfloat16 [64, 768], P('batch')
- patch_output: bfloat16 [64, 196, 768], P('batch', 'seq')
- logits: bfloat16 [64, 100], P('batch')
- cls_grad: float32 [64, 768], P('batch')
- patch_grad: float32 [64, 196, 768], P('batch', 'seq')
- prompt_grad: float32 [16, 2, 50, 768], replicated
- head_weight_grad: float32 [768, 16, 100], replicated
- head_bias_grad: float32 [16, 100], replicated
The draws below stay inside these ranges and needn't reach their ends.
All inputs are finite; a program needn't handle non-finite values.
Results may differ from the reference program's by a relative error of at most 0.018.
Values may be sent and summed in bfloat16 or wider, within the bound.
A program may use at most 192 MiB of HBM per device.

```python
import math
import jax
import jax.numpy as jnp
import numpy as np
from jax import lax

D = 768
HEADS = 12
HEAD_DIM = 64
FF = 3072
PATCHES = 196
PROMPTS = 50
CLASSES = 100
TASKS = 16
LAYERS = 2
IMAGES = 64


def plant(result, key, least, largest):
    shape = result.shape
    place = [jax.random.randint(jax.random.fold_in(key, axis), (), 0, shape[axis]) for axis in range(len(shape))]
    result = result.at[tuple(place)].set(least)
    longest = shape.index(max(shape))
    place[longest] = (place[longest] + 1) % shape[longest]
    return result.at[tuple(place)].set(largest)


def block_levels(key, dims, cuts, low, largest):
    factor_of, own = 1.0, jax.random.fold_in(key, 6)
    for axis_at, shards_of in cuts:
        draws = jnp.exp(jax.random.uniform(jax.random.fold_in(own, axis_at), (shards_of,), jnp.float32, low / len(cuts), largest / len(cuts)))
        factor_of = factor_of * jnp.repeat(draws, dims[axis_at] // shards_of).reshape([-1 if axis == axis_at else 1 for axis in range(len(dims))])
    return factor_of


def cumulative_ranks(amount, skew):
    weights = [(1 << 20) // math.isqrt(grade ** skew) + 1 for grade in range(1, amount + 1)]
    width = 1 + sum(weights) // (1 << 30)
    return np.cumsum(np.array([max(1, weight // width) for weight in weights]))


def skewed_ids(rng, extent, amount, skew):
    listing = cumulative_ranks(amount, skew)
    pick = jax.random.randint(jax.random.fold_in(rng, 1), extent, 0, int(listing[amount - 1]))
    grade = jnp.searchsorted(jnp.asarray(listing, jnp.int32), pick, side="right")
    return jax.random.permutation(jax.random.fold_in(rng, 2), amount)[grade].astype(jnp.int32)


def normal_values(stream_key, shape, scale, most, shards=(), held_as=jnp.bfloat16):
    array = scale * jax.random.normal(stream_key, shape, jnp.float32)
    if shards:
        array = array * block_levels(stream_key, shape, shards, -0.22, 0.18)
    return jnp.clip(array, -most, most).astype(held_as)


def setup_inputs(seed: int = 0) -> dict:
    arg_keys = jax.random.split(jax.random.key(seed), 22)
    cls_input = normal_values(arg_keys[0], (IMAGES, D), 1.0, 6.0, ((0, 16),))
    patch_input = normal_values(arg_keys[1], (IMAGES, PATCHES, D), 1.0, 6.0, ((0, 16), (1, 2)))
    task_ids = plant(skewed_ids(arg_keys[2], (IMAGES,), TASKS, 2), jax.random.fold_in(arg_keys[2], 3), 0, TASKS - 1).astype(jnp.int32)
    prompts = normal_values(arg_keys[3], (TASKS, LAYERS, PROMPTS, D), 1.0, 6.0)
    attn_weight = normal_values(arg_keys[4], (LAYERS, D, 3 * D), D ** -0.5, 0.21875)
    attn_bias = normal_values(arg_keys[5], (LAYERS, 3 * D), 0.3, 3.0)
    out_weight = normal_values(arg_keys[6], (LAYERS, D, D), (D // 8) ** -0.5, 0.625)
    out_bias = normal_values(arg_keys[7], (LAYERS, D), 0.3, 3.0)
    up_weight = normal_values(arg_keys[8], (LAYERS, D, FF), D ** -0.5, 0.21875)
    up_bias = normal_values(arg_keys[9], (LAYERS, FF), 0.3, 3.0)
    down_weight = normal_values(arg_keys[10], (LAYERS, FF, D), (FF // 2) ** -0.5, 0.15625)
    down_bias = normal_values(arg_keys[11], (LAYERS, D), 0.3, 3.0)
    norm_gain = jnp.clip(1.0 + 0.18 * jax.random.normal(arg_keys[12], (LAYERS, 2, D), jnp.float32), 0.1, 1.9)
    norm_bias = normal_values(arg_keys[13], (LAYERS, 2, D), 0.3, 3.0, (), jnp.float32)
    final_gain = jnp.clip(1.0 + 0.18 * jax.random.normal(arg_keys[14], (D,), jnp.float32), 0.1, 1.9)
    final_bias = normal_values(arg_keys[15], (D,), 0.3, 3.0, (), jnp.float32)
    head_weight = normal_values(arg_keys[16], (D, TASKS, CLASSES), D ** -0.5, 0.21875)
    head_bias = normal_values(arg_keys[17], (TASKS, CLASSES), 1.0, 4.0)
    cls_cotangent = normal_values(arg_keys[18], (IMAGES, D), 1.0, 6.0, ((0, 16),))
    patch_cotangent = normal_values(arg_keys[19], (IMAGES, PATCHES, D), 1.0, 6.0, ((0, 16), (1, 2)))
    logit_cotangent = normal_values(arg_keys[20], (IMAGES, CLASSES), 1.0, 6.0, ((0, 16),))
    return dict(cls_input=cls_input, patch_input=patch_input, task_ids=task_ids, prompts=prompts, attn_weight=attn_weight, attn_bias=attn_bias, out_weight=out_weight, out_bias=out_bias, up_weight=up_weight, up_bias=up_bias, down_weight=down_weight, down_bias=down_bias, norm_gain=norm_gain, norm_bias=norm_bias, final_gain=final_gain, final_bias=final_bias, head_weight=head_weight, head_bias=head_bias, cls_cotangent=cls_cotangent, patch_cotangent=patch_cotangent, logit_cotangent=logit_cotangent)


EPSILON = 1e-06
HIGH = lax.Precision.HIGHEST

@jax.custom_vjp
def low(v):
    return lax.optimization_barrier(v.astype(jnp.bfloat16)).astype(jnp.float32)

@jax.custom_vjp
def low_back(v):
    return v

def low_keep(v):
    return (low(v), None)

def low_pass(kept, grad):
    return (grad,)

def back_keep(v):
    return (v, None)

def back_low(kept, grad):
    return (low(grad),)
low.defvjp(low_keep, low_pass)
low_back.defvjp(back_keep, back_low)

def normalize(values_in, gain, shift):
    center = values_in - lax.optimization_barrier(jnp.mean(values_in, -1, keepdims=True))
    spread = lax.optimization_barrier(jnp.mean(center * center, -1, keepdims=True))
    return center * lax.rsqrt(spread + EPSILON) * gain + shift

def matmul(matrix, other):
    return jnp.dot(matrix, other, precision=HIGH)

def block(tokens, prompt_rows, params):
    attn_weight, attn_bias, out_weight, out_bias, up_weight, up_bias, down_weight, down_bias, gains, shifts = params
    model_width = tokens.shape[-1]
    prompt_count = prompt_rows.shape[0]
    joined = jnp.concatenate([tokens[:1], prompt_rows, tokens[1:]], 0)
    normed = low(normalize(joined, gains[0], shifts[0]))
    projected = low_back(low(matmul(normed, attn_weight) + attn_bias))
    queries = jnp.concatenate([projected[:1, :model_width], projected[1 + prompt_count:, :model_width]], 0)
    queries = queries.reshape(-1, HEADS, HEAD_DIM)
    key_rows = projected[:, model_width:2 * model_width].reshape(-1, HEADS, HEAD_DIM)
    value_rows = projected[:, 2 * model_width:].reshape(-1, HEADS, HEAD_DIM)
    scores = low_back(jnp.einsum('qhd,khd->hqk', queries, key_rows, precision=HIGH) * HEAD_DIM ** (-0.5))
    weights = low(jax.nn.softmax(scores, axis=-1))
    mixed_heads = jnp.einsum('hqk,khd->qhd', weights, value_rows, precision=HIGH).reshape(-1, model_width)
    mixed_heads = low_back(low(mixed_heads))
    midway = tokens + low_back(matmul(mixed_heads, out_weight) + out_bias)
    normed_mid = low(normalize(midway, gains[1], shifts[1]))
    hidden_pre = low_back(matmul(normed_mid, up_weight) + up_bias)
    activated = low(jax.nn.gelu(hidden_pre, approximate=False))
    return midway + low_back(matmul(activated, down_weight) + down_bias)

def reference(cls_input, patch_input, task_ids, prompts, attn_weight, attn_bias, out_weight, out_bias, up_weight, up_bias, down_weight, down_bias, norm_gain, norm_bias, final_gain, final_bias, head_weight, head_bias, cls_cotangent, patch_cotangent, logit_cotangent):
    frozen_layers = jax.tree.map(lambda entry: entry.astype(jnp.float32), (attn_weight, attn_bias, out_weight, out_bias, up_weight, up_bias, down_weight, down_bias, norm_gain, norm_bias))
    final_gain32 = final_gain.astype(jnp.float32)
    final_bias32 = final_bias.astype(jnp.float32)
    onehot = (task_ids[:, None] == jnp.arange(TASKS, dtype=jnp.int32)[None, :]).astype(jnp.float32)

    def forward(cls_rows, patch_rows, prompt_table, head_matrix, head_shift):

        def one_image(cls_row, patch_block, task):
            tokens = jnp.concatenate([cls_row[None], patch_block], 0)
            for depth in range(LAYERS):
                params = jax.tree.map(lambda entry: entry[depth], frozen_layers)
                tokens = block(tokens, prompt_table[task, depth], params)
            return tokens
        tokens = jax.vmap(one_image)(cls_rows, patch_rows, task_ids)
        features = low(normalize(tokens[:, 0], final_gain32, final_bias32))
        all_logits = jnp.einsum('id,dtc->itc', features, head_matrix, precision=HIGH)
        logits = low_back(lax.optimization_barrier(jnp.sum(all_logits * onehot[:, :, None], 1)) + matmul(onehot, head_shift))
        return (tokens[:, 0], tokens[:, 1:], logits)
    outputs, pullback = jax.vjp(forward, cls_input.astype(jnp.float32), patch_input.astype(jnp.float32), prompts.astype(jnp.float32), head_weight.astype(jnp.float32), head_bias.astype(jnp.float32))
    grads = pullback((cls_cotangent.astype(jnp.float32), patch_cotangent.astype(jnp.float32), logit_cotangent.astype(jnp.float32)))
    return (outputs[0].astype(jnp.bfloat16), outputs[1].astype(jnp.bfloat16), outputs[2].astype(jnp.bfloat16), grads[0], grads[1], grads[2], grads[3], grads[4])
```

```python
import jax
import jax.numpy as jnp
from jax import lax
from jax.experimental import pallas as pl
from jax.experimental.pallas import tpu as pltpu
from jax.sharding import PartitionSpec as P

HEADS = 12
HEAD_DIM = 64
LAYERS = 2
EPSILON = 1e-06
BF = jnp.bfloat16
F32 = jnp.float32

JOINT = 256
QUERY = 208
PROMPT_AT = 200
PAIR = 2 * HEAD_DIM
PAIRS = HEADS // 2
CHUNK = 32
HIDDEN_TILE = 512

NN = (((1,), (0,)), ((), ()))
NT = (((1,), (1,)), ((), ()))
TN = (((0,), (0,)), ((), ()))


def dot(left, right, dims):
    return lax.dot_general(left, right, dims, preferred_element_type=F32)


def gelu_and_slope(u):
    phi = 0.5 + 0.5 * lax.erf(u * 0.7071067811865476)
    return u * phi, phi + u * (0.3989422804014327 * jnp.exp(-0.5 * u * u))


def norm_parts(x):
    center = x - jnp.mean(x, -1, keepdims=True)
    inverse = lax.rsqrt(jnp.mean(center * center, -1, keepdims=True) + EPSILON)
    return center * inverse, inverse


def norm_back(grad, gain, unit, inverse):
    scaled = grad * gain
    first = jnp.mean(scaled, -1, keepdims=True)
    second = jnp.mean(scaled * unit, -1, keepdims=True)
    return inverse * (scaled - first - unit * second)


def pick_row(ref, index):
    values = ref[...].astype(F32)
    rows = lax.broadcasted_iota(jnp.int32, values.shape, 0)
    return jnp.sum(jnp.where(rows == index, values, 0.0), 0, keepdims=True)


def encoder_kernel(
    own, patches, prompt_count,
    patch_own, patch_other, cls_in, cot_own, cot_other, cls_cot, logit_cot,
    prompts, head, head_bias, attn_bias, out_bias, up_bias, down_bias, gains, shifts, final_gain, final_bias,
    attn_hbm, out_hbm, up_hbm, down_hbm,
    y_own, y_other, y_cls, logits, dx_own, dx_other, dx_cls, prompt_out, features_out,
    attn_w, out_w, up_w, down_w, x_ref, m_ref, t_ref, dx_ref, a_ref, o_ref, g_ref, dqkv_ref,
    qkv, probs, slope, unit1, unit2, inv1, inv2, sems,
):
    half = patches // 2
    cls_at = patches
    width = x_ref.shape[1]
    hidden = up_w.shape[2]
    first = lax.axis_index("seq") * own

    copies = {}
    for layer in range(LAYERS):
        for k, (src, dst) in enumerate(((attn_hbm, attn_w), (out_hbm, out_w), (up_hbm, up_w), (down_hbm, down_w))):
            pltpu.make_async_copy(src.at[layer], dst.at[layer], sems.at[k, layer]).start()

    def arrived(k, src, dst, layer):
        pltpu.make_async_copy(src.at[layer], dst.at[layer], sems.at[k, layer]).wait()

    lane = lax.broadcasted_iota(jnp.int32, (1, PAIR), 1)
    is_low = lane < HEAD_DIM
    column = lax.broadcasted_iota(jnp.int32, (1, JOINT), 1)
    is_key = (column <= cls_at) | ((column >= PROMPT_AT) & (column < PROMPT_AT + prompt_count))
    key_bias = jnp.where(is_key, 0.0, -1e30).astype(F32)

    def stack_pair(block):
        zero = jnp.zeros_like(block)
        return jnp.concatenate([jnp.where(is_low, block, zero), jnp.where(is_low, zero, block)], 0)

    def merge_pair(block):
        return jnp.where(is_low, block[:QUERY], block[QUERY:])

    for i in range(own):
        at = i * JOINT
        x_ref[at : at + JOINT] = jnp.zeros((JOINT, width), F32)
        x_ref[at : at + half] = patch_own[first + i].astype(F32)
        x_ref[at + half : at + patches] = patch_other[i].astype(F32)
        x_ref[at + cls_at : at + cls_at + 1] = pick_row(cls_in, first + i)
        dqkv_ref[at + QUERY : at + JOINT, :width] = jnp.zeros((JOINT - QUERY, width), BF)

    def forward(layer, carry):
        for i in range(own):
            at = i * JOINT + PROMPT_AT
            x_ref[at : at + prompt_count] = prompts[i, layer].astype(F32)
        gain, shift = gains[layer, 0:1], shifts[layer, 0:1]
        for r in range(0, own * JOINT, CHUNK):
            unit, inverse = norm_parts(x_ref[r : r + CHUNK])
            unit1[layer, r : r + CHUNK] = unit.astype(BF)
            inv1[layer, r : r + CHUNK] = inverse
            a_ref[r : r + CHUNK] = (unit * gain + shift).astype(BF)
        arrived(0, attn_hbm, attn_w, layer)
        bias = pick_row(attn_bias, layer)
        for n in range(3):
            part = slice(n * width, (n + 1) * width)
            qkv[layer, :, part] = (dot(a_ref[...], attn_w[layer, :, part], NN) + bias[:, part]).astype(BF)
        for i in range(own):
            at = i * JOINT
            for h in range(PAIRS):
                lanes = slice(h * PAIR, (h + 1) * PAIR)
                query = stack_pair(qkv[layer, at : at + QUERY, lanes])
                keys = qkv[layer, at : at + JOINT, width + h * PAIR : width + (h + 1) * PAIR]
                values = qkv[layer, at : at + JOINT, 2 * width + h * PAIR : 2 * width + (h + 1) * PAIR]
                scores = dot(query, keys, NT) * HEAD_DIM**-0.5 + key_bias
                expo = jnp.exp(scores - jnp.max(scores, -1, keepdims=True))
                prob = (expo * (1.0 / jnp.sum(expo, -1, keepdims=True))).astype(BF)
                probs[layer, i * PAIRS + h] = prob
                o_ref[i * QUERY : (i + 1) * QUERY, lanes] = merge_pair(dot(prob, values, NN)).astype(BF)
        arrived(1, out_hbm, out_w, layer)
        mixed = dot(o_ref[...], out_w[layer], NN) + pick_row(out_bias, layer)
        for i in range(own):
            m_ref[i * QUERY : (i + 1) * QUERY] = x_ref[i * JOINT : i * JOINT + QUERY] + mixed[i * QUERY : (i + 1) * QUERY]
        gain, shift = gains[layer, 1:2], shifts[layer, 1:2]
        for r in range(0, own * QUERY, CHUNK):
            unit, inverse = norm_parts(m_ref[r : r + CHUNK])
            unit2[layer, r : r + CHUNK] = unit.astype(BF)
            inv2[layer, r : r + CHUNK] = inverse
            a_ref[r : r + CHUNK] = (unit * gain + shift).astype(BF)
        arrived(2, up_hbm, up_w, layer)
        bias = pick_row(up_bias, layer)
        for c in range(0, hidden, HIDDEN_TILE):
            part = slice(c, c + HIDDEN_TILE)
            act, act_slope = gelu_and_slope(dot(a_ref[: own * QUERY], up_w[layer, :, part], NN) + bias[:, part])
            g_ref[:, part] = act.astype(BF)
            slope[layer, :, part] = act_slope.astype(BF)
        arrived(3, down_hbm, down_w, layer)
        result = m_ref[...] + (dot(g_ref[...], down_w[layer], NN) + pick_row(down_bias, layer))
        for i in range(own):
            x_ref[i * JOINT : i * JOINT + QUERY] = result[i * QUERY : (i + 1) * QUERY]
        return carry

    lax.fori_loop(0, LAYERS, forward, 0)

    for i in range(own):
        at, to = i * JOINT, i * QUERY
        y_own[i] = x_ref[at : at + half].astype(BF)
        y_other[i] = x_ref[at + half : at + patches].astype(BF)
        row = x_ref[at + cls_at : at + cls_at + 1]
        y_cls[i] = row
        unit, inverse = norm_parts(row)
        feature = (unit * final_gain[...] + final_bias[...]).astype(BF)
        features_out[i] = feature.astype(F32)
        classes = head.shape[2]
        eight = jnp.broadcast_to(feature, (8, width))
        logits[i] = dot(eight, head[i], NN)[:1] + head_bias[i : i + 1]
        cot = jnp.broadcast_to(pick_row(logit_cot, first + i).astype(BF), (8, classes))
        grad = dot(cot, head[i], NT)[:1]
        dx_ref[to + cls_at : to + QUERY] = jnp.zeros((QUERY - cls_at, width), F32)
        dx_ref[to : to + half] = cot_own[first + i].astype(F32)
        dx_ref[to + half : to + patches] = cot_other[i].astype(F32)
        dx_ref[to + cls_at : to + cls_at + 1] = pick_row(cls_cot, first + i) + norm_back(
            grad, final_gain[...], unit, inverse
        )

    def backward(step, carry):
        layer = LAYERS - 1 - step
        a_ref[: own * QUERY] = dx_ref[...].astype(BF)
        for c in range(0, hidden, HIDDEN_TILE):
            part = slice(c, c + HIDDEN_TILE)
            grad = dot(a_ref[: own * QUERY], down_w[layer, part], NT)
            g_ref[:, part] = (grad * slope[layer, :, part].astype(F32)).astype(BF)
        t_ref[: own * QUERY] = dot(g_ref[...], up_w[layer], NT)
        gain = gains[layer, 1:2]
        for r in range(0, own * QUERY, CHUNK):
            part = slice(r, r + CHUNK)
            total = dx_ref[part] + norm_back(
                t_ref[part], gain, unit2[layer, part].astype(F32), inv2[layer, part]
            )
            dx_ref[part] = total
            a_ref[part] = total.astype(BF)
        o_ref[...] = dot(a_ref[: own * QUERY], out_w[layer], NT).astype(BF)
        for i in range(own):
            at = i * JOINT
            for h in range(PAIRS):
                lanes = slice(h * PAIR, (h + 1) * PAIR)
                key_lanes = slice(width + h * PAIR, width + (h + 1) * PAIR)
                value_lanes = slice(2 * width + h * PAIR, 2 * width + (h + 1) * PAIR)
                query = stack_pair(qkv[layer, at : at + QUERY, lanes])
                grad = stack_pair(o_ref[i * QUERY : (i + 1) * QUERY, lanes])
                prob = probs[layer, i * PAIRS + h]
                wide = prob.astype(F32)
                grad_prob = dot(grad, qkv[layer, at : at + JOINT, value_lanes], NT)
                center = jnp.sum(grad_prob * wide, -1, keepdims=True)
                grad_score = (wide * (grad_prob - center)).astype(BF)
                dqkv_ref[at : at + JOINT, value_lanes] = dot(grad, prob, TN).astype(BF).T
                dqkv_ref[at : at + JOINT, key_lanes] = (dot(query, grad_score, TN) * HEAD_DIM**-0.5).astype(BF).T
                grad_query = dot(grad_score, qkv[layer, at : at + JOINT, key_lanes], NN) * HEAD_DIM**-0.5
                dqkv_ref[at : at + QUERY, lanes] = merge_pair(grad_query).astype(BF)
        t_ref[...] = dot(dqkv_ref[...], attn_w[layer], NT)
        gain = gains[layer, 0:1]
        for i in range(own):
            at, to = i * JOINT, i * QUERY
            for r in range(0, JOINT, CHUNK):
                part = slice(at + r, at + r + CHUNK)
                t_ref[part] = norm_back(t_ref[part], gain, unit1[layer, part].astype(F32), inv1[layer, part])
            prompt_out[layer, i] = t_ref[at + PROMPT_AT : at + PROMPT_AT + prompt_count]
            dx_ref[to : to + cls_at] += t_ref[at : at + cls_at]
            dx_ref[to + cls_at : to + cls_at + 1] += t_ref[at + cls_at : at + cls_at + 1]
        return carry

    lax.fori_loop(0, LAYERS, backward, 0)

    for i in range(own):
        to = i * QUERY
        dx_own[i] = dx_ref[to : to + half]
        dx_other[i] = dx_ref[to + half : to + patches]
        dx_cls[i] = dx_ref[to + cls_at : to + cls_at + 1]


def run_encoder(
    patch_input, patch_other, cls_input, patch_cotangent, cot_other, cls_cotangent, logit_cotangent,
    prompts, head, head_bias, attn_bias, out_bias, up_bias, down_bias, gains, shifts, final_gain, final_bias,
    attn_weight, out_weight, up_weight, down_weight,
):
    own, half, width = patch_other.shape
    prompt_count, classes = prompts.shape[2], head.shape[2]
    hidden = up_weight.shape[2]
    queries, joints = own * QUERY, own * JOINT
    shape = jax.ShapeDtypeStruct
    vmem = pl.BlockSpec(memory_space=pltpu.VMEM)
    outs = (
        shape((own, half, width), BF),
        shape((own, half, width), BF),
        shape((own, 1, width), F32),
        shape((own, 1, classes), F32),
        shape((own, half, width), F32),
        shape((own, half, width), F32),
        shape((own, 1, width), F32),
        shape((LAYERS, own, prompt_count, width), F32),
        shape((own, 1, width), F32),
    )

    def kernel(*refs):
        encoder_kernel(own, 2 * half, prompt_count, *refs)

    return pl.pallas_call(
        kernel,
        out_shape=outs,
        in_specs=[vmem] * 18 + [pl.BlockSpec(memory_space=pl.ANY)] * 4,
        out_specs=[vmem] * len(outs),
        scratch_shapes=[
            pltpu.VMEM(attn_weight.shape, BF),
            pltpu.VMEM(out_weight.shape, BF),
            pltpu.VMEM(up_weight.shape, BF),
            pltpu.VMEM(down_weight.shape, BF),
            pltpu.VMEM((joints, width), F32),
            pltpu.VMEM((queries, width), F32),
            pltpu.VMEM((joints, width), F32),
            pltpu.VMEM((queries, width), F32),
            pltpu.VMEM((joints, width), BF),
            pltpu.VMEM((queries, width), BF),
            pltpu.VMEM((queries, hidden), BF),
            pltpu.VMEM((joints, 3 * width), BF),
            pltpu.VMEM((LAYERS, joints, 3 * width), BF),
            pltpu.VMEM((LAYERS, own * PAIRS, 2 * QUERY, JOINT), BF),
            pltpu.VMEM((LAYERS, queries, hidden), BF),
            pltpu.VMEM((LAYERS, joints, width), BF),
            pltpu.VMEM((LAYERS, queries, width), BF),
            pltpu.VMEM((LAYERS, joints, 1), F32),
            pltpu.VMEM((LAYERS, queries, 1), F32),
            pltpu.SemaphoreType.DMA((4, LAYERS)),
        ],
        compiler_params=pltpu.CompilerParams(vmem_limit_bytes=64 << 20),
        name="encoder",
    )(
        patch_input, patch_other, cls_input, patch_cotangent, cot_other, cls_cotangent, logit_cotangent,
        prompts, head, head_bias, attn_bias, out_bias, up_bias, down_bias, gains, shifts,
        final_gain[None], final_bias[None], attn_weight, out_weight, up_weight, down_weight,
    )


def per_device(
    cls_input, patch_input, task_ids, prompts, attn_weight, attn_bias, out_weight, out_bias, up_weight, up_bias,
    down_weight, down_bias, norm_gain, norm_bias, final_gain, final_bias, head_weight, head_bias,
    cls_cotangent, patch_cotangent, logit_cotangent,
):
    cores = lax.axis_size("seq")
    core = lax.axis_index("seq")
    images, width = cls_input.shape
    own = images // cores
    tasks, class_count = head_bias.shape
    swap = [(a, cores - 1 - a) for a in range(cores)]

    def theirs(block):
        return lax.ppermute(lax.dynamic_slice_in_dim(block, (cores - 1 - core) * own, own, 0), "seq", swap)

    patch_other = theirs(patch_input)
    cot_other = theirs(patch_cotangent)
    own_ids = lax.dynamic_slice_in_dim(task_ids, core * own, own, 0)
    own_prompts = jnp.take(prompts, own_ids, axis=0)
    own_head = jnp.stack([lax.dynamic_index_in_dim(head_weight, own_ids[i], 1, False) for i in range(own)])
    own_head_bias = jnp.take(head_bias, own_ids, axis=0).astype(F32)
    y_own, y_other, y_cls, logits, dx_own, dx_other, dx_cls, prompt_part, features = run_encoder(
        patch_input, patch_other, cls_input, patch_cotangent, cot_other, cls_cotangent, logit_cotangent,
        own_prompts, own_head, own_head_bias, attn_bias, out_bias, up_bias, down_bias, norm_gain, norm_bias,
        final_gain, final_bias, attn_weight, out_weight, up_weight, down_weight,
    )

    def restore(mine, other):
        back = lax.ppermute(other, "seq", swap)
        whole = jnp.where(core == 0, jnp.concatenate([mine, back], 0), jnp.concatenate([back, mine], 0))
        return whole

    small = jnp.concatenate([y_cls, dx_cls], 1)
    small = lax.all_gather(small, "seq", axis=0, tiled=True)
    all_logits = lax.all_gather(logits[:, 0], "seq", axis=0, tiled=True)
    onehot = (own_ids[:, None] == jnp.arange(tasks, dtype=jnp.int32)[None, :]).astype(F32)
    dense = jnp.einsum("it,lipd->tlpd", onehot, prompt_part, precision=lax.Precision.HIGHEST).astype(BF)
    prompt_grad = lax.psum(dense, ("batch", "seq")).astype(F32)
    all_features = lax.all_gather(features[:, 0].astype(BF), ("batch", "seq"), axis=0, tiled=True)
    all_cot = lax.all_gather(logit_cotangent, "batch", axis=0, tiled=True)
    all_ids = lax.all_gather(task_ids.astype(F32), "batch", axis=0, tiled=True).astype(jnp.int32)
    all_onehot = (all_ids[:, None] == jnp.arange(tasks, dtype=jnp.int32)[None, :]).astype(BF)
    selected = (all_onehot[:, :, None] * all_cot[:, None, :]).reshape(all_ids.shape[0], -1)
    head_weight_grad = jnp.einsum("id,in->dn", all_features, selected, preferred_element_type=F32)
    head_bias_grad = jnp.einsum("it,ic->tc", all_onehot, all_cot, preferred_element_type=F32)
    return (
        small[:, 0].astype(BF),
        restore(y_own, y_other),
        all_logits.astype(BF),
        small[:, 1],
        restore(dx_own, dx_other),
        prompt_grad,
        head_weight_grad.reshape(width, tasks, class_count),
        head_bias_grad,
    )


def solution(mesh):
    rows, tokens, whole = P("batch", None), P("batch", "seq", None), P()
    return jax.shard_map(
        per_device,
        mesh=mesh,
        in_specs=(rows, tokens, P("batch")) + (whole,) * 15 + (rows, tokens, rows),
        out_specs=(rows, tokens, rows, rows, tokens, whole, whole, whole),
        check_vma=False,
    )
```

```python
import jax
import jax.numpy as jnp
from jax import lax
from jax.experimental import pallas as pl
from jax.experimental.pallas import tpu as pltpu
from jax.sharding import PartitionSpec as P

HEADS = 12
HEAD_DIM = 64
LAYERS = 2
EPSILON = 1e-06
BF = jnp.bfloat16
F32 = jnp.float32

JOINT = 256
QUERY = 208
PROMPT_AT = 200
PAIR = 2 * HEAD_DIM
PAIRS = HEADS // 2
CHUNK = 32
HIDDEN_TILE = 512

TAIL = 64
TAIL_AT = JOINT - TAIL
RAIL = 16
LINE = 4
EARLY = 32
MESH = pl.DeviceIdType.MESH

NN = (((1,), (0,)), ((), ()))
NT = (((1,), (1,)), ((), ()))
TN = (((0,), (0,)), ((), ()))


def dot(left, right, dims):
    return lax.dot_general(left, right, dims, preferred_element_type=F32)


def gelu_and_slope(u):
    phi = 0.5 + 0.5 * lax.erf(u * 0.7071067811865476)
    return u * phi, phi + u * (0.3989422804014327 * jnp.exp(-0.5 * u * u))


def norm_parts(x):
    center = x - jnp.mean(x, -1, keepdims=True)
    inverse = lax.rsqrt(jnp.mean(center * center, -1, keepdims=True) + EPSILON)
    return center * inverse, inverse


def norm_back(grad, gain, unit, inverse):
    scaled = grad * gain
    first = jnp.mean(scaled, -1, keepdims=True)
    second = jnp.mean(scaled * unit, -1, keepdims=True)
    return inverse * (scaled - first - unit * second)


def pick_row(ref, index):
    values = ref[...].astype(F32)
    rows = lax.broadcasted_iota(jnp.int32, values.shape, 0)
    return jnp.sum(jnp.where(rows == index, values, 0.0), 0, keepdims=True)


def encoder_kernel(
    own, patches, prompt_count, classes,
    task_ids, cls_in, cls_cot, logit_cot, prompts, head_bias, attn_bias, out_bias, up_bias, down_bias, gains, shifts,
    final_gain, final_bias,
    patch_hbm, cot_hbm, head_hbm, attn_hbm, out_hbm, up_hbm, down_hbm,
    y_out, dx_out, small_out, prompt_out, message_out,
    attn_w, out_w, up_w, down_w, head_w, x_ref, t_ref, dx_ref, a_ref, o_ref, wide_ref,
    qkv, probs, slope, unit1, unit2, inv1, inv2, unit_t, inv_t,
    patch_own, patch_other, cot_own, cot_other, y_own, y_other, small, weight_sems, local_sems, send_sems, recv_sems,
):
    half = patches // 2
    cls_at = patches
    width = x_ref.shape[1]
    hidden = up_w.shape[2]
    queries = own * QUERY
    tasks = head_bias.shape[0]
    core = lax.axis_index("seq")
    other_core = 1 - core
    first = core * own
    other_first = other_core * own

    weights = ((attn_hbm, attn_w), (out_hbm, out_w), (up_hbm, up_w), (down_hbm, down_w))

    def weight_copy(k, layer):
        source, target = weights[k]
        return pltpu.make_async_copy(source.at[layer], target.at[layer], weight_sems.at[k, layer])

    def local_copy(k, source, target):
        return pltpu.make_async_copy(source, target, local_sems.at[k])

    def swap(k, source, target):
        return pltpu.make_async_remote_copy(
            src_ref=source, dst_ref=target, send_sem=send_sems.at[k], recv_sem=recv_sems.at[k],
            device_id={"seq": other_core}, device_id_type=MESH,
        )

    take_patches = local_copy(0, patch_hbm.at[pl.ds(first, own)], patch_own)
    take_cots = local_copy(1, cot_hbm.at[pl.ds(first, own)], cot_own)
    take_head = local_copy(2, head_hbm, head_w)
    keep_y = local_copy(3, y_own, y_out.at[pl.ds(first, own)])
    keep_small = local_copy(4, small, small_out.at[pl.ds(first, own)])
    swap_patches = swap(0, patch_hbm.at[pl.ds(other_first, own)], patch_other)
    swap_cots = swap(1, cot_hbm.at[pl.ds(other_first, own)], cot_other)
    swap_y = swap(2, y_other, y_out.at[pl.ds(first, own)])
    swap_small = swap(3, small, small_out.at[pl.ds(first, own)])

    take_patches.start()
    weight_copy(0, 0).start()
    barrier = pltpu.get_barrier_semaphore()
    pl.semaphore_signal(barrier, inc=1, device_id={"seq": other_core}, device_id_type=MESH)
    pl.semaphore_wait(barrier, 1)
    swap_patches.start()
    for layer in range(LAYERS):
        for k in range(len(weights)):
            if (layer, k) != (0, 0):
                weight_copy(k, layer).start()
        if layer == 0:
            swap_cots.start()
            take_cots.start()
            take_head.start()

    lane = lax.broadcasted_iota(jnp.int32, (1, PAIR), 1)
    is_low = lane < HEAD_DIM
    column = lax.broadcasted_iota(jnp.int32, (1, JOINT), 1)
    is_key = (column <= cls_at) | ((column >= PROMPT_AT) & (column < PROMPT_AT + prompt_count))
    key_bias = jnp.where(is_key, 0.0, -1e30).astype(F32)

    def stack_pair(block):
        zero = jnp.zeros_like(block)
        return jnp.concatenate([jnp.where(is_low, block, zero), jnp.where(is_low, zero, block)], 0)

    def merge_pair(block):
        return jnp.where(is_low, block[:QUERY], block[QUERY:])

    def tails(ref, lanes):
        return jnp.concatenate([ref[i * JOINT + TAIL_AT : (i + 1) * JOINT, lanes] for i in range(own)], 0)

    take_patches.wait()
    for i in range(own):
        at = i * JOINT
        x_ref[at : at + half] = patch_own[i].astype(F32)
        x_ref[at + TAIL_AT : at + JOINT] = jnp.zeros((TAIL, width), F32)
        x_ref[at + cls_at : at + cls_at + 1] = pick_row(cls_in, first + i)
    swap_patches.wait()
    for i in range(own):
        at = i * JOINT + half
        x_ref[at : at + half] = patch_other[i].astype(F32)

    def forward(layer, carry):
        for i in range(own):
            at = i * JOINT + PROMPT_AT
            x_ref[at : at + prompt_count] = prompts[i, layer].astype(F32)
        gain, shift = gains[layer, 0:1], shifts[layer, 0:1]
        for r in range(0, own * JOINT, CHUNK):
            unit, inverse = norm_parts(x_ref[r : r + CHUNK])
            unit1[layer, r : r + CHUNK] = unit.astype(BF)
            inv1[layer, r : r + CHUNK] = inverse
            a_ref[r : r + CHUNK] = (unit * gain + shift).astype(BF)
        weight_copy(0, layer).wait()
        bias = pick_row(attn_bias, layer)
        for n in range(3):
            part = slice(n * width, (n + 1) * width)
            qkv[layer, :, part] = (dot(a_ref[...], attn_w[layer, :, part], NN) + bias[:, part]).astype(BF)
        turned = tails(x_ref, slice(None)).T
        center = turned - jnp.mean(turned, 0, keepdims=True)
        inverse = lax.rsqrt(jnp.mean(center * center, 0, keepdims=True) + EPSILON)
        unit_t[layer] = (center * inverse).astype(BF)
        inv_t[layer] = inverse
        for i in range(own):
            at = i * JOINT
            for h in range(PAIRS):
                lanes = slice(h * PAIR, (h + 1) * PAIR)
                query = stack_pair(qkv[layer, at : at + QUERY, lanes])
                keys = qkv[layer, at : at + JOINT, width + h * PAIR : width + (h + 1) * PAIR]
                values = qkv[layer, at : at + JOINT, 2 * width + h * PAIR : 2 * width + (h + 1) * PAIR]
                scores = dot(query, keys, NT) * HEAD_DIM**-0.5 + key_bias
                expo = jnp.exp(scores - jnp.max(scores, -1, keepdims=True))
                prob = (expo * (1.0 / jnp.sum(expo, -1, keepdims=True))).astype(BF)
                probs[layer, i * PAIRS + h] = prob
                o_ref[i * QUERY : (i + 1) * QUERY, lanes] = merge_pair(dot(prob, values, NN)).astype(BF)
        weight_copy(1, layer).wait()
        mixed = dot(o_ref[...], out_w[layer], NN) + pick_row(out_bias, layer)
        for i in range(own):
            at, to = i * JOINT, i * QUERY
            t_ref[to : to + QUERY] = x_ref[at : at + QUERY] + mixed[to : to + QUERY]
        gain, shift = gains[layer, 1:2], shifts[layer, 1:2]
        for r in range(0, queries, CHUNK):
            unit, inverse = norm_parts(t_ref[r : r + CHUNK])
            unit2[layer, r : r + CHUNK] = unit.astype(BF)
            inv2[layer, r : r + CHUNK] = inverse
            a_ref[r : r + CHUNK] = (unit * gain + shift).astype(BF)
        weight_copy(2, layer).wait()
        bias = pick_row(up_bias, layer)
        for c in range(0, hidden, HIDDEN_TILE):
            part = slice(c, c + HIDDEN_TILE)
            act, act_slope = gelu_and_slope(dot(a_ref[:queries], up_w[layer, :, part], NN) + bias[:, part])
            wide_ref[:queries, part] = act.astype(BF)
            slope[layer, :, part] = act_slope.astype(BF)
        weight_copy(3, layer).wait()
        result = t_ref[:queries] + (dot(wide_ref[:queries], down_w[layer], NN) + pick_row(down_bias, layer))
        for i in range(own):
            x_ref[i * JOINT : i * JOINT + QUERY] = result[i * QUERY : (i + 1) * QUERY]
        return carry

    lax.fori_loop(0, LAYERS, forward, 0)

    for i in range(own):
        at = i * JOINT
        y_own[i] = x_ref[at : at + half].astype(BF)
        y_other[i] = x_ref[at + half : at + patches].astype(BF)
    swap_y.start()
    keep_y.start()

    take_head.wait()
    rows = -(-classes // 8) * 8
    row = lax.broadcasted_iota(jnp.int32, (own * rows, tasks * classes), 0)
    col = lax.broadcasted_iota(jnp.int32, (own * rows, tasks * classes), 1)
    task = jnp.where(row < rows, task_ids[first], task_ids[first + 1])
    pick = jnp.where(row < rows, row, row - rows) * tasks + task == col
    own_head = dot(jnp.where(pick, 1.0, 0.0).astype(BF), head_w[...], NN).astype(BF)
    message = []
    ends = []
    swap_cots.wait()
    take_cots.wait()
    for i in range(own):
        at, to = i * JOINT, i * QUERY
        matrix = own_head[i * rows : (i + 1) * rows]
        last = x_ref[at + cls_at : at + cls_at + 1]
        unit, inverse = norm_parts(last)
        feature = (unit * final_gain[...] + final_bias[...]).astype(BF)
        task = lax.broadcasted_iota(jnp.int32, (tasks, classes), 0) == task_ids[first + i]
        offset = jnp.sum(jnp.where(task, head_bias[...].astype(F32), 0.0), 0, keepdims=True)
        offset = jnp.concatenate([offset, jnp.zeros((1, width - classes), F32)], 1)
        score = dot(jnp.broadcast_to(feature, (16, width)), matrix, NT)[:1]
        score = jnp.concatenate([score, jnp.zeros((1, width - rows), F32)], 1) + offset
        small[i, 0:1] = last
        small[i, 1:2] = score
        small[i, 3:8] = jnp.zeros((5, width), F32)
        cot = pick_row(logit_cot, first + i)
        cot = jnp.concatenate([cot, jnp.zeros((1, PAIR - classes), F32)], 1)
        grad = dot(jnp.broadcast_to(cot[:, :rows].astype(BF), (16, rows)), matrix, NN)[:1]
        dx_ref[to + TAIL_AT : to + QUERY] = jnp.zeros((QUERY - TAIL_AT, width), F32)
        dx_ref[to : to + half] = cot_own[i].astype(F32)
        dx_ref[to + half : to + patches] = cot_other[i].astype(F32)
        dx_ref[to + cls_at : to + cls_at + 1] = pick_row(cls_cot, first + i) + norm_back(
            grad, final_gain[...], unit, inverse
        )
        message += [feature.astype(F32)[:, j : j + PAIR] for j in range(0, width, PAIR)]
        ends.append(cot)
    names = jnp.where(is_low, task_ids[first], task_ids[first + 1]).astype(F32)
    message_out[...] = jnp.concatenate(message + ends + [names, jnp.zeros((1, PAIR), F32)], 0).astype(BF)

    def backward(step, carry):
        layer = LAYERS - 1 - step
        a_ref[:queries] = dx_ref[...].astype(BF)
        for c in range(0, hidden, HIDDEN_TILE):
            part = slice(c, c + HIDDEN_TILE)
            grad = dot(a_ref[:queries], down_w[layer, part], NT)
            wide_ref[:queries, part] = (grad * slope[layer, :, part].astype(F32)).astype(BF)
        t_ref[:queries] = dot(wide_ref[:queries], up_w[layer], NT)
        gain = gains[layer, 1:2]
        for r in range(0, queries, CHUNK):
            part = slice(r, r + CHUNK)
            total = dx_ref[part] + norm_back(t_ref[part], gain, unit2[layer, part].astype(F32), inv2[layer, part])
            dx_ref[part] = total
            a_ref[part] = total.astype(BF)
        o_ref[...] = dot(a_ref[:queries], out_w[layer], NT).astype(BF)
        for i in range(own):
            at = i * JOINT
            wide_ref[at + QUERY : at + JOINT, :width] = jnp.zeros((JOINT - QUERY, width), BF)
            for h in range(PAIRS):
                lanes = slice(h * PAIR, (h + 1) * PAIR)
                key_lanes = slice(width + h * PAIR, width + (h + 1) * PAIR)
                value_lanes = slice(2 * width + h * PAIR, 2 * width + (h + 1) * PAIR)
                query = stack_pair(qkv[layer, at : at + QUERY, lanes])
                grad = stack_pair(o_ref[i * QUERY : (i + 1) * QUERY, lanes])
                prob = probs[layer, i * PAIRS + h]
                wide = prob.astype(F32)
                grad_prob = dot(grad, qkv[layer, at : at + JOINT, value_lanes], NT)
                center = jnp.sum(grad_prob * wide, -1, keepdims=True)
                grad_score = (wide * (grad_prob - center)).astype(BF)
                wide_ref[at : at + JOINT, value_lanes] = dot(grad, prob, TN).astype(BF).T
                wide_ref[at : at + JOINT, key_lanes] = (dot(query, grad_score, TN) * HEAD_DIM**-0.5).astype(BF).T
                grad_query = dot(grad_score, qkv[layer, at : at + JOINT, key_lanes], NN) * HEAD_DIM**-0.5
                wide_ref[at : at + QUERY, lanes] = merge_pair(grad_query).astype(BF)
        gain = gains[layer, 0:1]
        gain_t = jnp.broadcast_to(gain, (PAIR, width)).T
        scaled = dot(attn_w[layer, :, width:], tails(wide_ref, slice(width, 3 * width)), NT) * gain_t
        unit = unit_t[layer].astype(F32)
        mean = jnp.mean(scaled, 0, keepdims=True)
        mean_unit = jnp.mean(scaled * unit, 0, keepdims=True)
        prompt_out[layer] = (inv_t[layer] * (scaled - mean - unit * mean_unit)).astype(BF)
        t_ref[...] = dot(wide_ref[:, : 3 * width], attn_w[layer], NT)
        for i in range(own):
            at, to = i * JOINT, i * QUERY
            for r in range(0, QUERY, 16):
                part = slice(at + r, at + r + 16)
                grad = norm_back(t_ref[part], gain, unit1[layer, part].astype(F32), inv1[layer, part])
                if r + 16 > cls_at:
                    keep = lax.broadcasted_iota(jnp.int32, (16, 1), 0) + r <= cls_at
                    grad = jnp.where(keep, grad, 0.0)
                dx_ref[to + r : to + r + 16] += grad
        return carry

    lax.fori_loop(0, LAYERS, backward, 0)

    keep_dx, swap_dx = [], []
    padded = dx_out.shape[1]
    for i in range(own):
        at, to = i * JOINT, i * QUERY
        x_ref[at : at + half] = dx_ref[to : to + half]
        x_ref[at + 128 : at + 128 + half] = dx_ref[to + half : to + patches]
        small[i, 2:3] = dx_ref[to + cls_at : to + cls_at + 1]
        keep_dx.append(local_copy(5 + i, x_ref.at[pl.ds(at, padded)], dx_out.at[first + i]))
        swap_dx.append(swap(4 + i, x_ref.at[pl.ds(at + 128, padded)], dx_out.at[first + i]))
        swap_dx[i].start()
        keep_dx[i].start()
    swap_small.start()
    keep_small.start()
    for copy in [swap_y, keep_y, swap_small, keep_small] + swap_dx + keep_dx:
        copy.wait()


def run_encoder(
    task_ids, patch_input, cls_input, patch_cotangent, cls_cotangent, logit_cotangent, prompts, head_weight, head_bias,
    attn_weight, attn_bias, out_weight, out_bias, up_weight, up_bias, down_weight, down_bias,
    gains, shifts, final_gain, final_bias,
):
    images, half, width = patch_input.shape
    own, prompt_count = prompts.shape[0], prompts.shape[2]
    classes = head_bias.shape[1]
    hidden = up_weight.shape[2]
    queries, joints = own * QUERY, own * JOINT
    shape = jax.ShapeDtypeStruct
    vmem = pl.BlockSpec(memory_space=pltpu.VMEM)
    anywhere = pl.BlockSpec(memory_space=pl.ANY)
    outs = (
        shape((images, half, width), BF),
        shape((images, -(-half // 8) * 8, width), F32),
        shape((images, 8, width), F32),
        shape((LAYERS, width, own * TAIL), BF),
        shape((16, PAIR), BF),
    )

    def kernel(*refs):
        encoder_kernel(own, 2 * half, prompt_count, classes, *refs)

    head_rows = head_weight.transpose(2, 1, 0).reshape(-1, width)
    return pl.pallas_call(
        kernel,
        out_shape=outs,
        in_specs=[pl.BlockSpec(memory_space=pltpu.SMEM)] + [vmem] * 13 + [anywhere] * 7,
        out_specs=[anywhere, anywhere, anywhere, vmem, vmem],
        scratch_shapes=[
            pltpu.VMEM(attn_weight.shape, BF),
            pltpu.VMEM(out_weight.shape, BF),
            pltpu.VMEM(up_weight.shape, BF),
            pltpu.VMEM(down_weight.shape, BF),
            pltpu.VMEM(head_rows.shape, BF),
            pltpu.VMEM((joints, width), F32),
            pltpu.VMEM((joints, width), F32),
            pltpu.VMEM((queries, width), F32),
            pltpu.VMEM((joints, width), BF),
            pltpu.VMEM((queries, width), BF),
            pltpu.VMEM((joints, hidden), BF),
            pltpu.VMEM((LAYERS, joints, 3 * width), BF),
            pltpu.VMEM((LAYERS, own * PAIRS, 2 * QUERY, JOINT), BF),
            pltpu.VMEM((LAYERS, queries, hidden), BF),
            pltpu.VMEM((LAYERS, joints, width), BF),
            pltpu.VMEM((LAYERS, queries, width), BF),
            pltpu.VMEM((LAYERS, joints, 1), F32),
            pltpu.VMEM((LAYERS, queries, 1), F32),
            pltpu.VMEM((LAYERS, width, own * TAIL), BF),
            pltpu.VMEM((LAYERS, 1, own * TAIL), F32),
            pltpu.VMEM((own, half, width), BF),
            pltpu.VMEM((own, half, width), BF),
            pltpu.VMEM((own, half, width), BF),
            pltpu.VMEM((own, half, width), BF),
            pltpu.VMEM((own, half, width), BF),
            pltpu.VMEM((own, half, width), BF),
            pltpu.VMEM((own, 8, width), F32),
            pltpu.SemaphoreType.DMA((4, LAYERS)),
            pltpu.SemaphoreType.DMA((7,)),
            pltpu.SemaphoreType.DMA((6,)),
            pltpu.SemaphoreType.DMA((6,)),
        ],
        compiler_params=pltpu.CompilerParams(vmem_limit_bytes=64 << 20, collective_id=0, has_side_effects=True),
        name="encoder",
    )(
        task_ids, cls_input, cls_cotangent, logit_cotangent, prompts, head_bias, attn_bias, out_bias, up_bias, down_bias,
        gains, shifts, final_gain[None], final_bias[None],
        patch_input, patch_cotangent, head_rows, attn_weight, out_weight, up_weight, down_weight,
    )


def reduce_kernel(
    tasks, grads, message, early_out, late_out, messages_out,
    got, got_messages, sums, got_sums, early, late, local_sems, send_sems, recv_sems,
):
    me = lax.axis_index("batch")
    core = lax.axis_index("seq")
    other_core = 1 - core
    line, place = me // LINE, me % LINE
    share = got.shape[2]
    pairs = early.shape[1]

    def along(k, source, target, device):
        return pltpu.make_async_remote_copy(
            src_ref=source, dst_ref=target, send_sem=send_sems.at[k], recv_sem=recv_sems.at[k],
            device_id=device, device_id_type=MESH,
        )

    barrier = pltpu.get_barrier_semaphore()
    for step in range(1, RAIL):
        pl.semaphore_signal(barrier, inc=1, device_id={"batch": (me + step) % RAIL}, device_id_type=MESH)
    pl.semaphore_signal(barrier, inc=1, device_id={"seq": other_core}, device_id_type=MESH)
    pl.semaphore_wait(barrier, RAIL)

    copies = []
    for step in range(1, RAIL):
        target = (me + step) % RAIL
        rows = pl.ds(pl.multiple_of(target * share, 16), share)
        copies.append(along(step, grads.at[:, rows], got.at[me], {"batch": target}))
        copies.append(along(RAIL + step, message, got_messages.at[me], {"batch": target}))
    for copy in copies:
        copy.start()
    got[me] = grads[:, pl.ds(pl.multiple_of(me * share, 16), share)]
    got_messages[me] = message[...]
    for copy in copies:
        copy.wait()

    lane = lax.broadcasted_iota(jnp.int32, (1, 2 * TAIL), 1)
    is_low = lane < TAIL

    def add_up(t, carry):
        for layer in range(LAYERS):
            halves = []
            for side in range(2):
                task = (2 * t + side).astype(F32)
                total = jnp.zeros((share, 2 * TAIL), F32)
                for s in range(RAIL):
                    weight = jnp.where(got_messages[s, 14:15].astype(F32) == task, 1.0, 0.0)
                    total = total + got[s, layer].astype(F32) * weight
                halves.append(total + pltpu.roll(total, TAIL, 1))
            sums[layer, t] = jnp.where(is_low, halves[0], halves[1])
        return carry

    lax.fori_loop(0, tasks // 2, add_up, 0)
    partner = {"seq": other_core}
    swap_sums = along(0, sums.at[:, pl.ds(other_core * pairs, pairs)], got_sums, partner)
    swap_messages = along(RAIL, got_messages, messages_out.at[core], partner)
    keep_messages = pltpu.make_async_copy(got_messages, messages_out.at[core], local_sems.at[0])
    swap_sums.start()
    swap_messages.start()
    keep_messages.start()
    swap_sums.wait()
    total = (sums[:, pl.ds(core * pairs, pairs)] + got_sums[...]).astype(BF)
    early[...] = total[:, :, :EARLY]
    late[...] = total[:, :, EARLY:]

    base = 2 * RAIL
    keeps, copies = [], []
    for layer in range(LAYERS):
        early_at, late_at = early_out.at[layer, core, line, place], late_out.at[layer, core, line, place]
        keeps.append(pltpu.make_async_copy(early.at[layer], early_at, local_sems.at[1 + 2 * layer]))
        keeps.append(pltpu.make_async_copy(late.at[layer], late_at, local_sems.at[2 + 2 * layer]))
        for step in range(1, LINE):
            to_line = {"batch": (line + step) % LINE * LINE + place}
            to_place = {"batch": line * LINE + (place + step) % LINE}
            copies.append(along(base + len(copies), early.at[layer], early_at, to_line))
            copies.append(along(base + len(copies), late.at[layer], late_at, to_place))
    for copy in copies + keeps:
        copy.start()
    for copy in copies + keeps:
        copy.wait()
    base += len(copies)
    copies = []
    for layer in range(LAYERS):
        early_at, late_at = early_out.at[layer, core, :, place], late_out.at[layer, core, line]
        for step in range(1, LINE):
            to_line = {"batch": (line + step) % LINE * LINE + place}
            to_place = {"batch": line * LINE + (place + step) % LINE}
            copies.append(along(base + len(copies), early_at, early_at, to_place))
            copies.append(along(base + len(copies), late_at, late_at, to_line))
    for copy in copies:
        copy.start()
    for copy in copies:
        copy.wait()
    base += len(copies)
    copies = []
    for layer in range(LAYERS):
        for k, ref in enumerate((early_out, late_out)):
            copies.append(along(base + len(copies), ref.at[layer, core], ref.at[layer, core], partner))
    for copy in copies:
        copy.start()
    for copy in copies + [swap_messages, keep_messages]:
        copy.wait()


def run_reduce(grads, message, tasks):
    layers, width, lanes = grads.shape
    share = width // RAIL
    pairs = tasks // 4
    shape = jax.ShapeDtypeStruct
    vmem = pl.BlockSpec(memory_space=pltpu.VMEM)
    anywhere = pl.BlockSpec(memory_space=pl.ANY)
    count = 2 * RAIL + 2 * 2 * layers * (LINE - 1) + 2 * layers

    def kernel(*refs):
        reduce_kernel(tasks, *refs)

    return pl.pallas_call(
        kernel,
        out_shape=(
            shape((layers, 2, LINE, LINE, pairs, EARLY, lanes), BF),
            shape((layers, 2, LINE, LINE, pairs, share - EARLY, lanes), BF),
            shape((2, RAIL) + message.shape, BF),
        ),
        in_specs=[vmem, vmem],
        out_specs=[anywhere, anywhere, anywhere],
        scratch_shapes=[
            pltpu.VMEM((RAIL, layers, share, lanes), BF),
            pltpu.VMEM((RAIL,) + message.shape, BF),
            pltpu.VMEM((layers, 2 * pairs, share, lanes), F32),
            pltpu.VMEM((layers, pairs, share, lanes), F32),
            pltpu.VMEM((layers, pairs, EARLY, lanes), BF),
            pltpu.VMEM((layers, pairs, share - EARLY, lanes), BF),
            pltpu.SemaphoreType.DMA((1 + 2 * layers,)),
            pltpu.SemaphoreType.DMA((count,)),
            pltpu.SemaphoreType.DMA((count,)),
        ],
        compiler_params=pltpu.CompilerParams(collective_id=1, has_side_effects=True, vmem_limit_bytes=32 << 20),
        name="reduce",
    )(grads, message)


def finish_kernel(
    own, prompt_count, early, late, messages, small, prompt_grad, head_grad, bias_grad, y_cls, logits, dx_cls,
    rows_ref, left_ref, features_ref,
):
    classes, tasks, width = head_grad.shape[0], head_grad.shape[1], head_grad.shape[2]
    devices = 2 * RAIL
    count = own * devices
    step = pl.program_id(0)

    @pl.when(step == 0)
    def prepare():
        rows_ref[...] = messages[...].astype(F32).reshape(rows_ref.shape)

        def gather(k):
            return rows_ref[pl.ds(k, devices, stride=16)]

        chunks = width // PAIR
        for i in range(own):
            for j in range(chunks):
                features_ref[i * devices : (i + 1) * devices, j * PAIR : (j + 1) * PAIR] = gather(
                    i * chunks + j
                ).astype(BF)
        cots = jnp.concatenate([gather(own * chunks + i) for i in range(own)], 0)
        ids = gather(own * chunks + own).T
        ids = jnp.concatenate([ids[i * TAIL : i * TAIL + 1] for i in range(own)], 1)
        match = jnp.where(lax.broadcasted_iota(jnp.int32, (tasks, count), 0).astype(F32) == ids, 1.0, 0.0)
        total = dot(match.astype(BF), cots.astype(BF), NN)
        bias_grad[...] = total[:, : bias_grad.shape[1]]
        cots_t = cots.T[: bias_grad.shape[1]]
        left_ref[...] = (cots_t[:, None, :] * match[None]).astype(BF)
        y_cls[...] = small[:, 0, :].astype(BF)
        logits[...] = small[:, 1, : logits.shape[1]].astype(BF)
        dx_cls[...] = small[:, 2, :]

    left = left_ref[pl.ds(step * classes, classes)].reshape(classes * tasks, count)
    head_grad[...] = dot(left, features_ref[...], NN).reshape(head_grad.shape)

    pairs = early.shape[4]
    row = lax.broadcasted_iota(jnp.int32, (2 * prompt_count, LAYERS * 2 * TAIL), 0)
    col = lax.broadcasted_iota(jnp.int32, (2 * prompt_count, LAYERS * 2 * TAIL), 1)
    for k in range(pairs):
        both = []
        for layer in range(LAYERS):
            blocks = []
            for b in range(RAIL):
                blocks.append(early[layer, 0, b // LINE, b % LINE, k])
                blocks.append(late[layer, 0, b // LINE, b % LINE, k])
            both.append(jnp.concatenate(blocks, 0))
        both = jnp.concatenate(both, 1)
        for side in range(2):
            source = (row % 2) * 2 * TAIL + side * TAIL + (PROMPT_AT - TAIL_AT) + row // 2
            turn = jnp.where(source == col, 1.0, 0.0).astype(BF)
            prompt_grad[2 * k + side] = dot(turn, both, NT).reshape(prompt_grad.shape[1:])


def run_finish(early, late, messages, small, prompt_count, class_count, own):
    layers, cores, _, _, pairs, _, lanes = early.shape
    width = RAIL * (early.shape[5] + late.shape[5])
    tasks = 2 * cores * pairs
    images = small.shape[0]
    steps = 4
    per_step = pairs * cores // steps
    shape = jax.ShapeDtypeStruct

    def kernel(*refs):
        finish_kernel(own, prompt_count, *refs)

    def at(step):
        return (0, step // 2, 0, 0, step % 2, 0, 0)

    def whole(*dims):
        return pl.BlockSpec(dims, lambda step: (0,) * len(dims))

    return pl.pallas_call(
        kernel,
        grid=(steps,),
        out_shape=(
            shape((tasks, prompt_count, layers, width), F32),
            shape((class_count, tasks, width), F32),
            shape((tasks, class_count), F32),
            shape((images, width), BF),
            shape((images, class_count), BF),
            shape((images, width), F32),
        ),
        in_specs=[
            pl.BlockSpec((layers, 1, LINE, LINE, per_step, early.shape[5], lanes), at),
            pl.BlockSpec((layers, 1, LINE, LINE, per_step, late.shape[5], lanes), at),
            whole(*messages.shape),
            whole(*small.shape),
        ],
        out_specs=[
            pl.BlockSpec((tasks // steps, prompt_count, layers, width), lambda step: (step, 0, 0, 0)),
            pl.BlockSpec((class_count // steps, tasks, width), lambda step: (step, 0, 0)),
            whole(tasks, class_count),
            whole(images, width),
            whole(images, class_count),
            whole(images, width),
        ],
        scratch_shapes=[
            pltpu.VMEM((2 * RAIL * 16, PAIR), F32),
            pltpu.VMEM((class_count, tasks, own * 2 * RAIL), BF),
            pltpu.VMEM((own * 2 * RAIL, width), BF),
        ],
        compiler_params=pltpu.CompilerParams(vmem_limit_bytes=48 << 20),
        name="finish",
    )(early, late, messages, small)


def gathered_sums(grads, message, own_ids, task_ids, logit_cot, prompt_count, tasks):
    layers, width, lanes = grads.shape
    own = own_ids.shape[0]
    start = PROMPT_AT - TAIL_AT
    parts = grads.reshape(layers, width, own, TAIL)[..., start : start + prompt_count].astype(F32)
    names = jnp.arange(tasks, dtype=jnp.int32)[None, :]
    onehot = (own_ids[:, None] == names).astype(F32)
    dense = jnp.einsum("it,ldip->tlpd", onehot, parts, precision=lax.Precision.HIGHEST)
    prompt_grad = lax.psum(dense, ("batch", "seq"))
    features = message[: own * width // PAIR].reshape(own, width)
    features = lax.all_gather(features, ("batch", "seq"), axis=0, tiled=True)
    cots = lax.all_gather(logit_cot, "batch", axis=0, tiled=True)
    ids = lax.all_gather(task_ids.astype(F32), "batch", axis=0, tiled=True).astype(jnp.int32)
    match = (ids[:, None] == names).astype(BF)
    head_grad = jnp.einsum("id,it,ic->dtc", features, match, cots, preferred_element_type=F32)
    bias_grad = jnp.einsum("it,ic->tc", match, cots, preferred_element_type=F32)
    return prompt_grad, head_grad, bias_grad


def per_device(
    cls_input, patch_input, task_ids, prompts, attn_weight, attn_bias, out_weight, out_bias, up_weight, up_bias,
    down_weight, down_bias, norm_gain, norm_bias, final_gain, final_bias, head_weight, head_bias,
    cls_cotangent, patch_cotangent, logit_cotangent,
):
    cores = lax.axis_size("seq")
    core = lax.axis_index("seq")
    images, width = cls_input.shape
    own = images // cores
    tasks, class_count = head_bias.shape
    prompt_count = prompts.shape[2]
    own_ids = lax.dynamic_slice_in_dim(task_ids, core * own, own, 0)
    own_prompts = jnp.take(prompts, own_ids, axis=0)
    y, dx, small, grads, message = run_encoder(
        task_ids, patch_input, cls_input, patch_cotangent, cls_cotangent, logit_cotangent, own_prompts,
        head_weight, head_bias, attn_weight, attn_bias, out_weight, out_bias, up_weight, up_bias,
        down_weight, down_bias, norm_gain, norm_bias, final_gain, final_bias,
    )
    if lax.axis_size("batch") == RAIL:
        early, late, messages = run_reduce(grads, message, tasks)
        prompt_grad, head_grad, bias_grad, y_cls, logits, dx_cls = run_finish(
            early, late, messages, small, prompt_count, class_count, own
        )
        prompt_grad = prompt_grad.transpose(0, 2, 1, 3)
        head_grad = head_grad.transpose(2, 1, 0)
    else:
        prompt_grad, head_grad, bias_grad = gathered_sums(
            grads, message, own_ids, task_ids, logit_cotangent, prompt_count, tasks
        )
        y_cls, logits, dx_cls = small[:, 0].astype(BF), small[:, 1, :class_count].astype(BF), small[:, 2]
    return y_cls, y, logits, dx_cls, dx[:, : patch_input.shape[1]], prompt_grad, head_grad, bias_grad


def solution(mesh):
    rows, tokens, whole = P("batch", None), P("batch", "seq", None), P()
    return jax.shard_map(
        per_device,
        mesh=mesh,
        in_specs=(rows, tokens, P("batch")) + (whole,) * 15 + (rows, tokens, rows),
        out_specs=(rows, tokens, rows, rows, tokens, whole, whole, whole),
        check_vma=False,
    )
```

```python
import jax
import jax.numpy as jnp
from jax import lax
from jax.experimental import pallas as pl
from jax.experimental.pallas import tpu as pltpu
from jax.sharding import PartitionSpec as P

HEADS = 12
HEAD_DIM = 64
LAYERS = 2
EPSILON = 1e-06
BF = jnp.bfloat16
F32 = jnp.float32

JOINT = 256
QUERY = 208
PROMPT_AT = 200
PAIR = 2 * HEAD_DIM
PAIRS = HEADS // 2
CHUNK = 32
HIDDEN_TILE = 512

TAIL = 64
TAIL_AT = JOINT - TAIL
RAIL = 16
LINE = 4
EARLY = 32
FINISH_PARTS = 4
MESH = pl.DeviceIdType.MESH

NN = (((1,), (0,)), ((), ()))
NT = (((1,), (1,)), ((), ()))
TN = (((0,), (0,)), ((), ()))


def dot(left, right, dims):
    return lax.dot_general(left, right, dims, preferred_element_type=F32)


def gelu_and_slope(u):
    phi = 0.5 + 0.5 * lax.erf(u * 0.7071067811865476)
    return u * phi, phi + u * (0.3989422804014327 * jnp.exp(-0.5 * u * u))


def norm_parts(x):
    center = x - jnp.mean(x, -1, keepdims=True)
    inverse = lax.rsqrt(jnp.mean(center * center, -1, keepdims=True) + EPSILON)
    return center * inverse, inverse


def norm_back(grad, gain, unit, inverse):
    scaled = grad * gain
    first = jnp.mean(scaled, -1, keepdims=True)
    second = jnp.mean(scaled * unit, -1, keepdims=True)
    return inverse * (scaled - first - unit * second)


def pick_row(ref, index):
    values = ref[...].astype(F32)
    rows = lax.broadcasted_iota(jnp.int32, values.shape, 0)
    return jnp.sum(jnp.where(rows == index, values, 0.0), 0, keepdims=True)


class Copies:
    def __init__(self, send_sems, recv_sems):
        self.send_sems, self.recv_sems, self.made = send_sems, recv_sems, []

    def __call__(self, source, target, device):
        k = len(self.made)
        copy = pltpu.make_async_remote_copy(
            src_ref=source, dst_ref=target, send_sem=self.send_sems.at[k], recv_sem=self.recv_sems.at[k],
            device_id=device, device_id_type=MESH,
        )
        self.made.append(copy)
        return copy


class Reduction:
    def __init__(self, layer, tasks, remote, local_sems, refs):
        self.layer, self.tasks, self.remote, self.local_sems = layer, tasks, remote, local_sems
        self.grads, self.got, self.match, self.sums, self.got_sums, self.early, self.late, self.early_out, self.late_out = refs
        self.me, self.core = lax.axis_index("batch"), lax.axis_index("seq")
        self.line, self.place = self.me // LINE, self.me % LINE
        self.partner = {"seq": 1 - self.core}
        self.pairs = self.early.shape[1]
        self.share = self.got.shape[2]

    def rows(self, owner):
        return pl.ds(pl.multiple_of(owner * self.share, 16), self.share)

    def scatter(self):
        layer = self.layer
        self.copies = []
        for step in range(1, RAIL):
            target = (self.me + step) % RAIL
            source = self.grads.at[layer, self.rows(target)]
            self.copies.append(self.remote(source, self.got.at[layer, self.me], {"batch": target}))
        for copy in self.copies:
            copy.start()
        self.got[layer, self.me] = self.grads[layer, self.rows(self.me)]

    def add(self):
        layer = self.layer
        for copy in self.copies:
            copy.wait_recv()
        is_low = lax.broadcasted_iota(jnp.int32, (1, 2 * TAIL), 1) < TAIL
        for r in range(0, self.share, 16):

            def add_up(s, totals):
                part = self.got[layer, s, r : r + 16].astype(F32)
                match = self.match[s]
                return tuple(total + part * match[t : t + 1] for t, total in enumerate(totals))

            zero = jnp.zeros((16, 2 * TAIL), F32)
            totals = lax.fori_loop(0, RAIL, add_up, (zero,) * self.tasks)
            totals = [total + pltpu.roll(total, TAIL, 1) for total in totals]
            for pair in range(self.tasks // 2):
                self.sums[layer, pair, r : r + 16] = jnp.where(is_low, totals[2 * pair], totals[2 * pair + 1])
        theirs = self.sums.at[layer, pl.ds((1 - self.core) * self.pairs, self.pairs)]
        self.swap = self.remote(theirs, self.got_sums.at[layer], self.partner)
        self.swap.start()

    def spread(self):
        layer, core, line, place = self.layer, self.core, self.line, self.place
        self.swap.wait_recv()
        total = (self.sums[layer, pl.ds(core * self.pairs, self.pairs)] + self.got_sums[layer]).astype(BF)
        self.early[layer] = total[:, :EARLY]
        self.late[layer] = total[:, EARLY:]
        early_at, late_at = self.early_out.at[layer, core, line, place], self.late_out.at[layer, core, line, place]
        self.keeps = [
            pltpu.make_async_copy(self.early.at[layer], early_at, self.local_sems.at[2 * layer]),
            pltpu.make_async_copy(self.late.at[layer], late_at, self.local_sems.at[2 * layer + 1]),
        ]
        self.copies = []
        for step in range(1, LINE):
            to_line = {"batch": (line + step) % LINE * LINE + place}
            to_place = {"batch": line * LINE + (place + step) % LINE}
            self.copies.append(self.remote(self.early.at[layer], early_at, to_line))
            self.copies.append(self.remote(self.late.at[layer], late_at, to_place))
        for copy in self.copies + self.keeps:
            copy.start()

    def relay(self):
        layer, core, line, place = self.layer, self.core, self.line, self.place
        for copy in self.copies:
            copy.wait_recv()
        for copy in self.keeps:
            copy.wait()
        early_at, late_at = self.early_out.at[layer, core, :, place], self.late_out.at[layer, core, line]
        self.copies, self.handed = [], []
        for step in range(1, LINE):
            to_line = {"batch": (line + step) % LINE * LINE + place}
            to_place = {"batch": line * LINE + (place + step) % LINE}
            self.copies.append(self.remote(early_at, early_at, to_place))
            self.copies.append(self.remote(late_at, late_at, to_line))
        for at in (early_at, late_at):
            self.handed.append(self.remote(at, at, self.partner))
        for copy in self.copies + self.handed:
            copy.start()

    def hand_over(self):
        layer, core, line, place = self.layer, self.core, self.line, self.place
        for k, copy in enumerate(self.copies):
            back = RAIL - k // 2 - 1
            copy.wait_recv()
            if k % 2 == 0:
                at = self.early_out.at[layer, core, :, (place + back) % LINE]
            else:
                at = self.late_out.at[layer, core, (line + back) % LINE]
            self.handed.append(self.remote(at, at, self.partner))
            self.handed[-1].start()

    def close(self):
        for copy in self.handed:
            copy.wait_recv()


def encoder_kernel(
    own, patches, prompt_count, classes, reduce,
    task_ids, cls_in, cls_cot, logit_cot, head_bias, attn_bias, out_bias, up_bias, down_bias, gains, shifts,
    final_gain, final_bias,
    patch_hbm, cot_hbm, prompts_hbm, head_hbm, attn_hbm, out_hbm, up_hbm, down_hbm,
    y_out, dx_out, small_out, *rest,
):
    if reduce:
        early_out, late_out, messages_out = rest[:3]
        rest = rest[3:]
    else:
        grads, message = rest[:2]
        rest = rest[2:]
    (
        attn_w, out_w, up_w, down_w, x_ref, t_ref, a_ref, o_ref, wide_ref,
        mixed, scores_ref, qkv, probs, slope, unit1, unit2, inv_ref, unit_t, inv_t, table, prompt_rows,
        patch_own, patch_other, cot_other, y_own, y_other, small,
        weight_sems, local_sems, send_sems, recv_sems,
    ) = rest[:31]
    if reduce:
        grads, message, got, got_messages, match_ref, sums, got_sums, early, late, keep_sems = rest[31:]
    half = patches // 2
    cls_at = patches
    width = x_ref.shape[1]
    hidden = up_w.shape[2]
    queries = own * QUERY
    tasks = head_bias.shape[0]
    core = lax.axis_index("seq")
    me = lax.axis_index("batch")
    first = core * own
    partner = {"seq": 1 - core}
    remote = Copies(send_sems, recv_sems)

    weights = ((attn_hbm, attn_w), (out_hbm, out_w), (up_hbm, up_w), (down_hbm, down_w))

    def weight_copy(k, layer):
        source, target = weights[k]
        return pltpu.make_async_copy(source.at[layer], target.at[layer], weight_sems.at[k, layer])

    def local_copy(k, source, target):
        return pltpu.make_async_copy(source, target, local_sems.at[k])

    dx_ref = x_ref
    head_rows = head_hbm.shape[0]
    take_patches = local_copy(0, patch_hbm, patch_own)
    take_cots = local_copy(1, cot_hbm, patch_own)
    half_tasks = tasks // 2
    take_table = [local_copy(2, prompts_hbm.at[pl.ds(k * half_tasks, half_tasks)], table) for k in range(2)]
    take_head = local_copy(3, head_hbm, down_w.at[0, pl.ds(0, head_rows)])
    put_back = local_copy(4, down_hbm.at[0, pl.ds(0, head_rows)], down_w.at[0, pl.ds(0, head_rows)])
    keep_y = local_copy(5, y_own, y_out.at[pl.ds(first, own)])
    keep_small = local_copy(6, small, small_out.at[pl.ds(first, own)])
    swap_patches = remote(patch_hbm, patch_other, partner)
    swap_cots = remote(cot_hbm, cot_other, partner)
    swap_y = remote(y_other, y_out.at[pl.ds(first, own)], partner)
    swap_small = remote(small, small_out.at[pl.ds(first, own)], partner)

    take_patches.start()
    take_table[0].start()
    weight_copy(0, 0).start()
    barrier = pltpu.get_barrier_semaphore()
    peers = [partner]
    if reduce:
        peers += [{"batch": (me + step) % RAIL} for step in range(1, RAIL)]
    for peer in peers:
        pl.semaphore_signal(barrier, inc=1, device_id=peer, device_id_type=MESH)

    lane = lax.broadcasted_iota(jnp.int32, (1, PAIR), 1)
    is_low = lane < HEAD_DIM
    column = lax.broadcasted_iota(jnp.int32, (1, JOINT), 1)
    is_key = (column <= cls_at) | ((column >= PROMPT_AT) & (column < PROMPT_AT + prompt_count))
    key_bias = jnp.where(is_key, 0.0, -1e30).astype(F32)

    def stack_pair(block):
        zero = jnp.zeros_like(block)
        return jnp.concatenate([jnp.where(is_low, block, zero), jnp.where(is_low, zero, block)], 0)

    def merge_pair(block):
        return jnp.where(is_low, block[:QUERY], block[QUERY:])

    def places(n):
        i, h = n // PAIRS, n % PAIRS
        lanes = [slice(k * width + h * PAIR, k * width + (h + 1) * PAIR) for k in range(3)]
        return slice(i * JOINT, (i + 1) * JOINT), slice(i * QUERY, (i + 1) * QUERY), lanes

    def tails(ref, lanes):
        return jnp.concatenate([ref[i * JOINT + TAIL_AT : (i + 1) * JOINT, lanes] for i in range(own)], 0)

    def own_rows(ref, i):
        values = ref[...].astype(F32)
        return jnp.where(core == 0, values[:, i, :], values[:, own + i, :])

    def take_prompts(k):
        take_table[k].wait()
        for i in range(own):
            name = task_ids[first + i] - k * half_tasks
            entry = table[jnp.clip(name, 0, half_tasks - 1)].astype(F32)
            for layer in range(LAYERS):
                rows = entry[:, layer, :].astype(BF)
                if k == 0:
                    prompt_rows[layer, i] = rows
                else:
                    prompt_rows[layer, i] = jnp.where(name >= 0, rows, prompt_rows[layer, i])

    take_prompts(0)
    take_table[1].start()
    pl.semaphore_wait(barrier, len(peers))
    swap_patches.start()
    take_patches.wait()
    for i in range(own):
        at = i * JOINT
        x_ref[at + TAIL_AT : at + JOINT] = jnp.zeros((TAIL, width), F32)
        x_ref[at : at + half] = own_rows(patch_own, i)
        x_ref[at + cls_at : at + cls_at + 1] = pick_row(cls_in, first + i)
    take_prompts(1)
    swap_patches.wait_recv()
    for k in range(1, len(weights)):
        weight_copy(k, 0).start()
    for i in range(own):
        x_ref[i * JOINT + half : i * JOINT + patches] = own_rows(patch_other, i)

    def forward(layer):
        for i in range(own):
            at = i * JOINT + PROMPT_AT
            x_ref[at : at + prompt_count] = prompt_rows[layer, i].astype(F32)
        gain, shift = gains[layer, 0:1], shifts[layer, 0:1]
        for i in range(own):
            for r in range(0, JOINT, CHUNK):
                at, to = i * JOINT + r, i * QUERY + r
                unit, inverse = norm_parts(x_ref[at : at + CHUNK])
                a_ref[at : at + CHUNK] = (unit * gain + shift).astype(BF)
                kept = min(CHUNK, QUERY - r)
                if kept > 0:
                    unit1[layer, to : to + kept] = unit[:kept].astype(BF)
                    inv_ref[to : to + kept, 2 * layer : 2 * layer + 1] = inverse[:kept]
        weight_copy(0, layer).wait()
        bias = pick_row(attn_bias, layer)
        for n in range(3):
            part = slice(n * width, (n + 1) * width)
            qkv[layer, :, part] = (dot(a_ref[...], attn_w[layer, :, part], NN) + bias[:, part]).astype(BF)
        turned = tails(x_ref, slice(None)).T
        center = turned - jnp.mean(turned, 0, keepdims=True)
        inverse = lax.rsqrt(jnp.mean(center * center, 0, keepdims=True) + EPSILON)
        unit_t[layer] = (center * inverse).astype(BF)
        inv_t[layer] = inverse

        def mix(n):
            rows, tokens, lanes = places(n)
            values = qkv[layer, rows, lanes[2]]
            mixed[layer, tokens, lanes[0]] = merge_pair(dot(probs[layer, n], values, NN)).astype(BF)

        for n in range(own * PAIRS):
            rows, _, lanes = places(n)
            query = stack_pair(qkv[layer, rows.start : rows.start + QUERY, lanes[0]])
            scores = dot(query, qkv[layer, rows, lanes[1]], NT) * HEAD_DIM**-0.5 + key_bias
            expo = jnp.exp(scores - jnp.max(scores, -1, keepdims=True))
            probs[layer, n] = (expo * (1.0 / jnp.sum(expo, -1, keepdims=True))).astype(BF)
            if n > 0:
                mix(n - 1)
        mix(own * PAIRS - 1)
        weight_copy(1, layer).wait()
        if layer == 0:
            for k in range(len(weights)):
                weight_copy(k, 1).start()
        branch = dot(mixed[layer], out_w[layer], NN) + pick_row(out_bias, layer)
        for i in range(own):
            at, to = i * JOINT, i * QUERY
            t_ref[to : to + QUERY] = x_ref[at : at + QUERY] + branch[to : to + QUERY]
        gain, shift = gains[layer, 1:2], shifts[layer, 1:2]
        for r in range(0, queries, CHUNK):
            unit, inverse = norm_parts(t_ref[r : r + CHUNK])
            unit2[layer, r : r + CHUNK] = unit.astype(BF)
            inv_ref[r : r + CHUNK, 2 * layer + 1 : 2 * layer + 2] = inverse
            a_ref[r : r + CHUNK] = (unit * gain + shift).astype(BF)
        weight_copy(2, layer).wait()
        bias = pick_row(up_bias, layer)
        for c in range(0, hidden, HIDDEN_TILE):
            part = slice(c, c + HIDDEN_TILE)
            act, act_slope = gelu_and_slope(dot(a_ref[:queries], up_w[layer, :, part], NN) + bias[:, part])
            wide_ref[:queries, part] = act.astype(BF)
            slope[layer, :, part] = act_slope.astype(BF)
        weight_copy(3, layer).wait()
        result = t_ref[...] + (dot(wide_ref[:queries], down_w[layer], NN) + pick_row(down_bias, layer))
        for i in range(own):
            x_ref[i * JOINT : i * JOINT + QUERY] = result[i * QUERY : (i + 1) * QUERY]

    forward(0)
    swap_cots.start()
    take_cots.start()
    forward(1)
    take_head.start()

    for i in range(own):
        at = i * JOINT
        y_own[i] = x_ref[at : at + half].astype(BF)
        y_other[i] = x_ref[at + half : at + patches].astype(BF)
    swap_y.start()
    keep_y.start()

    lasts = [x_ref[i * JOINT + cls_at : i * JOINT + cls_at + 1] for i in range(own)]
    swap_cots.wait_recv()
    take_cots.wait()
    for i in range(own):
        to = i * QUERY
        dx_ref[to + TAIL_AT : to + QUERY] = jnp.zeros((QUERY - TAIL_AT, width), F32)
        dx_ref[to : to + half] = own_rows(patch_own, i)
        dx_ref[to + half : to + patches] = own_rows(cot_other, i)
    rows = -(-classes // 8) * 8
    row = lax.broadcasted_iota(jnp.int32, (own * rows, tasks * classes), 0)
    col = lax.broadcasted_iota(jnp.int32, (own * rows, tasks * classes), 1)
    task = jnp.where(row < rows, task_ids[first], task_ids[first + 1])
    pick = jnp.where(row < rows, row, row - rows) * tasks + task == col
    pick = jnp.where(pick, 1.0, 0.0).astype(BF)
    take_head.wait()
    own_head = dot(pick, down_w[0, :head_rows], NN).astype(BF)
    parts = []
    ends = []
    for i in range(own):
        to = i * QUERY
        matrix = own_head[i * rows : (i + 1) * rows]
        unit, inverse = norm_parts(lasts[i])
        feature = (unit * final_gain[...].reshape(1, width) + final_bias[...].reshape(1, width)).astype(BF)
        task = lax.broadcasted_iota(jnp.int32, (tasks, classes), 0) == task_ids[first + i]
        offset = jnp.sum(jnp.where(task, head_bias[...].astype(F32), 0.0), 0, keepdims=True)
        offset = jnp.concatenate([offset, jnp.zeros((1, width - classes), F32)], 1)
        score = dot(jnp.broadcast_to(feature, (16, width)), matrix, NT)[:1]
        score = jnp.concatenate([score, jnp.zeros((1, width - rows), F32)], 1) + offset
        small[i, 0:1] = lasts[i]
        small[i, 1:2] = score
        small[i, 3:8] = jnp.zeros((5, width), F32)
        cot = pick_row(logit_cot, first + i)
        cot = jnp.concatenate([cot, jnp.zeros((1, PAIR - classes), F32)], 1)
        grad = dot(jnp.broadcast_to(cot[:, :rows].astype(BF), (16, rows)), matrix, NN)[:1]
        dx_ref[to + cls_at : to + cls_at + 1] = pick_row(cls_cot, first + i) + norm_back(
            grad, final_gain[...].reshape(1, width), unit, inverse
        )
        parts += [feature.astype(F32)[:, j : j + PAIR] for j in range(0, width, PAIR)]
        ends.append(cot)
    names = jnp.where(is_low, task_ids[first], task_ids[first + 1]).astype(F32)
    message[...] = jnp.concatenate(parts + ends + [names, jnp.zeros((1, PAIR), F32)], 0).astype(BF)
    put_back.start()
    if reduce:
        refs = (grads, got, match_ref, sums, got_sums, early, late, early_out, late_out)
        sums_of = [Reduction(layer, tasks, remote, keep_sems, refs) for layer in range(LAYERS)]
        give_messages = []
        for step in range(1, RAIL):
            give_messages.append(remote(message, got_messages.at[me], {"batch": (me + step) % RAIL}))
        for copy in give_messages:
            copy.start()
        got_messages[me] = message[...]

    def backward(layer, hooks):
        a_ref[:queries] = dx_ref[:queries].astype(BF)
        hooks[0]()
        for c in range(0, hidden, HIDDEN_TILE):
            part = slice(c, c + HIDDEN_TILE)
            grad = dot(a_ref[:queries], down_w[layer, part], NT)
            wide_ref[:queries, part] = (grad * slope[layer, :, part].astype(F32)).astype(BF)
        hooks[1]()
        t_ref[...] = dot(wide_ref[:queries], up_w[layer], NT)
        hooks[2]()
        gain = gains[layer, 1:2]
        for r in range(0, queries, CHUNK):
            part = slice(r, r + CHUNK)
            inverse = inv_ref[part, 2 * layer + 1 : 2 * layer + 2]
            total = dx_ref[part] + norm_back(t_ref[part], gain, unit2[layer, part].astype(F32), inverse)
            dx_ref[part] = total
            a_ref[part] = total.astype(BF)
        o_ref[...] = dot(a_ref[:queries], out_w[layer], NT).astype(BF)

        def key_grad(n):
            rows, _, lanes = places(n)
            query = stack_pair(qkv[layer, rows.start : rows.start + QUERY, lanes[0]])
            grad_score = scores_ref[n % 2]
            grad_key = dot(query, grad_score, TN) * HEAD_DIM**-0.5
            wide_ref[rows, lanes[1]] = grad_key.astype(BF).T
            grad_query = dot(grad_score, qkv[layer, rows, lanes[1]], NN) * HEAD_DIM**-0.5
            wide_ref[rows.start : rows.start + QUERY, lanes[0]] = merge_pair(grad_query).astype(BF)

        for n in range(own * PAIRS):
            rows, tokens, lanes = places(n)
            grad = stack_pair(o_ref[tokens, lanes[0]])
            twice = jnp.concatenate([mixed[layer, tokens, lanes[0]]] * 2, 0)
            center = jnp.sum(grad.astype(F32) * twice.astype(F32), -1, keepdims=True)
            grad_prob = dot(grad, qkv[layer, rows, lanes[2]], NT)
            prob = probs[layer, n]
            scores_ref[n % 2] = (prob.astype(F32) * (grad_prob - center)).astype(BF)
            wide_ref[rows, lanes[2]] = dot(grad, prob, TN).astype(BF).T
            if n > 0:
                key_grad(n - 1)
            if n == PAIRS:
                hooks[3]()
        key_grad(own * PAIRS - 1)
        gain = gains[layer, 0:1]
        gain_t = jnp.broadcast_to(gain, (PAIR, width)).T
        scaled = dot(attn_w[layer, :, width:], tails(wide_ref, slice(width, 3 * width)), NT) * gain_t
        unit = unit_t[layer].astype(F32)
        mean = jnp.mean(scaled, 0, keepdims=True)
        mean_unit = jnp.mean(scaled * unit, 0, keepdims=True)
        grads[layer] = (inv_t[layer] * (scaled - mean - unit * mean_unit)).astype(BF)
        hooks[4]()
        rows = [wide_ref[i * JOINT : i * JOINT + QUERY, : 3 * width] for i in range(own)]
        t_ref[...] = dot(jnp.concatenate(rows, 0), attn_w[layer], NT)
        for i in range(own):
            to = i * QUERY
            for r in range(0, QUERY, 16):
                part = slice(to + r, to + r + 16)
                inverse = inv_ref[part, 2 * layer : 2 * layer + 1]
                grad = norm_back(t_ref[part], gain, unit1[layer, part].astype(F32), inverse)
                if r + 16 > cls_at:
                    keep = lax.broadcasted_iota(jnp.int32, (16, 1), 0) + r <= cls_at
                    grad = jnp.where(keep, grad, 0.0)
                dx_ref[part] += grad

    def nothing():
        pass

    def add_last():
        for copy in give_messages:
            copy.wait_recv()
        order = lax.broadcasted_iota(jnp.int32, (tasks, PAIR), 0).astype(F32)
        for s in range(RAIL):
            match_ref[s] = jnp.where(got_messages[s, 14:15].astype(F32) == order, 1.0, 0.0)
        sums_of[1].add()

    if reduce:
        backward(1, [nothing, nothing, nothing, nothing, sums_of[1].scatter])
        put_back.wait()
        backward(0, [nothing, nothing, add_last, sums_of[1].spread, sums_of[0].scatter])
    else:
        backward(1, [nothing] * 5)
        put_back.wait()
        backward(0, [nothing] * 5)

    keep_dx, swap_dx = [], []
    padded = dx_out.shape[1]
    for i in range(own):
        to = i * QUERY
        t_ref[to : to + half] = dx_ref[to + half : to + patches]
        small[i, 2:3] = dx_ref[to + cls_at : to + cls_at + 1]
        keep_dx.append(local_copy(7 + i, dx_ref.at[pl.ds(to, padded)], dx_out.at[first + i]))
        swap_dx.append(remote(t_ref.at[pl.ds(to, padded)], dx_out.at[first + i], partner))
        swap_dx[i].start()
        keep_dx[i].start()
    swap_small.start()
    keep_small.start()
    if reduce:
        last, first_layer = sums_of[1], sums_of[0]
        last.relay()
        first_layer.add()
        swap_messages = remote(got_messages, messages_out.at[core], partner)
        keep_messages = local_copy(7 + own, got_messages, messages_out.at[core])
        swap_messages.start()
        keep_messages.start()
        first_layer.spread()
        last.hand_over()
        first_layer.relay()
        first_layer.hand_over()
        last.close()
        first_layer.close()
        swap_messages.wait_recv()
        keep_messages.wait()
    for copy in [swap_y, swap_small] + swap_dx:
        copy.wait_recv()
    for copy in [keep_y, keep_small] + keep_dx:
        copy.wait()
    for copy in remote.made:
        copy.wait_send()


def run_encoder(
    reduce, task_ids, patch_input, cls_input, patch_cotangent, cls_cotangent, logit_cotangent, prompts, head_weight,
    head_bias, attn_weight, attn_bias, out_weight, out_bias, up_weight, up_bias, down_weight, down_bias,
    gains, shifts, final_gain, final_bias, own,
):
    images, half, width = patch_input.shape
    tasks, classes = head_bias.shape
    prompt_count = prompts.shape[2]
    hidden = up_weight.shape[2]
    queries, joints = own * QUERY, own * JOINT
    lanes = own * TAIL
    pairs = tasks // 4
    share = width // RAIL
    shape = jax.ShapeDtypeStruct
    vmem = pl.BlockSpec(memory_space=pltpu.VMEM)
    anywhere = pl.BlockSpec(memory_space=pl.ANY)
    table = prompts.transpose(0, 2, 1, 3)
    head_rows = head_weight.transpose(2, 1, 0).reshape(-1, width)
    outs = [
        shape((images, half, width), BF),
        shape((images, -(-half // 8) * 8, width), F32),
        shape((images, 8, width), F32),
    ]
    out_specs = [anywhere] * 3
    scratch = [
        pltpu.VMEM(attn_weight.shape, BF),
        pltpu.VMEM(out_weight.shape, BF),
        pltpu.VMEM(up_weight.shape, BF),
        pltpu.VMEM(down_weight.shape, BF),
        pltpu.VMEM((joints, width), F32),
        pltpu.VMEM((queries, width), F32),
        pltpu.VMEM((joints, width), BF),
        pltpu.VMEM((queries, width), BF),
        pltpu.VMEM((joints, hidden), BF),
        pltpu.VMEM((LAYERS, queries, width), BF),
        pltpu.VMEM((2, 2 * QUERY, JOINT), BF),
        pltpu.VMEM((LAYERS, joints, 3 * width), BF),
        pltpu.VMEM((LAYERS, own * PAIRS, 2 * QUERY, JOINT), BF),
        pltpu.VMEM((LAYERS, queries, hidden), BF),
        pltpu.VMEM((LAYERS, queries, width), BF),
        pltpu.VMEM((LAYERS, queries, width), BF),
        pltpu.VMEM((queries, 2 * LAYERS), F32),
        pltpu.VMEM((LAYERS, width, lanes), BF),
        pltpu.VMEM((LAYERS, 1, lanes), F32),
        pltpu.VMEM((tasks // 2,) + table.shape[1:], BF),
        pltpu.VMEM((LAYERS, own, prompt_count, width), BF),
        pltpu.VMEM((half, images, width), BF),
        pltpu.VMEM((half, images, width), BF),
        pltpu.VMEM((half, images, width), BF),
        pltpu.VMEM((own, half, width), BF),
        pltpu.VMEM((own, half, width), BF),
        pltpu.VMEM((own, 8, width), F32),
        pltpu.SemaphoreType.DMA((4, LAYERS)),
        pltpu.SemaphoreType.DMA((8 + own,)),
    ]
    if reduce:
        steps = 6 * (LINE - 1) + 3
        count = 4 + own + RAIL + LAYERS * (RAIL - 1 + steps)
        outs += [
            shape((LAYERS, 2, LINE, LINE, pairs, EARLY, lanes), BF),
            shape((LAYERS, 2, LINE, LINE, pairs, share - EARLY, lanes), BF),
            shape((2, RAIL, 16, PAIR), BF),
        ]
        out_specs += [anywhere] * 3
        scratch += [
            pltpu.SemaphoreType.DMA((count,)),
            pltpu.SemaphoreType.DMA((count,)),
            pltpu.VMEM((LAYERS, width, lanes), BF),
            pltpu.VMEM((16, PAIR), BF),
            pltpu.VMEM((LAYERS, RAIL, share, lanes), BF),
            pltpu.VMEM((RAIL, 16, PAIR), BF),
            pltpu.VMEM((RAIL, tasks, PAIR), F32),
            pltpu.VMEM((LAYERS, 2 * pairs, share, lanes), F32),
            pltpu.VMEM((LAYERS, pairs, share, lanes), F32),
            pltpu.VMEM((LAYERS, pairs, EARLY, lanes), BF),
            pltpu.VMEM((LAYERS, pairs, share - EARLY, lanes), BF),
            pltpu.SemaphoreType.DMA((2 * LAYERS,)),
        ]
    else:
        outs += [shape((LAYERS, width, lanes), BF), shape((16, PAIR), BF)]
        out_specs += [vmem] * 2
        scratch += [pltpu.SemaphoreType.DMA((4 + own,)), pltpu.SemaphoreType.DMA((4 + own,))]

    def kernel(*refs):
        encoder_kernel(own, 2 * half, prompt_count, classes, reduce, *refs)

    return pl.pallas_call(
        kernel,
        out_shape=outs,
        in_specs=[pl.BlockSpec(memory_space=pltpu.SMEM)] + [vmem] * 12 + [anywhere] * 8,
        out_specs=out_specs,
        scratch_shapes=scratch,
        compiler_params=pltpu.CompilerParams(vmem_limit_bytes=64 << 20, collective_id=0, has_side_effects=True),
        name="encoder",
    )(
        task_ids, cls_input, cls_cotangent, logit_cotangent, head_bias, attn_bias, out_bias, up_bias, down_bias,
        gains, shifts, final_gain, final_bias,
        patch_input.transpose(1, 0, 2), patch_cotangent.transpose(1, 0, 2), table, head_rows,
        attn_weight, out_weight, up_weight, down_weight,
    )


def finish_kernel(
    own, prompt_count, early_hbm, late_hbm, messages_hbm, small, y_hbm, dx_hbm,
    prompt_hbm, head_hbm, bias_grad, y_cls, logits, dx_cls, y_patch_hbm, dx_patch_hbm,
    early, late, messages, y, dx, prompt_grad, head_grad, y_patch, dx_patch, rows_ref, left_ref, features_ref, sems,
):
    classes, tasks, width = head_grad.shape
    devices = 2 * RAIL
    count = own * devices
    pairs = early.shape[4]
    class_part = classes // FINISH_PARTS
    copies = []

    def copy(source, target):
        copies.append(pltpu.make_async_copy(source, target, sems.at[len(copies)]))
        copies[-1].start()
        return copies[-1]

    take_messages = copy(messages_hbm, messages)
    take_dx, take_y = copy(dx_hbm, dx), copy(y_hbm, y)
    takes = []
    for side in range(2):
        for layer in range(LAYERS):
            takes.append(copy(early_hbm.at[layer, side], early.at[layer, side]))
            takes.append(copy(late_hbm.at[layer, side], late.at[layer, side]))
    gives = []

    y_cls[...] = small[:, 0, :].astype(BF)
    logits[...] = small[:, 1, : logits.shape[1]].astype(BF)
    dx_cls[...] = small[:, 2, :]

    def gather(k):
        return rows_ref[pl.ds(k, devices, stride=16)]

    take_messages.wait()
    rows_ref[...] = messages[...].astype(F32).reshape(rows_ref.shape)
    chunks = width // PAIR
    for i in range(own):
        for j in range(chunks):
            rows = slice(i * devices, (i + 1) * devices)
            features_ref[rows, j * PAIR : (j + 1) * PAIR] = gather(i * chunks + j).astype(BF)
    cots = jnp.concatenate([gather(own * chunks + i) for i in range(own)], 0)
    ids = gather(own * chunks + own).T
    ids = jnp.concatenate([ids[i * TAIL : i * TAIL + 1] for i in range(own)], 1)
    match = jnp.where(lax.broadcasted_iota(jnp.int32, (tasks, count), 0).astype(F32) == ids, 1.0, 0.0)
    cots_t = cots.T[:classes]
    left_ref[...] = (cots_t[:, None, :] * match[None]).astype(BF)
    for k in range(FINISH_PARTS):
        part = slice(k * class_part, (k + 1) * class_part)
        left = left_ref[part].reshape(class_part * tasks, count)
        head_grad[part] = dot(left, features_ref[...], NN).reshape(class_part, tasks, width)
        gives.append(copy(head_grad.at[part], head_hbm.at[part]))
    total = dot(match.astype(BF), cots.astype(BF), NN)
    bias_grad[...] = total[:, :classes]

    take_dx.wait()
    take_y.wait()
    for i in range(y.shape[0]):
        dx_patch[:, i, :] = dx[i, : y.shape[1]]
        y_patch[:, i, :] = y[i]
    gives.append(copy(dx_patch, dx_patch_hbm))
    gives.append(copy(y_patch, y_patch_hbm))

    row = lax.broadcasted_iota(jnp.int32, (2 * TAIL, 2 * TAIL), 0)
    col = lax.broadcasted_iota(jnp.int32, (2 * TAIL, 2 * TAIL), 1)
    turn = jnp.where(row == col, 1.0, 0.0).astype(BF)
    start = PROMPT_AT - TAIL_AT
    for core in range(2):
        for take in takes[2 * LAYERS * core : 2 * LAYERS * (core + 1)]:
            take.wait()
        for k in range(pairs):
            task = 2 * (core * pairs + k)
            for layer in range(LAYERS):
                blocks = []
                for b in range(RAIL):
                    blocks.append(early[layer, core, b // LINE, b % LINE, k])
                    blocks.append(late[layer, core, b // LINE, b % LINE, k])
                both = dot(turn, jnp.concatenate(blocks, 0), NT)
                for side in range(2):
                    at = side * TAIL + start
                    prompt_grad[task + side, :, layer, :] = both[at : at + prompt_count]
            part = slice(task, task + 2)
            gives.append(copy(prompt_grad.at[part], prompt_hbm.at[part]))
    for give in gives:
        give.wait()


def run_finish(early, late, messages, small, y, dx, prompt_count, class_count, own):
    layers, cores, _, _, pairs, _, lanes = early.shape
    width = RAIL * (early.shape[5] + late.shape[5])
    tasks = 2 * cores * pairs
    images, half = y.shape[:2]
    shape = jax.ShapeDtypeStruct
    vmem = pl.BlockSpec(memory_space=pltpu.VMEM)
    anywhere = pl.BlockSpec(memory_space=pl.ANY)
    prompt_shape, head_shape = (tasks, prompt_count, layers, width), (class_count, tasks, width)
    patch_shape = (half, images, width)

    def kernel(*refs):
        finish_kernel(own, prompt_count, *refs)

    return pl.pallas_call(
        kernel,
        out_shape=(
            shape(prompt_shape, F32),
            shape(head_shape, F32),
            shape((tasks, class_count), F32),
            shape((images, width), BF),
            shape((images, class_count), BF),
            shape((images, width), F32),
            shape(patch_shape, BF),
            shape(patch_shape, F32),
        ),
        in_specs=[anywhere] * 3 + [vmem] + [anywhere] * 2,
        out_specs=[anywhere] * 2 + [vmem] * 4 + [anywhere] * 2,
        scratch_shapes=[
            pltpu.VMEM(early.shape, BF),
            pltpu.VMEM(late.shape, BF),
            pltpu.VMEM(messages.shape, BF),
            pltpu.VMEM(y.shape, BF),
            pltpu.VMEM(dx.shape, F32),
            pltpu.VMEM(prompt_shape, F32),
            pltpu.VMEM(head_shape, F32),
            pltpu.VMEM(patch_shape, BF),
            pltpu.VMEM(patch_shape, F32),
            pltpu.VMEM((2 * RAIL * 16, PAIR), F32),
            pltpu.VMEM((class_count, tasks, own * 2 * RAIL), BF),
            pltpu.VMEM((own * 2 * RAIL, width), BF),
            pltpu.SemaphoreType.DMA((3 + 4 * layers + FINISH_PARTS + 2 + cores * pairs,)),
        ],
        compiler_params=pltpu.CompilerParams(vmem_limit_bytes=62 << 20),
        name="finish",
    )(early, late, messages, small, y, dx)


def gathered_sums(grads, message, own_ids, task_ids, logit_cot, prompt_count, tasks):
    layers, width, lanes = grads.shape
    own = own_ids.shape[0]
    start = PROMPT_AT - TAIL_AT
    parts = grads.reshape(layers, width, own, TAIL)[..., start : start + prompt_count].astype(F32)
    names = jnp.arange(tasks, dtype=jnp.int32)[None, :]
    onehot = (own_ids[:, None] == names).astype(F32)
    dense = jnp.einsum("it,ldip->tlpd", onehot, parts, precision=lax.Precision.HIGHEST)
    prompt_grad = lax.psum(dense, ("batch", "seq"))
    features = message[: own * width // PAIR].reshape(own, width)
    features = lax.all_gather(features, ("batch", "seq"), axis=0, tiled=True)
    cots = lax.all_gather(logit_cot, "batch", axis=0, tiled=True)
    ids = lax.all_gather(task_ids.astype(F32), "batch", axis=0, tiled=True).astype(jnp.int32)
    match = (ids[:, None] == names).astype(BF)
    head_grad = jnp.einsum("id,it,ic->dtc", features, match, cots, preferred_element_type=F32)
    bias_grad = jnp.einsum("it,ic->tc", match, cots, preferred_element_type=F32)
    return prompt_grad, head_grad, bias_grad


def per_device(
    cls_input, patch_input, task_ids, prompts, attn_weight, attn_bias, out_weight, out_bias, up_weight, up_bias,
    down_weight, down_bias, norm_gain, norm_bias, final_gain, final_bias, head_weight, head_bias,
    cls_cotangent, patch_cotangent, logit_cotangent,
):
    cores = lax.axis_size("seq")
    core = lax.axis_index("seq")
    images, width = cls_input.shape
    own = images // cores
    tasks, class_count = head_bias.shape
    prompt_count = prompts.shape[2]
    reduce = lax.axis_size("batch") == RAIL
    y, dx, small, *sums = run_encoder(
        reduce, task_ids, patch_input, cls_input, patch_cotangent, cls_cotangent, logit_cotangent, prompts,
        head_weight, head_bias, attn_weight, attn_bias, out_weight, out_bias, up_weight, up_bias,
        down_weight, down_bias, norm_gain, norm_bias, final_gain, final_bias, own,
    )
    if reduce:
        prompt_grad, head_grad, bias_grad, y_cls, logits, dx_cls, y, dx = run_finish(
            *sums, small, y, dx, prompt_count, class_count, own
        )
        prompt_grad = prompt_grad.transpose(0, 2, 1, 3)
        head_grad = head_grad.transpose(2, 1, 0)
        y, dx = y.transpose(1, 0, 2), dx.transpose(1, 0, 2)
    else:
        own_ids = lax.dynamic_slice_in_dim(task_ids, core * own, own, 0)
        prompt_grad, head_grad, bias_grad = gathered_sums(
            *sums, own_ids, task_ids, logit_cotangent, prompt_count, tasks
        )
        y_cls, logits, dx_cls = small[:, 0].astype(BF), small[:, 1, :class_count].astype(BF), small[:, 2]
        dx = dx[:, : patch_input.shape[1]]
    return y_cls, y, logits, dx_cls, dx, prompt_grad, head_grad, bias_grad


def solution(mesh):
    rows, tokens, whole = P("batch", None), P("batch", "seq", None), P()
    return jax.shard_map(
        per_device,
        mesh=mesh,
        in_specs=(rows, tokens, P("batch")) + (whole,) * 15 + (rows, tokens, rows),
        out_specs=(rows, tokens, rows, rows, tokens, whole, whole, whole),
        check_vma=False,
    )
```

```python
import jax
import jax.numpy as jnp
from jax import lax
from jax.experimental import pallas as pl
from jax.experimental.pallas import tpu as pltpu
from jax.sharding import PartitionSpec as P

HEADS = 12
HEAD_DIM = 64
LAYERS = 2
EPSILON = 1e-06
BF = jnp.bfloat16
F32 = jnp.float32

JOINT = 256
QUERY = 208
PROMPT_AT = 200
PAIR = 2 * HEAD_DIM
PAIRS = HEADS // 2
CHUNK = 32
HIDDEN_TILE = 512

TAIL = 64
TAIL_AT = JOINT - TAIL
RAIL = 16
LINE = 4
EARLY = 32
FINISH_PARTS = 4
MESH = pl.DeviceIdType.MESH

NN = (((1,), (0,)), ((), ()))
NT = (((1,), (1,)), ((), ()))
TN = (((0,), (0,)), ((), ()))


def dot(left, right, dims):
    return lax.dot_general(left, right, dims, preferred_element_type=F32)


def gelu_and_slope(u):
    phi = 0.5 + 0.5 * lax.erf(u * 0.7071067811865476)
    return u * phi, phi + u * (0.3989422804014327 * jnp.exp(-0.5 * u * u))


def norm_parts(x):
    center = x - jnp.mean(x, -1, keepdims=True)
    inverse = lax.rsqrt(jnp.mean(center * center, -1, keepdims=True) + EPSILON)
    return center * inverse, inverse


def norm_back(grad, gain, unit, inverse):
    scaled = grad * gain
    first = jnp.mean(scaled, -1, keepdims=True)
    second = jnp.mean(scaled * unit, -1, keepdims=True)
    return inverse * (scaled - first - unit * second)


def pick_row(ref, index):
    values = ref[...].astype(F32)
    rows = lax.broadcasted_iota(jnp.int32, values.shape, 0)
    return jnp.sum(jnp.where(rows == index, values, 0.0), 0, keepdims=True)


class Copies:
    def __init__(self, send_sems, recv_sems):
        self.send_sems, self.recv_sems, self.made = send_sems, recv_sems, []

    def __call__(self, source, target, device):
        k = len(self.made)
        copy = pltpu.make_async_remote_copy(
            src_ref=source, dst_ref=target, send_sem=self.send_sems.at[k], recv_sem=self.recv_sems.at[k],
            device_id=device, device_id_type=MESH,
        )
        self.made.append(copy)
        return copy


class Reduction:
    def __init__(self, layer, tasks, remote, local_sems, refs):
        self.layer, self.tasks = layer, tasks
        self.grads, self.got, self.match, self.sums, self.got_sums, self.early, self.late, early_out, late_out = refs
        self.me, core = lax.axis_index("batch"), lax.axis_index("seq")
        line, place = self.me // LINE, self.me % LINE
        partner = {"seq": 1 - core}
        pairs = self.early.shape[1]
        self.share = self.got.shape[2]
        self.mine = pl.ds(core * pairs, pairs)
        targets = [(self.me + step) % RAIL for step in range(RAIL)]
        self.rows = [pl.ds(pl.multiple_of(target * self.share, 16), self.share) for target in targets]
        self.scattered = [
            remote(self.grads.at[layer, self.rows[k]], self.got.at[layer, self.me], {"batch": targets[k]})
            for k in range(1, RAIL)
        ]
        theirs = self.sums.at[layer, pl.ds((1 - core) * pairs, pairs)]
        self.swap = remote(theirs, self.got_sums.at[layer], partner)
        early_at, late_at = early_out.at[layer, core, line, place], late_out.at[layer, core, line, place]
        self.keeps = [
            pltpu.make_async_copy(self.early.at[layer], early_at, local_sems.at[2 * layer]),
            pltpu.make_async_copy(self.late.at[layer], late_at, local_sems.at[2 * layer + 1]),
        ]
        to_line = [{"batch": (line + step) % LINE * LINE + place} for step in range(LINE)]
        to_place = [{"batch": line * LINE + (place + step) % LINE} for step in range(LINE)]
        self.spreads, self.relays = [], []
        for step in range(1, LINE):
            self.spreads.append(remote(self.early.at[layer], early_at, to_line[step]))
            self.spreads.append(remote(self.late.at[layer], late_at, to_place[step]))
        early_at, late_at = early_out.at[layer, core, :, place], late_out.at[layer, core, line]
        self.handed = [remote(at, at, partner) for at in (early_at, late_at)]
        for step in range(1, LINE):
            self.relays.append(remote(early_at, early_at, to_place[step]))
            self.relays.append(remote(late_at, late_at, to_line[step]))
        for step in range(1, LINE):
            for at in (
                early_out.at[layer, core, :, (place + LINE - step) % LINE],
                late_out.at[layer, core, (line + LINE - step) % LINE],
            ):
                self.handed.append(remote(at, at, partner))

    def scatter(self):
        for copy in self.scattered:
            copy.start()
        self.got[self.layer, self.me] = self.grads[self.layer, self.rows[0]]

    def add(self):
        layer = self.layer
        for copy in self.scattered:
            copy.wait_recv()
        is_low = lax.broadcasted_iota(jnp.int32, (1, 2 * TAIL), 1) < TAIL
        for r in range(0, self.share, 16):

            def add_up(s, totals):
                part = self.got[layer, s, r : r + 16].astype(F32)
                match = self.match[s]
                return tuple(total + part * match[t : t + 1] for t, total in enumerate(totals))

            zero = jnp.zeros((16, 2 * TAIL), F32)
            totals = lax.fori_loop(0, RAIL, add_up, (zero,) * self.tasks)
            totals = [total + pltpu.roll(total, TAIL, 1) for total in totals]
            for pair in range(self.tasks // 2):
                self.sums[layer, pair, r : r + 16] = jnp.where(is_low, totals[2 * pair], totals[2 * pair + 1])
        self.swap.start()

    def spread(self):
        layer = self.layer
        self.swap.wait_recv()
        total = (self.sums[layer, self.mine] + self.got_sums[layer]).astype(BF)
        self.early[layer] = total[:, :EARLY]
        self.late[layer] = total[:, EARLY:]
        for copy in self.spreads + self.keeps:
            copy.start()

    def relay(self):
        for copy in self.spreads:
            copy.wait_recv()
        for copy in self.keeps:
            copy.wait()
        for copy in self.relays + self.handed[:2]:
            copy.start()

    def hand_over(self):
        for k, copy in enumerate(self.relays):
            copy.wait_recv()
            self.handed[2 + k].start()

    def close(self):
        for copy in self.handed:
            copy.wait_recv()


def encoder_kernel(
    own, patches, prompt_count, classes, reduce,
    task_ids, cls_in, cls_cot, logit_cot, head_bias, attn_bias, out_bias, up_bias, down_bias, gains, shifts,
    final_gain, final_bias,
    patch_hbm, cot_hbm, prompts_hbm, head_hbm, attn_hbm, out_hbm, up_hbm, down_hbm,
    y_out, dx_out, small_out, *rest,
):
    if reduce:
        early_out, late_out, messages_out = rest[:3]
        rest = rest[3:]
    else:
        grads, message = rest[:2]
        rest = rest[2:]
    (
        attn_w, out_w, up_w, down_w, x_ref, t_ref, a_ref, o_ref, wide_ref,
        mixed, scores_ref, qkv, probs, slope, unit1, unit2, inv_ref, unit_t, inv_t, table, prompt_rows,
        patch_own, patch_other, cot_other, y_own, y_other, small,
        weight_sems, local_sems, send_sems, recv_sems,
    ) = rest[:31]
    if reduce:
        grads, message, got, got_messages, match_ref, sums, got_sums, early, late, keep_sems = rest[31:]
    half = patches // 2
    cls_at = patches
    width = x_ref.shape[1]
    hidden = up_w.shape[2]
    queries = own * QUERY
    tasks = head_bias.shape[0]
    core = lax.axis_index("seq")
    me = lax.axis_index("batch")
    first = core * own
    partner = {"seq": 1 - core}
    remote = Copies(send_sems, recv_sems)

    weights = ((attn_hbm, attn_w), (out_hbm, out_w), (up_hbm, up_w), (down_hbm, down_w))

    def weight_copy(k, layer):
        source, target = weights[k]
        return pltpu.make_async_copy(source.at[layer], target.at[layer], weight_sems.at[k, layer])

    def local_copy(k, source, target):
        return pltpu.make_async_copy(source, target, local_sems.at[k])

    dx_ref = x_ref
    head_rows = head_hbm.shape[0]
    take_patches = local_copy(0, patch_hbm, patch_own)
    take_cots = local_copy(1, cot_hbm, patch_own)
    half_tasks = tasks // 2
    take_table = [local_copy(2, prompts_hbm.at[pl.ds(k * half_tasks, half_tasks)], table) for k in range(2)]
    take_head = local_copy(3, head_hbm, down_w.at[0, pl.ds(0, head_rows)])
    put_back = local_copy(4, down_hbm.at[0, pl.ds(0, head_rows)], down_w.at[0, pl.ds(0, head_rows)])
    keep_y = local_copy(5, y_own, y_out.at[pl.ds(first, own)])
    keep_small = local_copy(6, small, small_out.at[pl.ds(first, own)])
    swap_patches = remote(patch_hbm, patch_other, partner)
    swap_cots = remote(cot_hbm, cot_other, partner)
    swap_y = remote(y_other, y_out.at[pl.ds(first, own)], partner)
    swap_small = remote(small, small_out.at[pl.ds(first, own)], partner)

    take_patches.start()
    take_table[0].start()
    weight_copy(0, 0).start()
    barrier = pltpu.get_barrier_semaphore()
    peers = [partner]
    if reduce:
        peers += [{"batch": (me + step) % RAIL} for step in range(1, RAIL)]
    for peer in peers:
        pl.semaphore_signal(barrier, inc=1, device_id=peer, device_id_type=MESH)

    lane = lax.broadcasted_iota(jnp.int32, (1, PAIR), 1)
    is_low = lane < HEAD_DIM
    column = lax.broadcasted_iota(jnp.int32, (1, JOINT), 1)
    is_key = (column <= cls_at) | ((column >= PROMPT_AT) & (column < PROMPT_AT + prompt_count))
    key_bias = jnp.where(is_key, 0.0, -1e30).astype(F32)

    def stack_pair(block):
        zero = jnp.zeros_like(block)
        return jnp.concatenate([jnp.where(is_low, block, zero), jnp.where(is_low, zero, block)], 0)

    def merge_pair(block):
        return jnp.where(is_low, block[:QUERY], block[QUERY:])

    def places(n):
        i, h = n // PAIRS, n % PAIRS
        lanes = [slice(k * width + h * PAIR, k * width + (h + 1) * PAIR) for k in range(3)]
        return slice(i * JOINT, (i + 1) * JOINT), slice(i * QUERY, (i + 1) * QUERY), lanes

    def tails(ref, lanes):
        return jnp.concatenate([ref[i * JOINT + TAIL_AT : (i + 1) * JOINT, lanes] for i in range(own)], 0)

    def own_rows(ref, i):
        values = ref[...].astype(F32)
        return jnp.where(core == 0, values[:, i, :], values[:, own + i, :])

    def take_prompts(k):
        take_table[k].wait()
        for i in range(own):
            name = task_ids[first + i] - k * half_tasks
            entry = table[jnp.clip(name, 0, half_tasks - 1)].astype(F32)
            for layer in range(LAYERS):
                rows = entry[:, layer, :].astype(BF)
                if k == 0:
                    prompt_rows[layer, i] = rows
                else:
                    prompt_rows[layer, i] = jnp.where(name >= 0, rows, prompt_rows[layer, i])

    take_prompts(0)
    take_table[1].start()
    pl.semaphore_wait(barrier, len(peers))
    swap_patches.start()
    take_patches.wait()
    for i in range(own):
        at = i * JOINT
        x_ref[at + TAIL_AT : at + JOINT] = jnp.zeros((TAIL, width), F32)
        x_ref[at : at + half] = own_rows(patch_own, i)
        x_ref[at + cls_at : at + cls_at + 1] = pick_row(cls_in, first + i)
    take_prompts(1)
    swap_patches.wait_recv()
    for k in range(1, len(weights)):
        weight_copy(k, 0).start()
    for i in range(own):
        x_ref[i * JOINT + half : i * JOINT + patches] = own_rows(patch_other, i)

    def forward(layer, carry):
        for i in range(own):
            at = i * JOINT + PROMPT_AT
            x_ref[at : at + prompt_count] = prompt_rows[layer, i].astype(F32)
        gain, shift = gains[layer, 0:1], shifts[layer, 0:1]
        for i in range(own):
            for r in range(0, JOINT, CHUNK):
                at, to = i * JOINT + r, i * QUERY + r
                unit, inverse = norm_parts(x_ref[at : at + CHUNK])
                a_ref[at : at + CHUNK] = (unit * gain + shift).astype(BF)
                kept = min(CHUNK, QUERY - r)
                if kept > 0:
                    unit1[layer, to : to + kept] = unit[:kept].astype(BF)
                    inv_ref[layer, to : to + kept, 0:1] = inverse[:kept]
        weight_copy(0, layer).wait()
        bias = pick_row(attn_bias, layer)
        for n in range(3):
            part = slice(n * width, (n + 1) * width)
            qkv[layer, :, part] = (dot(a_ref[...], attn_w[layer, :, part], NN) + bias[:, part]).astype(BF)
        turned = tails(x_ref, slice(None)).T
        center = turned - jnp.mean(turned, 0, keepdims=True)
        inverse = lax.rsqrt(jnp.mean(center * center, 0, keepdims=True) + EPSILON)
        unit_t[layer] = (center * inverse).astype(BF)
        inv_t[layer] = inverse

        def mix(n):
            rows, tokens, lanes = places(n)
            values = qkv[layer, rows, lanes[2]]
            mixed[layer, tokens, lanes[0]] = merge_pair(dot(probs[layer, n], values, NN)).astype(BF)

        for n in range(own * PAIRS):
            rows, _, lanes = places(n)
            query = stack_pair(qkv[layer, rows.start : rows.start + QUERY, lanes[0]])
            scores = dot(query, qkv[layer, rows, lanes[1]], NT) * HEAD_DIM**-0.5 + key_bias
            expo = jnp.exp(scores - jnp.max(scores, -1, keepdims=True))
            probs[layer, n] = (expo * (1.0 / jnp.sum(expo, -1, keepdims=True))).astype(BF)
            if n > 0:
                mix(n - 1)
        mix(own * PAIRS - 1)
        weight_copy(1, layer).wait()

        @pl.when(layer == 0)
        def fetch():
            for k in range(len(weights)):
                weight_copy(k, 1).start()
            swap_cots.start()
            take_cots.start()

        branch = dot(mixed[layer], out_w[layer], NN) + pick_row(out_bias, layer)
        for i in range(own):
            at, to = i * JOINT, i * QUERY
            t_ref[to : to + QUERY] = x_ref[at : at + QUERY] + branch[to : to + QUERY]
        gain, shift = gains[layer, 1:2], shifts[layer, 1:2]
        for r in range(0, queries, CHUNK):
            unit, inverse = norm_parts(t_ref[r : r + CHUNK])
            unit2[layer, r : r + CHUNK] = unit.astype(BF)
            inv_ref[layer, r : r + CHUNK, 1:2] = inverse
            a_ref[r : r + CHUNK] = (unit * gain + shift).astype(BF)
        weight_copy(2, layer).wait()
        bias = pick_row(up_bias, layer)
        for c in range(0, hidden, HIDDEN_TILE):
            part = slice(c, c + HIDDEN_TILE)
            act, act_slope = gelu_and_slope(dot(a_ref[:queries], up_w[layer, :, part], NN) + bias[:, part])
            wide_ref[:queries, part] = act.astype(BF)
            slope[layer, :, part] = act_slope.astype(BF)
        weight_copy(3, layer).wait()
        result = t_ref[...] + (dot(wide_ref[:queries], down_w[layer], NN) + pick_row(down_bias, layer))
        for i in range(own):
            x_ref[i * JOINT : i * JOINT + QUERY] = result[i * QUERY : (i + 1) * QUERY]
        return carry

    lax.fori_loop(0, LAYERS, forward, 0)
    take_head.start()

    for i in range(own):
        at = i * JOINT
        y_own[i] = x_ref[at : at + half].astype(BF)
        y_other[i] = x_ref[at + half : at + patches].astype(BF)
    swap_y.start()
    keep_y.start()

    lasts = [x_ref[i * JOINT + cls_at : i * JOINT + cls_at + 1] for i in range(own)]
    swap_cots.wait_recv()
    take_cots.wait()
    for i in range(own):
        to = i * QUERY
        dx_ref[to + TAIL_AT : to + QUERY] = jnp.zeros((QUERY - TAIL_AT, width), F32)
        dx_ref[to : to + half] = own_rows(patch_own, i)
        dx_ref[to + half : to + patches] = own_rows(cot_other, i)
    rows = -(-classes // 8) * 8
    row = lax.broadcasted_iota(jnp.int32, (own * rows, tasks * classes), 0)
    col = lax.broadcasted_iota(jnp.int32, (own * rows, tasks * classes), 1)
    task = jnp.where(row < rows, task_ids[first], task_ids[first + 1])
    pick = jnp.where(row < rows, row, row - rows) * tasks + task == col
    pick = jnp.where(pick, 1.0, 0.0).astype(BF)
    take_head.wait()
    own_head = dot(pick, down_w[0, :head_rows], NN).astype(BF)
    parts = []
    ends = []
    for i in range(own):
        to = i * QUERY
        matrix = own_head[i * rows : (i + 1) * rows]
        unit, inverse = norm_parts(lasts[i])
        feature = (unit * final_gain[...].reshape(1, width) + final_bias[...].reshape(1, width)).astype(BF)
        task = lax.broadcasted_iota(jnp.int32, (tasks, classes), 0) == task_ids[first + i]
        offset = jnp.sum(jnp.where(task, head_bias[...].astype(F32), 0.0), 0, keepdims=True)
        offset = jnp.concatenate([offset, jnp.zeros((1, width - classes), F32)], 1)
        score = dot(jnp.broadcast_to(feature, (16, width)), matrix, NT)[:1]
        score = jnp.concatenate([score, jnp.zeros((1, width - rows), F32)], 1) + offset
        small[i, 0:1] = lasts[i]
        small[i, 1:2] = score
        small[i, 3:8] = jnp.zeros((5, width), F32)
        cot = pick_row(logit_cot, first + i)
        cot = jnp.concatenate([cot, jnp.zeros((1, PAIR - classes), F32)], 1)
        grad = dot(jnp.broadcast_to(cot[:, :rows].astype(BF), (16, rows)), matrix, NN)[:1]
        dx_ref[to + cls_at : to + cls_at + 1] = pick_row(cls_cot, first + i) + norm_back(
            grad, final_gain[...].reshape(1, width), unit, inverse
        )
        parts += [feature.astype(F32)[:, j : j + PAIR] for j in range(0, width, PAIR)]
        ends.append(cot)
    names = jnp.where(is_low, task_ids[first], task_ids[first + 1]).astype(F32)
    message[...] = jnp.concatenate(parts + ends + [names, jnp.zeros((1, PAIR), F32)], 0).astype(BF)
    put_back.start()
    if reduce:
        refs = (grads, got, match_ref, sums, got_sums, early, late, early_out, late_out)
        sums_of = [Reduction(layer, tasks, remote, keep_sems, refs) for layer in range(LAYERS)]
        give_messages = []
        for step in range(1, RAIL):
            give_messages.append(remote(message, got_messages.at[me], {"batch": (me + step) % RAIL}))
        for copy in give_messages:
            copy.start()
        got_messages[me] = message[...]

    def hook(step, at, action):
        if reduce:
            pl.when(step == at)(action)

    def add_last():
        for copy in give_messages:
            copy.wait_recv()
        order = lax.broadcasted_iota(jnp.int32, (tasks, PAIR), 0).astype(F32)
        for s in range(RAIL):
            match_ref[s] = jnp.where(got_messages[s, 14:15].astype(F32) == order, 1.0, 0.0)
        sums_of[1].add()

    def spread_last():
        sums_of[1].spread()

    scatter = [sums_of[k].scatter if reduce else None for k in range(LAYERS)]

    def backward(step, carry):
        layer = LAYERS - 1 - step
        pl.when(step == 1)(put_back.wait)
        a_ref[:queries] = dx_ref[:queries].astype(BF)
        for c in range(0, hidden, HIDDEN_TILE):
            part = slice(c, c + HIDDEN_TILE)
            grad = dot(a_ref[:queries], down_w[layer, part], NT)
            wide_ref[:queries, part] = (grad * slope[layer, :, part].astype(F32)).astype(BF)
        t_ref[...] = dot(wide_ref[:queries], up_w[layer], NT)
        hook(step, 1, add_last)
        gain = gains[layer, 1:2]
        for r in range(0, queries, CHUNK):
            part = slice(r, r + CHUNK)
            inverse = inv_ref[layer, part, 1:2]
            total = dx_ref[part] + norm_back(t_ref[part], gain, unit2[layer, part].astype(F32), inverse)
            dx_ref[part] = total
            a_ref[part] = total.astype(BF)
        o_ref[...] = dot(a_ref[:queries], out_w[layer], NT).astype(BF)

        def key_grad(n):
            rows, _, lanes = places(n)
            query = stack_pair(qkv[layer, rows.start : rows.start + QUERY, lanes[0]])
            grad_score = scores_ref[n % 2]
            grad_key = dot(query, grad_score, TN) * HEAD_DIM**-0.5
            wide_ref[rows, lanes[1]] = grad_key.astype(BF).T
            grad_query = dot(grad_score, qkv[layer, rows, lanes[1]], NN) * HEAD_DIM**-0.5
            wide_ref[rows.start : rows.start + QUERY, lanes[0]] = merge_pair(grad_query).astype(BF)

        for n in range(own * PAIRS):
            rows, tokens, lanes = places(n)
            grad = stack_pair(o_ref[tokens, lanes[0]])
            twice = jnp.concatenate([mixed[layer, tokens, lanes[0]]] * 2, 0)
            center = jnp.sum(grad.astype(F32) * twice.astype(F32), -1, keepdims=True)
            grad_prob = dot(grad, qkv[layer, rows, lanes[2]], NT)
            prob = probs[layer, n]
            scores_ref[n % 2] = (prob.astype(F32) * (grad_prob - center)).astype(BF)
            wide_ref[rows, lanes[2]] = dot(grad, prob, TN).astype(BF).T
            if n > 0:
                key_grad(n - 1)
            if n == PAIRS:
                hook(step, 1, spread_last)
        key_grad(own * PAIRS - 1)
        gain = gains[layer, 0:1]
        gain_t = jnp.broadcast_to(gain, (PAIR, width)).T
        scaled = dot(attn_w[layer, :, width:], tails(wide_ref, slice(width, 3 * width)), NT) * gain_t
        unit = unit_t[layer].astype(F32)
        mean = jnp.mean(scaled, 0, keepdims=True)
        mean_unit = jnp.mean(scaled * unit, 0, keepdims=True)
        grads[layer] = (inv_t[layer] * (scaled - mean - unit * mean_unit)).astype(BF)
        for k in range(LAYERS):
            hook(step, LAYERS - 1 - k, scatter[k])
        rows = [wide_ref[i * JOINT : i * JOINT + QUERY, : 3 * width] for i in range(own)]
        t_ref[...] = dot(jnp.concatenate(rows, 0), attn_w[layer], NT)
        for i in range(own):
            to = i * QUERY
            for r in range(0, QUERY, 16):
                part = slice(to + r, to + r + 16)
                inverse = inv_ref[layer, part, 0:1]
                grad = norm_back(t_ref[part], gain, unit1[layer, part].astype(F32), inverse)
                if r + 16 > cls_at:
                    keep = lax.broadcasted_iota(jnp.int32, (16, 1), 0) + r <= cls_at
                    grad = jnp.where(keep, grad, 0.0)
                dx_ref[part] += grad
        return carry

    lax.fori_loop(0, LAYERS, backward, 0)

    keep_dx, swap_dx = [], []
    padded = dx_out.shape[1]
    for i in range(own):
        to = i * QUERY
        t_ref[to : to + half] = dx_ref[to + half : to + patches]
        small[i, 2:3] = dx_ref[to + cls_at : to + cls_at + 1]
        keep_dx.append(local_copy(7 + i, dx_ref.at[pl.ds(to, padded)], dx_out.at[first + i]))
        swap_dx.append(remote(t_ref.at[pl.ds(to, padded)], dx_out.at[first + i], partner))
        swap_dx[i].start()
        keep_dx[i].start()
    swap_small.start()
    keep_small.start()
    if reduce:
        last, first_layer = sums_of[1], sums_of[0]
        last.relay()
        first_layer.add()
        swap_messages = remote(got_messages, messages_out.at[core], partner)
        keep_messages = local_copy(7 + own, got_messages, messages_out.at[core])
        swap_messages.start()
        keep_messages.start()
        first_layer.spread()
        last.hand_over()
        first_layer.relay()
        first_layer.hand_over()
        last.close()
        first_layer.close()
        swap_messages.wait_recv()
        keep_messages.wait()
    for copy in [swap_y, swap_small] + swap_dx:
        copy.wait_recv()
    for copy in [keep_y, keep_small] + keep_dx:
        copy.wait()
    for copy in remote.made:
        copy.wait_send()


def run_encoder(
    reduce, task_ids, patch_input, cls_input, patch_cotangent, cls_cotangent, logit_cotangent, prompts, head_weight,
    head_bias, attn_weight, attn_bias, out_weight, out_bias, up_weight, up_bias, down_weight, down_bias,
    gains, shifts, final_gain, final_bias, own,
):
    images, half, width = patch_input.shape
    tasks, classes = head_bias.shape
    prompt_count = prompts.shape[2]
    hidden = up_weight.shape[2]
    queries, joints = own * QUERY, own * JOINT
    lanes = own * TAIL
    pairs = tasks // 4
    share = width // RAIL
    shape = jax.ShapeDtypeStruct
    vmem = pl.BlockSpec(memory_space=pltpu.VMEM)
    anywhere = pl.BlockSpec(memory_space=pl.ANY)
    table = prompts.transpose(0, 2, 1, 3)
    head_rows = head_weight.transpose(2, 1, 0).reshape(-1, width)
    outs = [
        shape((images, half, width), BF),
        shape((images, -(-half // 8) * 8, width), F32),
        shape((images, 8, width), F32),
    ]
    out_specs = [anywhere] * 3
    scratch = [
        pltpu.VMEM(attn_weight.shape, BF),
        pltpu.VMEM(out_weight.shape, BF),
        pltpu.VMEM(up_weight.shape, BF),
        pltpu.VMEM(down_weight.shape, BF),
        pltpu.VMEM((joints, width), F32),
        pltpu.VMEM((queries, width), F32),
        pltpu.VMEM((joints, width), BF),
        pltpu.VMEM((queries, width), BF),
        pltpu.VMEM((joints, hidden), BF),
        pltpu.VMEM((LAYERS, queries, width), BF),
        pltpu.VMEM((2, 2 * QUERY, JOINT), BF),
        pltpu.VMEM((LAYERS, joints, 3 * width), BF),
        pltpu.VMEM((LAYERS, own * PAIRS, 2 * QUERY, JOINT), BF),
        pltpu.VMEM((LAYERS, queries, hidden), BF),
        pltpu.VMEM((LAYERS, queries, width), BF),
        pltpu.VMEM((LAYERS, queries, width), BF),
        pltpu.VMEM((LAYERS, queries, 2), F32),
        pltpu.VMEM((LAYERS, width, lanes), BF),
        pltpu.VMEM((LAYERS, 1, lanes), F32),
        pltpu.VMEM((tasks // 2,) + table.shape[1:], BF),
        pltpu.VMEM((LAYERS, own, prompt_count, width), BF),
        pltpu.VMEM((half, images, width), BF),
        pltpu.VMEM((half, images, width), BF),
        pltpu.VMEM((half, images, width), BF),
        pltpu.VMEM((own, half, width), BF),
        pltpu.VMEM((own, half, width), BF),
        pltpu.VMEM((own, 8, width), F32),
        pltpu.SemaphoreType.DMA((4, LAYERS)),
        pltpu.SemaphoreType.DMA((8 + own,)),
    ]
    if reduce:
        steps = 6 * (LINE - 1) + 3
        count = 4 + own + RAIL + LAYERS * (RAIL - 1 + steps)
        outs += [
            shape((LAYERS, 2, LINE, LINE, pairs, EARLY, lanes), BF),
            shape((LAYERS, 2, LINE, LINE, pairs, share - EARLY, lanes), BF),
            shape((2, RAIL, 16, PAIR), BF),
        ]
        out_specs += [anywhere] * 3
        scratch += [
            pltpu.SemaphoreType.DMA((count,)),
            pltpu.SemaphoreType.DMA((count,)),
            pltpu.VMEM((LAYERS, width, lanes), BF),
            pltpu.VMEM((16, PAIR), BF),
            pltpu.VMEM((LAYERS, RAIL, share, lanes), BF),
            pltpu.VMEM((RAIL, 16, PAIR), BF),
            pltpu.VMEM((RAIL, tasks, PAIR), F32),
            pltpu.VMEM((LAYERS, 2 * pairs, share, lanes), F32),
            pltpu.VMEM((LAYERS, pairs, share, lanes), F32),
            pltpu.VMEM((LAYERS, pairs, EARLY, lanes), BF),
            pltpu.VMEM((LAYERS, pairs, share - EARLY, lanes), BF),
            pltpu.SemaphoreType.DMA((2 * LAYERS,)),
        ]
    else:
        outs += [shape((LAYERS, width, lanes), BF), shape((16, PAIR), BF)]
        out_specs += [vmem] * 2
        scratch += [pltpu.SemaphoreType.DMA((4 + own,)), pltpu.SemaphoreType.DMA((4 + own,))]

    def kernel(*refs):
        encoder_kernel(own, 2 * half, prompt_count, classes, reduce, *refs)

    return pl.pallas_call(
        kernel,
        out_shape=outs,
        in_specs=[pl.BlockSpec(memory_space=pltpu.SMEM)] + [vmem] * 12 + [anywhere] * 8,
        out_specs=out_specs,
        scratch_shapes=scratch,
        compiler_params=pltpu.CompilerParams(vmem_limit_bytes=64 << 20, collective_id=0, has_side_effects=True),
        name="encoder",
    )(
        task_ids, cls_input, cls_cotangent, logit_cotangent, head_bias, attn_bias, out_bias, up_bias, down_bias,
        gains, shifts, final_gain, final_bias,
        patch_input.transpose(1, 0, 2), patch_cotangent.transpose(1, 0, 2), table, head_rows,
        attn_weight, out_weight, up_weight, down_weight,
    )


def finish_kernel(
    own, prompt_count, early_hbm, late_hbm, messages_hbm, small, y_hbm, dx_hbm,
    prompt_hbm, head_hbm, bias_grad, y_cls, logits, dx_cls, y_patch_hbm, dx_patch_hbm,
    early, late, messages, y, dx, prompt_grad, head_grad, y_patch, dx_patch, rows_ref, left_ref, features_ref, sems,
):
    classes, tasks, width = head_grad.shape
    devices = 2 * RAIL
    count = own * devices
    pairs = early.shape[4]
    class_part = classes // FINISH_PARTS
    copies = []

    def copy(source, target):
        copies.append(pltpu.make_async_copy(source, target, sems.at[len(copies)]))
        copies[-1].start()
        return copies[-1]

    take_messages = copy(messages_hbm, messages)
    take_dx, take_y = copy(dx_hbm, dx), copy(y_hbm, y)
    takes = []
    for side in range(2):
        for layer in range(LAYERS):
            takes.append(copy(early_hbm.at[layer, side], early.at[layer, side]))
            takes.append(copy(late_hbm.at[layer, side], late.at[layer, side]))
    gives = []

    y_cls[...] = small[:, 0, :].astype(BF)
    logits[...] = small[:, 1, : logits.shape[1]].astype(BF)
    dx_cls[...] = small[:, 2, :]

    def gather(k):
        return rows_ref[pl.ds(k, devices, stride=16)]

    take_messages.wait()
    rows_ref[...] = messages[...].astype(F32).reshape(rows_ref.shape)
    chunks = width // PAIR
    for i in range(own):
        for j in range(chunks):
            rows = slice(i * devices, (i + 1) * devices)
            features_ref[rows, j * PAIR : (j + 1) * PAIR] = gather(i * chunks + j).astype(BF)
    cots = jnp.concatenate([gather(own * chunks + i) for i in range(own)], 0)
    ids = gather(own * chunks + own).T
    ids = jnp.concatenate([ids[i * TAIL : i * TAIL + 1] for i in range(own)], 1)
    match = jnp.where(lax.broadcasted_iota(jnp.int32, (tasks, count), 0).astype(F32) == ids, 1.0, 0.0)
    cots_t = cots.T[:classes]
    left_ref[...] = (cots_t[:, None, :] * match[None]).astype(BF)
    for k in range(FINISH_PARTS):
        part = slice(k * class_part, (k + 1) * class_part)
        left = left_ref[part].reshape(class_part * tasks, count)
        head_grad[part] = dot(left, features_ref[...], NN).reshape(class_part, tasks, width)
        gives.append(copy(head_grad.at[part], head_hbm.at[part]))
    total = dot(match.astype(BF), cots.astype(BF), NN)
    bias_grad[...] = total[:, :classes]

    take_dx.wait()
    take_y.wait()
    for i in range(y.shape[0]):
        dx_patch[:, i, :] = dx[i, : y.shape[1]]
        y_patch[:, i, :] = y[i]
    gives.append(copy(dx_patch, dx_patch_hbm))
    gives.append(copy(y_patch, y_patch_hbm))

    row = lax.broadcasted_iota(jnp.int32, (2 * TAIL, 2 * TAIL), 0)
    col = lax.broadcasted_iota(jnp.int32, (2 * TAIL, 2 * TAIL), 1)
    turn = jnp.where(row == col, 1.0, 0.0).astype(BF)
    start = PROMPT_AT - TAIL_AT
    for core in range(2):
        for take in takes[2 * LAYERS * core : 2 * LAYERS * (core + 1)]:
            take.wait()
        for k in range(pairs):
            task = 2 * (core * pairs + k)
            for layer in range(LAYERS):
                blocks = []
                for b in range(RAIL):
                    blocks.append(early[layer, core, b // LINE, b % LINE, k])
                    blocks.append(late[layer, core, b // LINE, b % LINE, k])
                both = dot(turn, jnp.concatenate(blocks, 0), NT)
                for side in range(2):
                    at = side * TAIL + start
                    prompt_grad[task + side, :, layer, :] = both[at : at + prompt_count]
            part = slice(task, task + 2)
            gives.append(copy(prompt_grad.at[part], prompt_hbm.at[part]))
    for give in gives:
        give.wait()


def run_finish(early, late, messages, small, y, dx, prompt_count, class_count, own):
    layers, cores, _, _, pairs, _, lanes = early.shape
    width = RAIL * (early.shape[5] + late.shape[5])
    tasks = 2 * cores * pairs
    images, half = y.shape[:2]
    shape = jax.ShapeDtypeStruct
    vmem = pl.BlockSpec(memory_space=pltpu.VMEM)
    anywhere = pl.BlockSpec(memory_space=pl.ANY)
    prompt_shape, head_shape = (tasks, prompt_count, layers, width), (class_count, tasks, width)
    patch_shape = (half, images, width)

    def kernel(*refs):
        finish_kernel(own, prompt_count, *refs)

    return pl.pallas_call(
        kernel,
        out_shape=(
            shape(prompt_shape, F32),
            shape(head_shape, F32),
            shape((tasks, class_count), F32),
            shape((images, width), BF),
            shape((images, class_count), BF),
            shape((images, width), F32),
            shape(patch_shape, BF),
            shape(patch_shape, F32),
        ),
        in_specs=[anywhere] * 3 + [vmem] + [anywhere] * 2,
        out_specs=[anywhere] * 2 + [vmem] * 4 + [anywhere] * 2,
        scratch_shapes=[
            pltpu.VMEM(early.shape, BF),
            pltpu.VMEM(late.shape, BF),
            pltpu.VMEM(messages.shape, BF),
            pltpu.VMEM(y.shape, BF),
            pltpu.VMEM(dx.shape, F32),
            pltpu.VMEM(prompt_shape, F32),
            pltpu.VMEM(head_shape, F32),
            pltpu.VMEM(patch_shape, BF),
            pltpu.VMEM(patch_shape, F32),
            pltpu.VMEM((2 * RAIL * 16, PAIR), F32),
            pltpu.VMEM((class_count, tasks, own * 2 * RAIL), BF),
            pltpu.VMEM((own * 2 * RAIL, width), BF),
            pltpu.SemaphoreType.DMA((3 + 4 * layers + FINISH_PARTS + 2 + cores * pairs,)),
        ],
        compiler_params=pltpu.CompilerParams(vmem_limit_bytes=62 << 20),
        name="finish",
    )(early, late, messages, small, y, dx)


def gathered_sums(grads, message, own_ids, task_ids, logit_cot, prompt_count, tasks):
    layers, width, lanes = grads.shape
    own = own_ids.shape[0]
    start = PROMPT_AT - TAIL_AT
    parts = grads.reshape(layers, width, own, TAIL)[..., start : start + prompt_count].astype(F32)
    names = jnp.arange(tasks, dtype=jnp.int32)[None, :]
    onehot = (own_ids[:, None] == names).astype(F32)
    dense = jnp.einsum("it,ldip->tlpd", onehot, parts, precision=lax.Precision.HIGHEST)
    prompt_grad = lax.psum(dense, ("batch", "seq"))
    features = message[: own * width // PAIR].reshape(own, width)
    features = lax.all_gather(features, ("batch", "seq"), axis=0, tiled=True)
    cots = lax.all_gather(logit_cot, "batch", axis=0, tiled=True)
    ids = lax.all_gather(task_ids.astype(F32), "batch", axis=0, tiled=True).astype(jnp.int32)
    match = (ids[:, None] == names).astype(BF)
    head_grad = jnp.einsum("id,it,ic->dtc", features, match, cots, preferred_element_type=F32)
    bias_grad = jnp.einsum("it,ic->tc", match, cots, preferred_element_type=F32)
    return prompt_grad, head_grad, bias_grad


def per_device(
    cls_input, patch_input, task_ids, prompts, attn_weight, attn_bias, out_weight, out_bias, up_weight, up_bias,
    down_weight, down_bias, norm_gain, norm_bias, final_gain, final_bias, head_weight, head_bias,
    cls_cotangent, patch_cotangent, logit_cotangent,
):
    cores = lax.axis_size("seq")
    core = lax.axis_index("seq")
    images, width = cls_input.shape
    own = images // cores
    tasks, class_count = head_bias.shape
    prompt_count = prompts.shape[2]
    reduce = lax.axis_size("batch") == RAIL
    y, dx, small, *sums = run_encoder(
        reduce, task_ids, patch_input, cls_input, patch_cotangent, cls_cotangent, logit_cotangent, prompts,
        head_weight, head_bias, attn_weight, attn_bias, out_weight, out_bias, up_weight, up_bias,
        down_weight, down_bias, norm_gain, norm_bias, final_gain, final_bias, own,
    )
    if reduce:
        prompt_grad, head_grad, bias_grad, y_cls, logits, dx_cls, y, dx = run_finish(
            *sums, small, y, dx, prompt_count, class_count, own
        )
        prompt_grad = prompt_grad.transpose(0, 2, 1, 3)
        head_grad = head_grad.transpose(2, 1, 0)
        y, dx = y.transpose(1, 0, 2), dx.transpose(1, 0, 2)
    else:
        own_ids = lax.dynamic_slice_in_dim(task_ids, core * own, own, 0)
        prompt_grad, head_grad, bias_grad = gathered_sums(
            *sums, own_ids, task_ids, logit_cotangent, prompt_count, tasks
        )
        y_cls, logits, dx_cls = small[:, 0].astype(BF), small[:, 1, :class_count].astype(BF), small[:, 2]
        dx = dx[:, : patch_input.shape[1]]
    return y_cls, y, logits, dx_cls, dx, prompt_grad, head_grad, bias_grad


def solution(mesh):
    rows, tokens, whole = P("batch", None), P("batch", "seq", None), P()
    return jax.shard_map(
        per_device,
        mesh=mesh,
        in_specs=(rows, tokens, P("batch")) + (whole,) * 15 + (rows, tokens, rows),
        out_specs=(rows, tokens, rows, rows, tokens, whole, whole, whole),
        check_vma=False,
    )
```

```python
import jax
import jax.numpy as jnp
from jax import lax
from jax.experimental import pallas as pl
from jax.experimental.pallas import tpu as pltpu
from jax.sharding import PartitionSpec as P

HEADS = 12
HEAD_DIM = 64
LAYERS = 2
EPSILON = 1e-06
BF = jnp.bfloat16
F32 = jnp.float32

JOINT = 256
QUERY = 208
PROMPT_AT = 200
PAIR = 2 * HEAD_DIM
PAIRS = HEADS // 2
CHUNK = 32
HIDDEN_TILE = 512

TAIL = 64
TAIL_AT = JOINT - TAIL
RAIL = 16
LINE = 4
EARLY = 32
FINISH_PARTS = 4
FAR_FIRST = (8, 7, 9, 6, 10, 5, 11, 4, 12, 3, 13, 2, 14, 1, 15)
MESH = pl.DeviceIdType.MESH

NN = (((1,), (0,)), ((), ()))
NT = (((1,), (1,)), ((), ()))
TN = (((0,), (0,)), ((), ()))


def dot(left, right, dims):
    return lax.dot_general(left, right, dims, preferred_element_type=F32)


def gelu_and_slope(u):
    phi = 0.5 + 0.5 * lax.erf(u * 0.7071067811865476)
    return u * phi, phi + u * (0.3989422804014327 * jnp.exp(-0.5 * u * u))


def norm_parts(x):
    center = x - jnp.mean(x, -1, keepdims=True)
    inverse = lax.rsqrt(jnp.mean(center * center, -1, keepdims=True) + EPSILON)
    return center * inverse, inverse


def norm_back(grad, gain, unit, inverse):
    scaled = grad * gain
    first = jnp.mean(scaled, -1, keepdims=True)
    second = jnp.mean(scaled * unit, -1, keepdims=True)
    return inverse * (scaled - first - unit * second)


def pick_row(ref, index):
    values = ref[...].astype(F32)
    rows = lax.broadcasted_iota(jnp.int32, values.shape, 0)
    return jnp.sum(jnp.where(rows == index, values, 0.0), 0, keepdims=True)


class Copies:
    def __init__(self, send_sems, recv_sems):
        self.send_sems, self.recv_sems, self.made = send_sems, recv_sems, []

    def __call__(self, source, target, device):
        k = len(self.made)
        copy = pltpu.make_async_remote_copy(
            src_ref=source, dst_ref=target, send_sem=self.send_sems.at[k], recv_sem=self.recv_sems.at[k],
            device_id=device, device_id_type=MESH,
        )
        self.made.append(copy)
        return copy


class Reduction:
    def __init__(self, layer, tasks, remote, local_sems, refs):
        self.layer, self.tasks = layer, tasks
        self.grads, self.got, self.match, self.sums, self.got_sums, self.early, self.late, early_out, late_out = refs
        self.me, core = lax.axis_index("batch"), lax.axis_index("seq")
        line, place = self.me // LINE, self.me % LINE
        partner = {"seq": 1 - core}
        pairs = self.early.shape[1]
        self.share = self.got.shape[2]
        self.mine = pl.ds(core * pairs, pairs)
        targets = [(self.me + step) % RAIL for step in range(RAIL)]
        self.rows = [pl.ds(pl.multiple_of(target * self.share, 16), self.share) for target in targets]
        self.scattered = [
            remote(self.grads.at[layer, self.rows[k]], self.got.at[layer, self.me], {"batch": targets[k]})
            for k in FAR_FIRST
        ]
        theirs = self.sums.at[layer, pl.ds((1 - core) * pairs, pairs)]
        self.swap = remote(theirs, self.got_sums.at[layer], partner)
        early_at, late_at = early_out.at[layer, core, line, place], late_out.at[layer, core, line, place]
        self.keeps = [
            pltpu.make_async_copy(self.early.at[layer], early_at, local_sems.at[2 * layer]),
            pltpu.make_async_copy(self.late.at[layer], late_at, local_sems.at[2 * layer + 1]),
        ]
        to_line = [{"batch": (line + step) % LINE * LINE + place} for step in range(LINE)]
        to_place = [{"batch": line * LINE + (place + step) % LINE} for step in range(LINE)]
        self.spreads, self.relays = [], []
        for step in range(1, LINE):
            self.spreads.append(remote(self.early.at[layer], early_at, to_line[step]))
            self.spreads.append(remote(self.late.at[layer], late_at, to_place[step]))
        early_at, late_at = early_out.at[layer, core, :, place], late_out.at[layer, core, line]
        self.handed = [remote(at, at, partner) for at in (early_at, late_at)]
        for step in range(1, LINE):
            self.relays.append(remote(early_at, early_at, to_place[step]))
            self.relays.append(remote(late_at, late_at, to_line[step]))
        for step in range(1, LINE):
            for at in (
                early_out.at[layer, core, :, (place + LINE - step) % LINE],
                late_out.at[layer, core, (line + LINE - step) % LINE],
            ):
                self.handed.append(remote(at, at, partner))

    def scatter(self):
        for copy in self.scattered:
            copy.start()
        self.got[self.layer, self.me] = self.grads[self.layer, self.rows[0]]

    def add(self):
        layer = self.layer
        for copy in self.scattered:
            copy.wait_recv()
        is_low = lax.broadcasted_iota(jnp.int32, (1, 2 * TAIL), 1) < TAIL
        for r in range(0, self.share, 16):

            def add_up(s, totals):
                part = self.got[layer, s, r : r + 16].astype(F32)
                match = self.match[s]
                return tuple(total + part * match[t : t + 1] for t, total in enumerate(totals))

            zero = jnp.zeros((16, 2 * TAIL), F32)
            totals = lax.fori_loop(0, RAIL, add_up, (zero,) * self.tasks, unroll=4)
            totals = [total + pltpu.roll(total, TAIL, 1) for total in totals]
            for pair in range(self.tasks // 2):
                self.sums[layer, pair, r : r + 16] = jnp.where(is_low, totals[2 * pair], totals[2 * pair + 1])
        self.swap.start()

    def spread(self):
        layer = self.layer
        self.swap.wait_recv()
        total = (self.sums[layer, self.mine] + self.got_sums[layer]).astype(BF)
        self.early[layer] = total[:, :EARLY]
        self.late[layer] = total[:, EARLY:]
        for copy in self.spreads + self.keeps:
            copy.start()

    def relay(self):
        for copy in self.spreads:
            copy.wait_recv()
        for copy in self.keeps:
            copy.wait()
        for copy in self.relays + self.handed[:2]:
            copy.start()

    def hand_over(self):
        for k, copy in enumerate(self.relays):
            copy.wait_recv()
            self.handed[2 + k].start()

    def close(self):
        for copy in self.handed:
            copy.wait_recv()


def encoder_kernel(
    own, patches, prompt_count, classes, reduce,
    task_ids, cls_in, cls_cot, logit_cot, head_bias, attn_bias, out_bias, up_bias, down_bias, gains, shifts,
    final_gain, final_bias,
    patch_hbm, cot_hbm, prompts_hbm, head_hbm, attn_hbm, out_hbm, up_hbm, down_hbm,
    y_out, dx_out, small_out, *rest,
):
    if reduce:
        early_out, late_out, messages_out = rest[:3]
        rest = rest[3:]
    else:
        grads, message = rest[:2]
        rest = rest[2:]
    (
        attn_w, out_w, up_w, down_w, x_ref, t_ref, a_ref, o_ref, wide_ref,
        mixed, qkv, probs, slope, unit1, unit2, inv_ref, unit_t, inv_t, table, prompt_rows,
        patch_own, patch_other, cot_other, y_own, y_other, small,
        weight_sems, local_sems, send_sems, recv_sems,
    ) = rest[:30]
    if reduce:
        grads, message, got, got_messages, match_ref, sums, got_sums, early, late, keep_sems = rest[30:]
    half = patches // 2
    cls_at = patches
    width = x_ref.shape[1]
    hidden = up_w.shape[2]
    queries = own * QUERY
    tasks = head_bias.shape[0]
    core = lax.axis_index("seq")
    me = lax.axis_index("batch")
    first = core * own
    partner = {"seq": 1 - core}
    remote = Copies(send_sems, recv_sems)

    weights = ((attn_hbm, attn_w), (out_hbm, out_w), (up_hbm, up_w), (down_hbm, down_w))

    def weight_copy(k, layer):
        source, target = weights[k]
        return pltpu.make_async_copy(source.at[layer], target.at[layer], weight_sems.at[k, layer])

    def local_copy(k, source, target):
        return pltpu.make_async_copy(source, target, local_sems.at[k])

    dx_ref = x_ref
    head_rows = head_hbm.shape[0]
    take_patches = local_copy(0, patch_hbm, patch_own)
    take_cots = local_copy(1, cot_hbm, patch_own)
    take_table = local_copy(2, prompts_hbm, table)
    take_head = local_copy(3, head_hbm, down_w.at[0, pl.ds(0, head_rows)])
    put_back = local_copy(4, down_hbm.at[0, pl.ds(0, head_rows)], down_w.at[0, pl.ds(0, head_rows)])
    keep_y = local_copy(5, y_own, y_out.at[pl.ds(first, own)])
    keep_small = local_copy(6, small, small_out.at[pl.ds(first, own)])
    swap_patches = remote(patch_hbm, patch_other, partner)
    swap_cots = remote(cot_hbm, cot_other, partner)
    swap_y = remote(y_other, y_out.at[pl.ds(first, own)], partner)
    swap_small = remote(small, small_out.at[pl.ds(first, own)], partner)

    take_patches.start()
    take_table.start()
    weight_copy(0, 0).start()
    barrier = pltpu.get_barrier_semaphore()
    peers = [partner]
    if reduce:
        peers += [{"batch": (me + step) % RAIL} for step in range(1, RAIL)]
    for peer in peers:
        pl.semaphore_signal(barrier, inc=1, device_id=peer, device_id_type=MESH)

    lane = lax.broadcasted_iota(jnp.int32, (1, PAIR), 1)
    is_low = lane < HEAD_DIM
    column = lax.broadcasted_iota(jnp.int32, (1, JOINT), 1)
    is_key = (column <= cls_at) | ((column >= PROMPT_AT) & (column < PROMPT_AT + prompt_count))
    key_bias = jnp.where(is_key, 0.0, -1e30).astype(F32)

    def stack_pair(block):
        zero = jnp.zeros_like(block)
        return jnp.concatenate([jnp.where(is_low, block, zero), jnp.where(is_low, zero, block)], 0)

    def merge_pair(block):
        return jnp.where(is_low, block[:QUERY], block[QUERY:])

    def places(n):
        i, h = n // PAIRS, n % PAIRS
        lanes = [slice(k * width + h * PAIR, k * width + (h + 1) * PAIR) for k in range(3)]
        return slice(i * JOINT, (i + 1) * JOINT), slice(i * QUERY, (i + 1) * QUERY), lanes

    def tails(ref, lanes):
        return jnp.concatenate([ref[i * JOINT + TAIL_AT : (i + 1) * JOINT, lanes] for i in range(own)], 0)

    def own_rows(ref, i):
        values = ref[...].astype(F32)
        return jnp.where(core == 0, values[:, i, :], values[:, own + i, :])

    pl.semaphore_wait(barrier, len(peers))
    swap_patches.start()
    take_patches.wait()
    for i in range(own):
        at = i * JOINT
        x_ref[at + TAIL_AT : at + JOINT] = jnp.zeros((TAIL, width), F32)
        x_ref[at : at + half] = own_rows(patch_own, i)
        x_ref[at + cls_at : at + cls_at + 1] = pick_row(cls_in, first + i)
    take_table.wait()
    for i in range(own):
        entry = table[task_ids[first + i]].astype(F32)
        for layer in range(LAYERS):
            prompt_rows[layer, i] = entry[:, layer, :].astype(BF)
    swap_patches.wait_recv()
    for k in range(1, len(weights)):
        weight_copy(k, 0).start()
    for i in range(own):
        x_ref[i * JOINT + half : i * JOINT + patches] = own_rows(patch_other, i)

    def forward(layer, carry):
        for i in range(own):
            at = i * JOINT + PROMPT_AT
            x_ref[at : at + prompt_count] = prompt_rows[layer, i].astype(F32)
        gain, shift = gains[layer, 0:1], shifts[layer, 0:1]
        for i in range(own):
            for r in range(0, JOINT, CHUNK):
                at, to = i * JOINT + r, i * QUERY + r
                unit, inverse = norm_parts(x_ref[at : at + CHUNK])
                a_ref[at : at + CHUNK] = (unit * gain + shift).astype(BF)
                kept = min(CHUNK, QUERY - r)
                if kept > 0:
                    unit1[layer, to : to + kept] = unit[:kept].astype(BF)
                    inv_ref[layer, to : to + kept, 0:1] = inverse[:kept]
        weight_copy(0, layer).wait()
        bias = pick_row(attn_bias, layer)
        for n in range(3):
            part = slice(n * width, (n + 1) * width)
            qkv[layer, :, part] = (dot(a_ref[...], attn_w[layer, :, part], NN) + bias[:, part]).astype(BF)
        turned = tails(x_ref, slice(None)).T
        center = turned - jnp.mean(turned, 0, keepdims=True)
        inverse = lax.rsqrt(jnp.mean(center * center, 0, keepdims=True) + EPSILON)
        unit_t[layer] = (center * inverse).astype(BF)
        inv_t[layer] = inverse

        def mix(n):
            rows, tokens, lanes = places(n)
            values = qkv[layer, rows, lanes[2]]
            mixed[layer, tokens, lanes[0]] = merge_pair(dot(probs[layer, n], values, NN)).astype(BF)

        for n in range(own * PAIRS):
            rows, _, lanes = places(n)
            query = stack_pair(qkv[layer, rows.start : rows.start + QUERY, lanes[0]])
            scores = dot(query, qkv[layer, rows, lanes[1]], NT) * HEAD_DIM**-0.5 + key_bias
            expo = jnp.exp(scores - jnp.max(scores, -1, keepdims=True))
            probs[layer, n] = (expo * (1.0 / jnp.sum(expo, -1, keepdims=True))).astype(BF)
            if n > 0:
                mix(n - 1)
        mix(own * PAIRS - 1)
        weight_copy(1, layer).wait()

        @pl.when(layer == 0)
        def fetch():
            for k in range(len(weights)):
                weight_copy(k, 1).start()
            swap_cots.start()
            take_cots.start()

        branch = dot(mixed[layer], out_w[layer], NN) + pick_row(out_bias, layer)
        for i in range(own):
            at, to = i * JOINT, i * QUERY
            t_ref[to : to + QUERY] = x_ref[at : at + QUERY] + branch[to : to + QUERY]
        gain, shift = gains[layer, 1:2], shifts[layer, 1:2]
        for r in range(0, queries, CHUNK):
            unit, inverse = norm_parts(t_ref[r : r + CHUNK])
            unit2[layer, r : r + CHUNK] = unit.astype(BF)
            inv_ref[layer, r : r + CHUNK, 1:2] = inverse
            a_ref[r : r + CHUNK] = (unit * gain + shift).astype(BF)
        weight_copy(2, layer).wait()
        bias = pick_row(up_bias, layer)
        for c in range(0, hidden, HIDDEN_TILE):
            part = slice(c, c + HIDDEN_TILE)
            act, act_slope = gelu_and_slope(dot(a_ref[:queries], up_w[layer, :, part], NN) + bias[:, part])
            wide_ref[:queries, part] = act.astype(BF)
            slope[layer, :, part] = act_slope.astype(BF)
        weight_copy(3, layer).wait()
        result = t_ref[...] + (dot(wide_ref[:queries], down_w[layer], NN) + pick_row(down_bias, layer))
        for i in range(own):
            x_ref[i * JOINT : i * JOINT + QUERY] = result[i * QUERY : (i + 1) * QUERY]
        return carry

    lax.fori_loop(0, LAYERS, forward, 0)
    take_head.start()

    for i in range(own):
        at = i * JOINT
        y_own[i] = x_ref[at : at + half].astype(BF)
        y_other[i] = x_ref[at + half : at + patches].astype(BF)
    swap_y.start()
    keep_y.start()

    lasts = [x_ref[i * JOINT + cls_at : i * JOINT + cls_at + 1] for i in range(own)]
    swap_cots.wait_recv()
    take_cots.wait()
    for i in range(own):
        to = i * QUERY
        dx_ref[to + TAIL_AT : to + QUERY] = jnp.zeros((QUERY - TAIL_AT, width), F32)
        dx_ref[to : to + half] = own_rows(patch_own, i)
        dx_ref[to + half : to + patches] = own_rows(cot_other, i)
    rows = -(-classes // 8) * 8
    row = lax.broadcasted_iota(jnp.int32, (own * rows, tasks * classes), 0)
    col = lax.broadcasted_iota(jnp.int32, (own * rows, tasks * classes), 1)
    task = jnp.where(row < rows, task_ids[first], task_ids[first + 1])
    pick = jnp.where(row < rows, row, row - rows) * tasks + task == col
    pick = jnp.where(pick, 1.0, 0.0).astype(BF)
    take_head.wait()
    own_head = dot(pick, down_w[0, :head_rows], NN).astype(BF)
    parts = []
    ends = []
    for i in range(own):
        to = i * QUERY
        matrix = own_head[i * rows : (i + 1) * rows]
        unit, inverse = norm_parts(lasts[i])
        feature = (unit * final_gain[...].reshape(1, width) + final_bias[...].reshape(1, width)).astype(BF)
        task = lax.broadcasted_iota(jnp.int32, (tasks, classes), 0) == task_ids[first + i]
        offset = jnp.sum(jnp.where(task, head_bias[...].astype(F32), 0.0), 0, keepdims=True)
        offset = jnp.concatenate([offset, jnp.zeros((1, width - classes), F32)], 1)
        score = dot(jnp.broadcast_to(feature, (16, width)), matrix, NT)[:1]
        score = jnp.concatenate([score, jnp.zeros((1, width - rows), F32)], 1) + offset
        small[i, 0:1] = lasts[i]
        small[i, 1:2] = score
        small[i, 3:8] = jnp.zeros((5, width), F32)
        cot = pick_row(logit_cot, first + i)
        cot = jnp.concatenate([cot, jnp.zeros((1, PAIR - classes), F32)], 1)
        grad = dot(jnp.broadcast_to(cot[:, :rows].astype(BF), (16, rows)), matrix, NN)[:1]
        dx_ref[to + cls_at : to + cls_at + 1] = pick_row(cls_cot, first + i) + norm_back(
            grad, final_gain[...].reshape(1, width), unit, inverse
        )
        parts += [feature.astype(F32)[:, j : j + PAIR] for j in range(0, width, PAIR)]
        ends.append(cot)
    names = jnp.where(is_low, task_ids[first], task_ids[first + 1]).astype(F32)
    message[...] = jnp.concatenate(parts + ends + [names, jnp.zeros((1, PAIR), F32)], 0).astype(BF)
    put_back.start()
    if reduce:
        refs = (grads, got, match_ref, sums, got_sums, early, late, early_out, late_out)
        sums_of = [Reduction(layer, tasks, remote, keep_sems, refs) for layer in range(LAYERS)]
        give_messages = []
        for step in range(1, RAIL):
            give_messages.append(remote(message, got_messages.at[me], {"batch": (me + step) % RAIL}))
        for copy in give_messages:
            copy.start()
        got_messages[me] = message[...]

    def hook(step, at, action):
        if reduce:
            pl.when(step == at)(action)

    def add_last():
        for copy in give_messages:
            copy.wait_recv()
        order = lax.broadcasted_iota(jnp.int32, (tasks, PAIR), 0).astype(F32)
        for s in range(RAIL):
            match_ref[s] = jnp.where(got_messages[s, 14:15].astype(F32) == order, 1.0, 0.0)
        sums_of[1].add()

    def spread_last():
        sums_of[1].spread()

    scatter = [sums_of[k].scatter if reduce else None for k in range(LAYERS)]

    def backward(step, carry):
        layer = LAYERS - 1 - step
        pl.when(step == 1)(put_back.wait)
        a_ref[:queries] = dx_ref[:queries].astype(BF)
        for c in range(0, hidden, HIDDEN_TILE):
            part = slice(c, c + HIDDEN_TILE)
            grad = dot(a_ref[:queries], down_w[layer, part], NT)
            wide_ref[:queries, part] = (grad * slope[layer, :, part].astype(F32)).astype(BF)
        t_ref[...] = dot(wide_ref[:queries], up_w[layer], NT)
        hook(step, 1, add_last)
        gain = gains[layer, 1:2]
        for r in range(0, queries, CHUNK):
            part = slice(r, r + CHUNK)
            inverse = inv_ref[layer, part, 1:2]
            total = dx_ref[part] + norm_back(t_ref[part], gain, unit2[layer, part].astype(F32), inverse)
            dx_ref[part] = total
            a_ref[part] = total.astype(BF)
        o_ref[...] = dot(a_ref[:queries], out_w[layer], NT).astype(BF)

        def scores_at(n):
            return slice(n * JOINT, (n + 1) * JOINT)

        def key_grad(n):
            rows, _, lanes = places(n)
            query = stack_pair(qkv[layer, rows.start : rows.start + QUERY, lanes[0]])
            grad_key = dot(query, slope[layer, :, scores_at(n)], TN) * HEAD_DIM**-0.5
            wide_ref[rows, lanes[1]] = grad_key.astype(BF).T

        def query_grad(n):
            rows, _, lanes = places(n)
            grad_query = dot(slope[layer, :, scores_at(n)], qkv[layer, rows, lanes[1]], NN) * HEAD_DIM**-0.5
            wide_ref[rows.start : rows.start + QUERY, lanes[0]] = merge_pair(grad_query).astype(BF)

        for n in range(own * PAIRS):
            rows, tokens, lanes = places(n)
            grad = stack_pair(o_ref[tokens, lanes[0]])
            twice = jnp.concatenate([mixed[layer, tokens, lanes[0]]] * 2, 0)
            center = jnp.sum(grad.astype(F32) * twice.astype(F32), -1, keepdims=True)
            grad_prob = dot(grad, qkv[layer, rows, lanes[2]], NT)
            prob = probs[layer, n]
            slope[layer, :, scores_at(n)] = (prob.astype(F32) * (grad_prob - center)).astype(BF)
            wide_ref[rows, lanes[2]] = dot(grad, prob, TN).astype(BF).T
            if n > 0:
                key_grad(n - 1)
            if n == PAIRS:
                hook(step, 1, spread_last)
        key_grad(own * PAIRS - 1)
        gain = gains[layer, 0:1]
        gain_t = jnp.broadcast_to(gain, (PAIR, width)).T
        scaled = dot(attn_w[layer, :, width:], tails(wide_ref, slice(width, 3 * width)), NT) * gain_t
        unit = unit_t[layer].astype(F32)
        mean = jnp.mean(scaled, 0, keepdims=True)
        mean_unit = jnp.mean(scaled * unit, 0, keepdims=True)
        grads[layer] = (inv_t[layer] * (scaled - mean - unit * mean_unit)).astype(BF)
        for k in range(LAYERS):
            hook(step, LAYERS - 1 - k, scatter[k])
        for n in range(own * PAIRS):
            query_grad(n)
        rows = [wide_ref[i * JOINT : i * JOINT + QUERY, : 3 * width] for i in range(own)]
        t_ref[...] = dot(jnp.concatenate(rows, 0), attn_w[layer], NT)
        for i in range(own):
            to = i * QUERY
            for r in range(0, QUERY, 16):
                part = slice(to + r, to + r + 16)
                inverse = inv_ref[layer, part, 0:1]
                grad = norm_back(t_ref[part], gain, unit1[layer, part].astype(F32), inverse)
                if r + 16 > cls_at:
                    keep = lax.broadcasted_iota(jnp.int32, (16, 1), 0) + r <= cls_at
                    grad = jnp.where(keep, grad, 0.0)
                dx_ref[part] += grad
        return carry

    lax.fori_loop(0, LAYERS, backward, 0)

    gone = []

    def sent(copies):
        for copy in copies:
            copy.wait_send()
        gone.extend(copies)

    keep_dx, swap_dx = [], []
    padded = dx_out.shape[1]
    for i in range(own):
        to = i * QUERY
        t_ref[to : to + half] = dx_ref[to + half : to + patches]
        small[i, 2:3] = dx_ref[to + cls_at : to + cls_at + 1]
        keep_dx.append(local_copy(7 + i, dx_ref.at[pl.ds(to, padded)], dx_out.at[first + i]))
        swap_dx.append(remote(t_ref.at[pl.ds(to, padded)], dx_out.at[first + i], partner))
        swap_dx[i].start()
        keep_dx[i].start()
    swap_small.start()
    keep_small.start()
    if reduce:
        last, first_layer = sums_of[1], sums_of[0]
        last.relay()
        first_layer.add()
        swap_messages = remote(got_messages, messages_out.at[core], partner)
        keep_messages = local_copy(7 + own, got_messages, messages_out.at[core])
        swap_messages.start()
        keep_messages.start()
        first_layer.spread()
        last.hand_over()
        sent([swap_patches, swap_cots, swap_y] + give_messages)
        sent(last.scattered + [last.swap] + last.spreads + first_layer.scattered + [first_layer.swap])
        first_layer.relay()
        sent([swap_small, swap_messages] + swap_dx + last.relays + last.handed + first_layer.spreads)
        first_layer.hand_over()
        last.close()
        first_layer.close()
        swap_messages.wait_recv()
        keep_messages.wait()
    for copy in [swap_y, swap_small] + swap_dx:
        copy.wait_recv()
    for copy in [keep_y, keep_small] + keep_dx:
        copy.wait()
    sent([copy for copy in remote.made if not any(copy is other for other in gone)])


def run_encoder(
    reduce, task_ids, patch_input, cls_input, patch_cotangent, cls_cotangent, logit_cotangent, prompts, head_weight,
    head_bias, attn_weight, attn_bias, out_weight, out_bias, up_weight, up_bias, down_weight, down_bias,
    gains, shifts, final_gain, final_bias, own,
):
    images, half, width = patch_input.shape
    tasks, classes = head_bias.shape
    prompt_count = prompts.shape[2]
    hidden = up_weight.shape[2]
    queries, joints = own * QUERY, own * JOINT
    lanes = own * TAIL
    pairs = tasks // 4
    share = width // RAIL
    shape = jax.ShapeDtypeStruct
    vmem = pl.BlockSpec(memory_space=pltpu.VMEM)
    anywhere = pl.BlockSpec(memory_space=pl.ANY)
    table = prompts.transpose(0, 2, 1, 3)
    head_rows = head_weight.transpose(2, 1, 0).reshape(-1, width)
    outs = [
        shape((images, half, width), BF),
        shape((images, -(-half // 8) * 8, width), F32),
        shape((images, 8, width), F32),
    ]
    out_specs = [anywhere] * 3
    scratch = [
        pltpu.VMEM(attn_weight.shape, BF),
        pltpu.VMEM(out_weight.shape, BF),
        pltpu.VMEM(up_weight.shape, BF),
        pltpu.VMEM(down_weight.shape, BF),
        pltpu.VMEM((joints, width), F32),
        pltpu.VMEM((queries, width), F32),
        pltpu.VMEM((joints, width), BF),
        pltpu.VMEM((queries, width), BF),
        pltpu.VMEM((joints, hidden), BF),
        pltpu.VMEM((LAYERS, queries, width), BF),
        pltpu.VMEM((LAYERS, joints, 3 * width), BF),
        pltpu.VMEM((LAYERS, own * PAIRS, 2 * QUERY, JOINT), BF),
        pltpu.VMEM((LAYERS, queries, hidden), BF),
        pltpu.VMEM((LAYERS, queries, width), BF),
        pltpu.VMEM((LAYERS, queries, width), BF),
        pltpu.VMEM((LAYERS, queries, 2), F32),
        pltpu.VMEM((LAYERS, width, lanes), BF),
        pltpu.VMEM((LAYERS, 1, lanes), F32),
        pltpu.VMEM(table.shape, BF),
        pltpu.VMEM((LAYERS, own, prompt_count, width), BF),
        pltpu.VMEM((half, images, width), BF),
        pltpu.VMEM((half, images, width), BF),
        pltpu.VMEM((half, images, width), BF),
        pltpu.VMEM((own, half, width), BF),
        pltpu.VMEM((own, half, width), BF),
        pltpu.VMEM((own, 8, width), F32),
        pltpu.SemaphoreType.DMA((4, LAYERS)),
        pltpu.SemaphoreType.DMA((8 + own,)),
    ]
    if reduce:
        steps = 6 * (LINE - 1) + 3
        count = 4 + own + RAIL + LAYERS * (RAIL - 1 + steps)
        outs += [
            shape((LAYERS, 2, LINE, LINE, pairs, EARLY, lanes), BF),
            shape((LAYERS, 2, LINE, LINE, pairs, share - EARLY, lanes), BF),
            shape((2, RAIL, 16, PAIR), BF),
        ]
        out_specs += [anywhere] * 3
        scratch += [
            pltpu.SemaphoreType.DMA((count,)),
            pltpu.SemaphoreType.DMA((count,)),
            pltpu.VMEM((LAYERS, width, lanes), BF),
            pltpu.VMEM((16, PAIR), BF),
            pltpu.VMEM((LAYERS, RAIL, share, lanes), BF),
            pltpu.VMEM((RAIL, 16, PAIR), BF),
            pltpu.VMEM((RAIL, tasks, PAIR), F32),
            pltpu.VMEM((LAYERS, 2 * pairs, share, lanes), F32),
            pltpu.VMEM((LAYERS, pairs, share, lanes), F32),
            pltpu.VMEM((LAYERS, pairs, EARLY, lanes), BF),
            pltpu.VMEM((LAYERS, pairs, share - EARLY, lanes), BF),
            pltpu.SemaphoreType.DMA((2 * LAYERS,)),
        ]
    else:
        outs += [shape((LAYERS, width, lanes), BF), shape((16, PAIR), BF)]
        out_specs += [vmem] * 2
        scratch += [pltpu.SemaphoreType.DMA((4 + own,)), pltpu.SemaphoreType.DMA((4 + own,))]

    def kernel(*refs):
        encoder_kernel(own, 2 * half, prompt_count, classes, reduce, *refs)

    return pl.pallas_call(
        kernel,
        out_shape=outs,
        in_specs=[pl.BlockSpec(memory_space=pltpu.SMEM)] + [vmem] * 12 + [anywhere] * 8,
        out_specs=out_specs,
        scratch_shapes=scratch,
        compiler_params=pltpu.CompilerParams(vmem_limit_bytes=64 << 20, collective_id=0, has_side_effects=True),
        name="encoder",
    )(
        task_ids, cls_input, cls_cotangent, logit_cotangent, head_bias, attn_bias, out_bias, up_bias, down_bias,
        gains, shifts, final_gain, final_bias,
        patch_input.transpose(1, 0, 2), patch_cotangent.transpose(1, 0, 2), table, head_rows,
        attn_weight, out_weight, up_weight, down_weight,
    )


def finish_kernel(
    own, prompt_count, early_hbm, late_hbm, messages_hbm, small_hbm, y_hbm, dx_hbm,
    prompt_hbm, head_hbm, bias_hbm, y_cls_hbm, logits_hbm, dx_cls_hbm, y_patch_hbm, dx_patch_hbm,
    early, late, messages, small, y, dx, prompt_grad, head_grad, bias_grad, y_cls, logits, dx_cls, y_patch, dx_patch,
    rows_ref, left_ref, features_ref, sems,
):
    classes, tasks, width = head_grad.shape
    devices = 2 * RAIL
    count = own * devices
    pairs = early.shape[4]
    class_part = classes // FINISH_PARTS
    copies = []

    def copy(source, target):
        copies.append(pltpu.make_async_copy(source, target, sems.at[len(copies)]))
        copies[-1].start()
        return copies[-1]

    take_messages = copy(messages_hbm, messages)
    take_small = copy(small_hbm, small)
    take_dx, take_y = copy(dx_hbm, dx), copy(y_hbm, y)
    takes = []
    for side in range(2):
        for layer in range(LAYERS):
            takes.append(copy(early_hbm.at[layer, side], early.at[layer, side]))
            takes.append(copy(late_hbm.at[layer, side], late.at[layer, side]))
    gives = []

    def gather(k):
        return rows_ref[pl.ds(k, devices, stride=16)]

    take_messages.wait()
    rows_ref[...] = messages[...].astype(F32).reshape(rows_ref.shape)
    chunks = width // PAIR
    for i in range(own):
        for j in range(chunks):
            rows = slice(i * devices, (i + 1) * devices)
            features_ref[rows, j * PAIR : (j + 1) * PAIR] = gather(i * chunks + j).astype(BF)
    cots = jnp.concatenate([gather(own * chunks + i) for i in range(own)], 0)
    ids = gather(own * chunks + own).T
    ids = jnp.concatenate([ids[i * TAIL : i * TAIL + 1] for i in range(own)], 1)
    match = jnp.where(lax.broadcasted_iota(jnp.int32, (tasks, count), 0).astype(F32) == ids, 1.0, 0.0)
    cots_t = cots.T[:classes]
    left_ref[...] = (cots_t[:, None, :] * match[None]).astype(BF)
    for k in range(FINISH_PARTS):
        part = slice(k * class_part, (k + 1) * class_part)
        left = left_ref[part].reshape(class_part * tasks, count)
        head_grad[part] = dot(left, features_ref[...], NN).reshape(class_part, tasks, width)
        gives.append(copy(head_grad.at[part], head_hbm.at[part]))
    total = dot(match.astype(BF), cots.astype(BF), NN)
    bias_grad[...] = total[:, :classes]
    take_small.wait()
    y_cls[...] = small[:, 0, :].astype(BF)
    logits[...] = small[:, 1, : logits.shape[1]].astype(BF)
    dx_cls[...] = small[:, 2, :]
    for source, target in ((bias_grad, bias_hbm), (y_cls, y_cls_hbm), (logits, logits_hbm), (dx_cls, dx_cls_hbm)):
        gives.append(copy(source, target))

    take_dx.wait()
    take_y.wait()
    for i in range(y.shape[0]):
        dx_patch[:, i, :] = dx[i, : y.shape[1]]
        y_patch[:, i, :] = y[i]
    gives.append(copy(dx_patch, dx_patch_hbm))
    gives.append(copy(y_patch, y_patch_hbm))

    row = lax.broadcasted_iota(jnp.int32, (2 * TAIL, 2 * TAIL), 0)
    col = lax.broadcasted_iota(jnp.int32, (2 * TAIL, 2 * TAIL), 1)
    turn = jnp.where(row == col, 1.0, 0.0).astype(BF)
    start = PROMPT_AT - TAIL_AT
    for core in range(2):
        for take in takes[2 * LAYERS * core : 2 * LAYERS * (core + 1)]:
            take.wait()
        for k in range(pairs):
            task = 2 * (core * pairs + k)
            for layer in range(LAYERS):
                blocks = []
                for b in range(RAIL):
                    blocks.append(early[layer, core, b // LINE, b % LINE, k])
                    blocks.append(late[layer, core, b // LINE, b % LINE, k])
                both = dot(turn, jnp.concatenate(blocks, 0), NT)
                for side in range(2):
                    at = side * TAIL + start
                    prompt_grad[task + side, :, layer, :] = both[at : at + prompt_count]
            part = slice(task, task + 2)
            gives.append(copy(prompt_grad.at[part], prompt_hbm.at[part]))
    for give in gives:
        give.wait()


def run_finish(early, late, messages, small, y, dx, prompt_count, class_count, own):
    layers, cores, _, _, pairs, _, lanes = early.shape
    width = RAIL * (early.shape[5] + late.shape[5])
    tasks = 2 * cores * pairs
    images, half = y.shape[:2]
    shape = jax.ShapeDtypeStruct
    vmem = pl.BlockSpec(memory_space=pltpu.VMEM)
    anywhere = pl.BlockSpec(memory_space=pl.ANY)
    prompt_shape, head_shape = (tasks, prompt_count, layers, width), (class_count, tasks, width)
    patch_shape = (half, images, width)

    def kernel(*refs):
        finish_kernel(own, prompt_count, *refs)

    return pl.pallas_call(
        kernel,
        out_shape=(
            shape(prompt_shape, F32),
            shape(head_shape, F32),
            shape((tasks, class_count), F32),
            shape((images, width), BF),
            shape((images, class_count), BF),
            shape((images, width), F32),
            shape(patch_shape, BF),
            shape(patch_shape, F32),
        ),
        in_specs=[anywhere] * 6,
        out_specs=[anywhere] * 8,
        scratch_shapes=[
            pltpu.VMEM(early.shape, BF),
            pltpu.VMEM(late.shape, BF),
            pltpu.VMEM(messages.shape, BF),
            pltpu.VMEM(small.shape, F32),
            pltpu.VMEM(y.shape, BF),
            pltpu.VMEM(dx.shape, F32),
            pltpu.VMEM(prompt_shape, F32),
            pltpu.VMEM(head_shape, F32),
            pltpu.VMEM((tasks, class_count), F32),
            pltpu.VMEM((images, width), BF),
            pltpu.VMEM((images, class_count), BF),
            pltpu.VMEM((images, width), F32),
            pltpu.VMEM(patch_shape, BF),
            pltpu.VMEM(patch_shape, F32),
            pltpu.VMEM((2 * RAIL * 16, PAIR), F32),
            pltpu.VMEM((class_count, tasks, own * 2 * RAIL), BF),
            pltpu.VMEM((own * 2 * RAIL, width), BF),
            pltpu.SemaphoreType.DMA((8 + 4 * layers + FINISH_PARTS + 2 + cores * pairs,)),
        ],
        compiler_params=pltpu.CompilerParams(vmem_limit_bytes=62 << 20),
        name="finish",
    )(early, late, messages, small, y, dx)


def gathered_sums(grads, message, own_ids, task_ids, logit_cot, prompt_count, tasks):
    layers, width, lanes = grads.shape
    own = own_ids.shape[0]
    start = PROMPT_AT - TAIL_AT
    parts = grads.reshape(layers, width, own, TAIL)[..., start : start + prompt_count].astype(F32)
    names = jnp.arange(tasks, dtype=jnp.int32)[None, :]
    onehot = (own_ids[:, None] == names).astype(F32)
    dense = jnp.einsum("it,ldip->tlpd", onehot, parts, precision=lax.Precision.HIGHEST)
    prompt_grad = lax.psum(dense, ("batch", "seq"))
    features = message[: own * width // PAIR].reshape(own, width)
    features = lax.all_gather(features, ("batch", "seq"), axis=0, tiled=True)
    cots = lax.all_gather(logit_cot, "batch", axis=0, tiled=True)
    ids = lax.all_gather(task_ids.astype(F32), "batch", axis=0, tiled=True).astype(jnp.int32)
    match = (ids[:, None] == names).astype(BF)
    head_grad = jnp.einsum("id,it,ic->dtc", features, match, cots, preferred_element_type=F32)
    bias_grad = jnp.einsum("it,ic->tc", match, cots, preferred_element_type=F32)
    return prompt_grad, head_grad, bias_grad


def per_device(
    cls_input, patch_input, task_ids, prompts, attn_weight, attn_bias, out_weight, out_bias, up_weight, up_bias,
    down_weight, down_bias, norm_gain, norm_bias, final_gain, final_bias, head_weight, head_bias,
    cls_cotangent, patch_cotangent, logit_cotangent,
):
    cores = lax.axis_size("seq")
    core = lax.axis_index("seq")
    images, width = cls_input.shape
    own = images // cores
    tasks, class_count = head_bias.shape
    prompt_count = prompts.shape[2]
    reduce = lax.axis_size("batch") == RAIL
    y, dx, small, *sums = run_encoder(
        reduce, task_ids, patch_input, cls_input, patch_cotangent, cls_cotangent, logit_cotangent, prompts,
        head_weight, head_bias, attn_weight, attn_bias, out_weight, out_bias, up_weight, up_bias,
        down_weight, down_bias, norm_gain, norm_bias, final_gain, final_bias, own,
    )
    if reduce:
        prompt_grad, head_grad, bias_grad, y_cls, logits, dx_cls, y, dx = run_finish(
            *sums, small, y, dx, prompt_count, class_count, own
        )
        prompt_grad = prompt_grad.transpose(0, 2, 1, 3)
        head_grad = head_grad.transpose(2, 1, 0)
        y, dx = y.transpose(1, 0, 2), dx.transpose(1, 0, 2)
    else:
        own_ids = lax.dynamic_slice_in_dim(task_ids, core * own, own, 0)
        prompt_grad, head_grad, bias_grad = gathered_sums(
            *sums, own_ids, task_ids, logit_cotangent, prompt_count, tasks
        )
        y_cls, logits, dx_cls = small[:, 0].astype(BF), small[:, 1, :class_count].astype(BF), small[:, 2]
        dx = dx[:, : patch_input.shape[1]]
    return y_cls, y, logits, dx_cls, dx, prompt_grad, head_grad, bias_grad


def solution(mesh):
    rows, tokens, whole = P("batch", None), P("batch", "seq", None), P()
    return jax.shard_map(
        per_device,
        mesh=mesh,
        in_specs=(rows, tokens, P("batch")) + (whole,) * 15 + (rows, tokens, rows),
        out_specs=(rows, tokens, rows, rows, tokens, whole, whole, whole),
        check_vma=False,
    )
```

```python
from functools import partial

import jax
import jax.numpy as jnp
from jax import lax
from jax.experimental import pallas as pl
from jax.experimental.pallas import tpu as pltpu
from jax.sharding import PartitionSpec as P

HEADS = 12
HEAD_DIM = 64
LAYERS = 2
EPSILON = 1e-06
BF = jnp.bfloat16
F32 = jnp.float32

JOINT = 256
QUERY = 208
PROMPT_AT = 200
PAIR = 2 * HEAD_DIM
PAIRS = HEADS // 2
CHUNK = 32
HIDDEN_TILE = 512

TAIL = 64
TAIL_AT = JOINT - TAIL
RAIL = 16
LINE = 4
EARLY = 32
FINISH_PARTS = 4
FAR_FIRST = (8, 7, 9, 6, 10, 5, 11, 4, 12, 3, 13, 2, 14, 1, 15)
MESH = pl.DeviceIdType.MESH

NN = (((1,), (0,)), ((), ()))
NT = (((1,), (1,)), ((), ()))
TN = (((0,), (0,)), ((), ()))


def dot(left, right, dims):
    return lax.dot_general(left, right, dims, preferred_element_type=F32)


def gelu_and_slope(u):
    phi = 0.5 + 0.5 * lax.erf(u * 0.7071067811865476)
    return u * phi, phi + u * (0.3989422804014327 * jnp.exp(-0.5 * u * u))


def norm_parts(x):
    center = x - jnp.mean(x, -1, keepdims=True)
    inverse = lax.rsqrt(jnp.mean(center * center, -1, keepdims=True) + EPSILON)
    return center * inverse, inverse


def norm_back(grad, gain, unit, inverse):
    scaled = grad * gain
    first = jnp.mean(scaled, -1, keepdims=True)
    second = jnp.mean(scaled * unit, -1, keepdims=True)
    return inverse * (scaled - first - unit * second)


def pick_row(ref, index):
    values = ref[...].astype(F32)
    rows = lax.broadcasted_iota(jnp.int32, values.shape, 0)
    return jnp.sum(jnp.where(rows == index, values, 0.0), 0, keepdims=True)


def interleave(products, others):
    done = 0
    for k, product in enumerate(products):
        product()
        upto = len(others) * (k + 1) // len(products)
        for other in others[done:upto]:
            other()
        done = upto


class Copies:
    def __init__(self, send_sems, recv_sems):
        self.send_sems, self.recv_sems, self.made = send_sems, recv_sems, []

    def __call__(self, source, target, device):
        k = len(self.made)
        copy = pltpu.make_async_remote_copy(
            src_ref=source, dst_ref=target, send_sem=self.send_sems.at[k], recv_sem=self.recv_sems.at[k],
            device_id=device, device_id_type=MESH,
        )
        self.made.append(copy)
        return copy


class Reduction:
    def __init__(self, layer, tasks, remote, local_sems, refs):
        self.layer, self.tasks = layer, tasks
        self.grads, self.got, self.match, self.sums, self.got_sums, self.early, self.late, early_out, late_out = refs
        self.me, self.core = lax.axis_index("batch"), lax.axis_index("seq")
        core = self.core
        line, place = self.me // LINE, self.me % LINE
        partner = {"seq": 1 - core}
        pairs = self.early.shape[1]
        self.share = self.got.shape[2]
        self.pairs = pairs
        self.mine = pl.ds(core * pairs, pairs)
        targets = [(self.me + step) % RAIL for step in range(RAIL)]
        self.rows = [pl.ds(pl.multiple_of(target * self.share, 16), self.share) for target in targets]
        self.scattered = [
            remote(self.grads.at[layer, self.rows[k]], self.got.at[layer, self.me], {"batch": targets[k]})
            for k in FAR_FIRST
        ]
        theirs = self.sums.at[pl.ds((1 - core) * pairs, pairs)]
        self.swap = remote(theirs, self.got_sums.at[layer], partner)
        early_at, late_at = early_out.at[layer, core, line, place], late_out.at[layer, core, line, place]
        self.keeps = [
            pltpu.make_async_copy(self.early.at[layer], early_at, local_sems.at[2 * layer]),
            pltpu.make_async_copy(self.late.at[layer], late_at, local_sems.at[2 * layer + 1]),
        ]
        to_line = [{"batch": (line + step) % LINE * LINE + place} for step in range(LINE)]
        x, y = place % 2, place // 2
        places = [place, 2 * y + 1 - x, 2 * (1 - y) + x, 2 * (1 - y) + 1 - x]
        to_place = [{"batch": line * LINE + other} for other in places]
        self.spreads, self.relays = [], []
        for step in range(1, LINE):
            self.spreads.append(remote(self.early.at[layer], early_at, to_line[step]))
            self.spreads.append(remote(self.late.at[layer], late_at, to_place[step]))
        early_at, late_at = early_out.at[layer, core, :, place], late_out.at[layer, core, line]
        self.handed = [remote(at, at, partner) for at in (early_at, late_at)]
        for step in range(1, LINE):
            self.relays.append(remote(early_at, early_at, to_place[step]))
            self.relays.append(remote(late_at, late_at, to_line[step]))
        for step in range(1, LINE):
            for at in (
                early_out.at[layer, core, :, places[step]],
                late_out.at[layer, core, (line + LINE - step) % LINE],
            ):
                self.handed.append(remote(at, at, partner))

    def scatter(self):
        for copy in self.scattered:
            copy.start()
        self.got[self.layer, self.me] = self.grads[self.layer, self.rows[0]]

    def add(self):
        layer = self.layer
        for copy in self.scattered:
            copy.wait_recv()
        is_low = lax.broadcasted_iota(jnp.int32, (1, 2 * TAIL), 1) < TAIL
        for owner in (1 - self.core, self.core):
            for r in range(0, self.share, 16):

                def add_up(s, totals):
                    part = self.got[layer, s, r : r + 16].astype(F32)
                    match = self.match[s, owner]
                    return tuple(total + part * match[t : t + 1] for t, total in enumerate(totals))

                zero = jnp.zeros((16, 2 * TAIL), F32)
                totals = lax.fori_loop(0, RAIL, add_up, (zero,) * (2 * self.pairs), unroll=4)
                totals = [total + pltpu.roll(total, TAIL, 1) for total in totals]
                for k in range(self.pairs):
                    self.sums[owner * self.pairs + k, r : r + 16] = jnp.where(
                        is_low, totals[2 * k], totals[2 * k + 1]
                    )
            if owner is not self.core:
                self.swap.start()

    def spread(self):
        layer = self.layer
        self.swap.wait_recv()
        total = (self.sums[self.mine] + self.got_sums[layer]).astype(BF)
        self.early[layer] = total[:, :EARLY]
        self.late[layer] = total[:, EARLY:]
        for copy in self.spreads + self.keeps:
            copy.start()

    def relay(self):
        for copy in self.spreads:
            copy.wait_recv()
        for copy in self.keeps:
            copy.wait()
        for copy in self.relays + self.handed[:2]:
            copy.start()

    def hand_over(self):
        for k, copy in enumerate(self.relays):
            copy.wait_recv()
            self.handed[2 + k].start()

    def close(self):
        for copy in self.handed:
            copy.wait_recv()


def encoder_kernel(
    own, patches, prompt_count, classes, reduce,
    task_ids, cls_in, cls_cot, logit_cot, head_bias, attn_bias, out_bias, up_bias, down_bias, gains, shifts,
    final_gain, final_bias,
    patch_hbm, cot_hbm, prompts_hbm, head_hbm, attn_hbm, out_hbm, up_hbm, down_hbm,
    y_out, dx_out, small_out, *rest,
):
    if reduce:
        early_out, late_out, messages_out = rest[:3]
        rest = rest[3:]
    else:
        grads, message = rest[:2]
        rest = rest[2:]
    (
        attn_w, out_w, up_w, down_w, x_ref, t_ref, a_ref, o_ref, wide_ref,
        mixed, qkv, probs, slope, unit1, unit2, inv_ref, unit_t, inv_t, table, prompt_rows,
        patch_own, patch_other, free_sem, y_own, y_other, small,
        weight_sems, local_sems, send_sems, recv_sems,
    ) = rest[:30]
    if reduce:
        grads, message, got, got_messages, match_ref, sums, got_sums, early, late, keep_sems = rest[30:]
    half = patches // 2
    cls_at = patches
    width = x_ref.shape[1]
    hidden = up_w.shape[2]
    queries = own * QUERY
    tasks = head_bias.shape[0]
    core = lax.axis_index("seq")
    me = lax.axis_index("batch")
    first = core * own
    partner = {"seq": 1 - core}
    remote = Copies(send_sems, recv_sems)

    weights = ((attn_hbm, attn_w), (out_hbm, out_w), (up_hbm, up_w), (down_hbm, down_w))

    def weight_copy(k, layer):
        source, target = weights[k]
        return pltpu.make_async_copy(source.at[layer], target.at[layer], weight_sems.at[k, layer])

    def local_copy(k, source, target):
        return pltpu.make_async_copy(source, target, local_sems.at[k])

    dx_ref = x_ref
    head_rows = head_hbm.shape[0]
    take_patches = local_copy(0, patch_hbm, patch_own)
    take_cots = local_copy(1, cot_hbm, patch_own)
    take_table = local_copy(2, prompts_hbm, table)
    take_head = local_copy(3, head_hbm, down_w.at[0, pl.ds(0, head_rows)])
    put_back = local_copy(4, down_hbm.at[0, pl.ds(0, head_rows)], down_w.at[0, pl.ds(0, head_rows)])
    keep_y = local_copy(5, y_own, y_out.at[pl.ds(first, own)])
    keep_small = local_copy(6, small, small_out.at[pl.ds(first, own)])
    swap_patches = remote(patch_hbm, patch_other, partner)
    swap_cots = remote(cot_hbm, patch_other, partner)
    swap_y = remote(y_other, y_out.at[pl.ds(first, own)], partner)
    swap_small = remote(small, small_out.at[pl.ds(first, own)], partner)

    take_patches.start()
    take_table.start()
    weight_copy(0, 0).start()
    barrier = pltpu.get_barrier_semaphore()
    peers = [partner]
    if reduce:
        peers += [{"batch": (me + step) % RAIL} for step in range(1, RAIL)]
    for peer in peers:
        pl.semaphore_signal(barrier, inc=1, device_id=peer, device_id_type=MESH)

    lane = lax.broadcasted_iota(jnp.int32, (1, PAIR), 1)
    is_low = lane < HEAD_DIM
    column = lax.broadcasted_iota(jnp.int32, (1, JOINT), 1)
    is_key = (column <= cls_at) | ((column >= PROMPT_AT) & (column < PROMPT_AT + prompt_count))
    key_bias = jnp.where(is_key, 0.0, -1e30).astype(F32)

    def stack_pair(block):
        zero = jnp.zeros_like(block)
        return jnp.concatenate([jnp.where(is_low, block, zero), jnp.where(is_low, zero, block)], 0)

    def merge_pair(block):
        return jnp.where(is_low, block[:QUERY], block[QUERY:])

    def places(n):
        i, h = n // PAIRS, n % PAIRS
        lanes = [slice(k * width + h * PAIR, k * width + (h + 1) * PAIR) for k in range(3)]
        return slice(i * JOINT, (i + 1) * JOINT), slice(i * QUERY, (i + 1) * QUERY), lanes

    def tails(ref, lanes):
        return jnp.concatenate([ref[i * JOINT + TAIL_AT : (i + 1) * JOINT, lanes] for i in range(own)], 0)

    def own_rows(ref, i):
        values = ref[...].astype(F32)
        return jnp.where(core == 0, values[:, i, :], values[:, own + i, :])

    pl.semaphore_wait(barrier, len(peers))
    swap_patches.start()
    take_patches.wait()
    for i in range(own):
        at = i * JOINT
        x_ref[at + TAIL_AT : at + JOINT] = jnp.zeros((TAIL, width), F32)
        x_ref[at : at + half] = own_rows(patch_own, i)
        x_ref[at + cls_at : at + cls_at + 1] = pick_row(cls_in, first + i)
    take_table.wait()
    for i in range(own):
        entry = table[task_ids[first + i]].astype(F32)
        for layer in range(LAYERS):
            prompt_rows[layer, i] = entry[:, layer, :].astype(BF)
    swap_patches.wait_recv()
    for k in range(1, len(weights)):
        weight_copy(k, 0).start()
    for i in range(own):
        x_ref[i * JOINT + half : i * JOINT + patches] = own_rows(patch_other, i)
    pl.semaphore_signal(free_sem, inc=1, device_id=partner, device_id_type=MESH)

    def forward(layer, carry):
        for i in range(own):
            at = i * JOINT + PROMPT_AT
            x_ref[at : at + prompt_count] = prompt_rows[layer, i].astype(F32)
        gain, shift = gains[layer, 0:1], shifts[layer, 0:1]
        bias = pick_row(attn_bias, layer)

        def norm_first(i, r):
            at, to = i * JOINT + r, i * QUERY + r
            unit, inverse = norm_parts(x_ref[at : at + CHUNK])
            a_ref[at : at + CHUNK] = (unit * gain + shift).astype(BF)
            kept = min(CHUNK, QUERY - r)
            if kept > 0:
                unit1[layer, to : to + kept] = unit[:kept].astype(BF)
                inv_ref[layer, to : to + kept, 0:1] = inverse[:kept]

        def project(i, n):
            rows, part = slice(i * JOINT, (i + 1) * JOINT), slice(n * width, (n + 1) * width)
            qkv[layer, rows, part] = (dot(a_ref[rows], attn_w[layer, :, part], NN) + bias[:, part]).astype(BF)

        def norm_tails():
            turned = tails(x_ref, slice(None)).T
            center = turned - jnp.mean(turned, 0, keepdims=True)
            inverse = lax.rsqrt(jnp.mean(center * center, 0, keepdims=True) + EPSILON)
            unit_t[layer] = (center * inverse).astype(BF)
            inv_t[layer] = inverse

        for r in range(0, JOINT, CHUNK):
            norm_first(0, r)
        weight_copy(0, layer).wait()
        for i in range(own):
            others = [norm_tails]
            if i + 1 < own:
                others = [partial(norm_first, i + 1, r) for r in range(0, JOINT, CHUNK)]
            interleave([partial(project, i, n) for n in range(3)], others)

        def mix(n):
            rows, tokens, lanes = places(n)
            values = qkv[layer, rows, lanes[2]]
            mixed[layer, tokens, lanes[0]] = merge_pair(dot(probs[layer, n], values, NN)).astype(BF)

        for n in range(own * PAIRS):
            rows, _, lanes = places(n)
            query = stack_pair(qkv[layer, rows.start : rows.start + QUERY, lanes[0]])
            scores = dot(query, qkv[layer, rows, lanes[1]], NT) * HEAD_DIM**-0.5 + key_bias
            expo = jnp.exp(scores - jnp.max(scores, -1, keepdims=True))
            probs[layer, n] = (expo * (1.0 / jnp.sum(expo, -1, keepdims=True))).astype(BF)
            if n > 0:
                mix(n - 1)
        mix(own * PAIRS - 1)
        weight_copy(1, layer).wait()

        @pl.when(layer == 0)
        def fetch():
            for k in range(len(weights)):
                weight_copy(k, 1).start()
            pl.semaphore_wait(free_sem, 1)
            swap_cots.start()
            take_cots.start()

        gain, shift = gains[layer, 1:2], shifts[layer, 1:2]
        offset = pick_row(out_bias, layer)

        def join_branch(i):
            at, tokens = i * JOINT, slice(i * QUERY, (i + 1) * QUERY)
            t_ref[tokens] = x_ref[at : at + QUERY] + (dot(mixed[layer, tokens], out_w[layer], NN) + offset)

        def norm_second(i, r):
            part = slice(i * QUERY + r, i * QUERY + min(r + CHUNK, QUERY))
            unit, inverse = norm_parts(t_ref[part])
            unit2[layer, part] = unit.astype(BF)
            inv_ref[layer, part, 1:2] = inverse
            a_ref[part] = (unit * gain + shift).astype(BF)

        def norms_second(i):
            return [partial(norm_second, i, r) for r in range(0, QUERY, CHUNK)]

        def widen(i, c):
            tokens, part = slice(i * QUERY, (i + 1) * QUERY), slice(c, c + HIDDEN_TILE)
            act, act_slope = gelu_and_slope(dot(a_ref[tokens], up_w[layer, :, part], NN) + bias[:, part])
            wide_ref[tokens, part] = act.astype(BF)
            slope[layer, tokens, part] = act_slope.astype(BF)

        def narrow(i):
            at, tokens = i * JOINT, slice(i * QUERY, (i + 1) * QUERY)
            x_ref[at : at + QUERY] = t_ref[tokens] + (dot(wide_ref[tokens], down_w[layer], NN) + offset_down)

        bias = pick_row(up_bias, layer)
        offset_down = pick_row(down_bias, layer)
        join_branch(0)
        interleave([partial(join_branch, 1)], norms_second(0))
        weight_copy(2, layer).wait()
        tiles = range(0, hidden, HIDDEN_TILE)
        interleave([partial(widen, 0, c) for c in tiles], norms_second(1))
        weight_copy(3, layer).wait()
        interleave([partial(widen, 1, c) for c in tiles], [partial(narrow, 0)])
        narrow(1)
        return carry

    lax.fori_loop(0, LAYERS, forward, 0)
    take_head.start()

    for i in range(own):
        at = i * JOINT
        y_own[i] = x_ref[at : at + half].astype(BF)
        y_other[i] = x_ref[at + half : at + patches].astype(BF)
    swap_y.start()
    keep_y.start()

    lasts = [x_ref[i * JOINT + cls_at : i * JOINT + cls_at + 1] for i in range(own)]
    swap_cots.wait_recv()
    take_cots.wait()
    for i in range(own):
        to = i * QUERY
        dx_ref[to + TAIL_AT : to + QUERY] = jnp.zeros((QUERY - TAIL_AT, width), F32)
        dx_ref[to : to + half] = own_rows(patch_own, i)
        dx_ref[to + half : to + patches] = own_rows(patch_other, i)
    rows = -(-classes // 8) * 8
    row = lax.broadcasted_iota(jnp.int32, (own * rows, tasks * classes), 0)
    col = lax.broadcasted_iota(jnp.int32, (own * rows, tasks * classes), 1)
    task = jnp.where(row < rows, task_ids[first], task_ids[first + 1])
    pick = jnp.where(row < rows, row, row - rows) * tasks + task == col
    pick = jnp.where(pick, 1.0, 0.0).astype(BF)
    take_head.wait()
    own_head = dot(pick, down_w[0, :head_rows], NN).astype(BF)
    parts = []
    ends = []
    for i in range(own):
        to = i * QUERY
        matrix = own_head[i * rows : (i + 1) * rows]
        unit, inverse = norm_parts(lasts[i])
        feature = (unit * final_gain[...].reshape(1, width) + final_bias[...].reshape(1, width)).astype(BF)
        task = lax.broadcasted_iota(jnp.int32, (tasks, classes), 0) == task_ids[first + i]
        offset = jnp.sum(jnp.where(task, head_bias[...].astype(F32), 0.0), 0, keepdims=True)
        offset = jnp.concatenate([offset, jnp.zeros((1, width - classes), F32)], 1)
        score = dot(jnp.broadcast_to(feature, (16, width)), matrix, NT)[:1]
        score = jnp.concatenate([score, jnp.zeros((1, width - rows), F32)], 1) + offset
        small[i, 0:1] = lasts[i]
        small[i, 1:2] = score
        small[i, 3:8] = jnp.zeros((5, width), F32)
        cot = pick_row(logit_cot, first + i)
        cot = jnp.concatenate([cot, jnp.zeros((1, PAIR - classes), F32)], 1)
        grad = dot(jnp.broadcast_to(cot[:, :rows].astype(BF), (16, rows)), matrix, NN)[:1]
        dx_ref[to + cls_at : to + cls_at + 1] = pick_row(cls_cot, first + i) + norm_back(
            grad, final_gain[...].reshape(1, width), unit, inverse
        )
        parts += [feature.astype(F32)[:, j : j + PAIR] for j in range(0, width, PAIR)]
        ends.append(cot)
    names = jnp.where(is_low, task_ids[first], task_ids[first + 1]).astype(F32)
    message[...] = jnp.concatenate(parts + ends + [names, jnp.zeros((1, PAIR), F32)], 0).astype(BF)
    put_back.start()
    if reduce:
        refs = (grads, got, match_ref, sums, got_sums, early, late, early_out, late_out)
        sums_of = [Reduction(layer, tasks, remote, keep_sems, refs) for layer in range(LAYERS)]
        give_messages = []
        for step in range(1, RAIL):
            give_messages.append(remote(message, got_messages.at[me], {"batch": (me + step) % RAIL}))
        for copy in give_messages:
            copy.start()
        got_messages[me] = message[...]

    def hook(step, at, action):
        if reduce:
            pl.when(step == at)(action)

    def add_last():
        for copy in give_messages:
            copy.wait_recv()
        order = lax.broadcasted_iota(jnp.int32, (tasks, PAIR), 0).astype(F32)
        for s in range(RAIL):
            match = jnp.where(got_messages[s, 14:15].astype(F32) == order, 1.0, 0.0)
            match_ref[s, 0], match_ref[s, 1] = match[: tasks // 2], match[tasks // 2 :]
        sums_of[1].add()

    def spread_last():
        sums_of[1].spread()

    scatter = [sums_of[k].scatter if reduce else None for k in range(LAYERS)]

    def backward(step, carry):
        layer = LAYERS - 1 - step
        pl.when(step == 1)(put_back.wait)
        gain = gains[layer, 1:2]

        def norm_second_back(i, r):
            part = slice(i * QUERY + r, i * QUERY + min(r + CHUNK, QUERY))
            inverse = inv_ref[layer, part, 1:2]
            total = dx_ref[part] + norm_back(t_ref[part], gain, unit2[layer, part].astype(F32), inverse)
            dx_ref[part] = total
            a_ref[part] = total.astype(BF)

        def norms_second_back(i):
            return [partial(norm_second_back, i, r) for r in range(0, QUERY, CHUNK)]

        def mix_back(i):
            tokens = slice(i * QUERY, (i + 1) * QUERY)
            o_ref[tokens] = dot(a_ref[tokens], out_w[layer], NT).astype(BF)

        a_ref[:queries] = dx_ref[:queries].astype(BF)
        for c in range(0, hidden, HIDDEN_TILE):
            part = slice(c, c + HIDDEN_TILE)
            grad = dot(a_ref[:queries], down_w[layer, part], NT)
            wide_ref[:queries, part] = (grad * slope[layer, :, part].astype(F32)).astype(BF)
        t_ref[...] = dot(wide_ref[:queries], up_w[layer], NT)
        hook(step, 1, add_last)
        for other in norms_second_back(0):
            other()
        mix_back(0)
        late_norms = norms_second_back(1)
        def scores_at(n):
            return slice(n * JOINT, (n + 1) * JOINT)

        def key_grad(n):
            rows, _, lanes = places(n)
            query = stack_pair(qkv[layer, rows.start : rows.start + QUERY, lanes[0]])
            grad_key = dot(query, slope[layer, :, scores_at(n)], TN) * HEAD_DIM**-0.5
            wide_ref[rows, lanes[1]] = grad_key.astype(BF).T

        def query_grad(n):
            rows, _, lanes = places(n)
            grad_query = dot(slope[layer, :, scores_at(n)], qkv[layer, rows, lanes[1]], NN) * HEAD_DIM**-0.5
            wide_ref[rows.start : rows.start + QUERY, lanes[0]] = merge_pair(grad_query).astype(BF)

        for n in range(own * PAIRS):
            rows, tokens, lanes = places(n)
            grad = stack_pair(o_ref[tokens, lanes[0]])
            twice = jnp.concatenate([mixed[layer, tokens, lanes[0]]] * 2, 0)
            center = jnp.sum(grad.astype(F32) * twice.astype(F32), -1, keepdims=True)
            grad_prob = dot(grad, qkv[layer, rows, lanes[2]], NT)
            prob = probs[layer, n]
            slope[layer, :, scores_at(n)] = (prob.astype(F32) * (grad_prob - center)).astype(BF)
            wide_ref[rows, lanes[2]] = dot(grad, prob, TN).astype(BF).T
            if n > 0:
                key_grad(n - 1)
            for other in late_norms[2 * n : 2 * n + 2]:
                other()
            if n == PAIRS - 1:
                mix_back(1)
                hook(step, 1, spread_last)
        key_grad(own * PAIRS - 1)
        gain = gains[layer, 0:1]
        gain_t = jnp.broadcast_to(gain, (PAIR, width)).T
        scaled = dot(attn_w[layer, :, width:], tails(wide_ref, slice(width, 3 * width)), NT) * gain_t
        unit = unit_t[layer].astype(F32)
        mean = jnp.mean(scaled, 0, keepdims=True)
        mean_unit = jnp.mean(scaled * unit, 0, keepdims=True)
        grads[layer] = (inv_t[layer] * (scaled - mean - unit * mean_unit)).astype(BF)
        for k in range(LAYERS):
            hook(step, LAYERS - 1 - k, scatter[k])

        def norm_first_back(i, r):
            part = slice(i * QUERY + r, i * QUERY + r + 16)
            inverse = inv_ref[layer, part, 0:1]
            grad = norm_back(t_ref[part], gain, unit1[layer, part].astype(F32), inverse)
            if r + 16 > cls_at:
                keep = lax.broadcasted_iota(jnp.int32, (16, 1), 0) + r <= cls_at
                grad = jnp.where(keep, grad, 0.0)
            dx_ref[part] += grad

        def norms_first_back(i):
            return [partial(norm_first_back, i, r) for r in range(0, QUERY, 16)]

        def project_back(i):
            rows = wide_ref[i * JOINT : i * JOINT + QUERY, : 3 * width]
            t_ref[i * QUERY : (i + 1) * QUERY] = dot(rows, attn_w[layer], NT)

        for n in range(PAIRS):
            query_grad(n)
        project_back(0)
        interleave([partial(query_grad, n) for n in range(PAIRS, own * PAIRS)], norms_first_back(0))
        project_back(1)
        for other in norms_first_back(1):
            other()
        return carry

    lax.fori_loop(0, LAYERS, backward, 0)

    gone = []

    def sent(copies):
        for copy in copies:
            copy.wait_send()
        gone.extend(copies)

    keep_dx, swap_dx = [], []
    padded = dx_out.shape[1]
    for i in range(own):
        to = i * QUERY
        t_ref[to : to + half] = dx_ref[to + half : to + patches]
        small[i, 2:3] = dx_ref[to + cls_at : to + cls_at + 1]
        keep_dx.append(local_copy(7 + i, dx_ref.at[pl.ds(to, padded)], dx_out.at[first + i]))
        swap_dx.append(remote(t_ref.at[pl.ds(to, padded)], dx_out.at[first + i], partner))
        swap_dx[i].start()
        keep_dx[i].start()
    swap_small.start()
    keep_small.start()
    if reduce:
        last, first_layer = sums_of[1], sums_of[0]
        last.relay()
        sent([last.swap])
        first_layer.add()
        swap_messages = remote(got_messages, messages_out.at[core], partner)
        keep_messages = local_copy(7 + own, got_messages, messages_out.at[core])
        swap_messages.start()
        keep_messages.start()
        first_layer.spread()
        last.hand_over()
        sent([swap_patches, swap_cots, swap_y] + give_messages)
        sent(last.scattered + last.spreads + first_layer.scattered + [first_layer.swap])
        first_layer.relay()
        sent([swap_small, swap_messages] + swap_dx + last.relays + last.handed + first_layer.spreads)
        first_layer.hand_over()
        last.close()
        first_layer.close()
        swap_messages.wait_recv()
        keep_messages.wait()
    for copy in [swap_y, swap_small] + swap_dx:
        copy.wait_recv()
    for copy in [keep_y, keep_small] + keep_dx:
        copy.wait()
    sent([copy for copy in remote.made if not any(copy is other for other in gone)])


def run_encoder(
    reduce, task_ids, patch_input, cls_input, patch_cotangent, cls_cotangent, logit_cotangent, prompts, head_weight,
    head_bias, attn_weight, attn_bias, out_weight, out_bias, up_weight, up_bias, down_weight, down_bias,
    gains, shifts, final_gain, final_bias, own,
):
    images, half, width = patch_input.shape
    tasks, classes = head_bias.shape
    prompt_count = prompts.shape[2]
    hidden = up_weight.shape[2]
    queries, joints = own * QUERY, own * JOINT
    lanes = own * TAIL
    pairs = tasks // 4
    share = width // RAIL
    shape = jax.ShapeDtypeStruct
    vmem = pl.BlockSpec(memory_space=pltpu.VMEM)
    anywhere = pl.BlockSpec(memory_space=pl.ANY)
    table = prompts.transpose(0, 2, 1, 3)
    head_rows = head_weight.transpose(2, 1, 0).reshape(-1, width)
    outs = [
        shape((images, half, width), BF),
        shape((images, -(-half // 8) * 8, width), F32),
        shape((images, 8, width), F32),
    ]
    out_specs = [anywhere] * 3
    scratch = [
        pltpu.VMEM(attn_weight.shape, BF),
        pltpu.VMEM(out_weight.shape, BF),
        pltpu.VMEM(up_weight.shape, BF),
        pltpu.VMEM(down_weight.shape, BF),
        pltpu.VMEM((joints, width), F32),
        pltpu.VMEM((queries, width), F32),
        pltpu.VMEM((joints, width), BF),
        pltpu.VMEM((queries, width), BF),
        pltpu.VMEM((joints, hidden), BF),
        pltpu.VMEM((LAYERS, queries, width), BF),
        pltpu.VMEM((LAYERS, joints, 3 * width), BF),
        pltpu.VMEM((LAYERS, own * PAIRS, 2 * QUERY, JOINT), BF),
        pltpu.VMEM((LAYERS, queries, hidden), BF),
        pltpu.VMEM((LAYERS, queries, width), BF),
        pltpu.VMEM((LAYERS, queries, width), BF),
        pltpu.VMEM((LAYERS, queries, 2), F32),
        pltpu.VMEM((LAYERS, width, lanes), BF),
        pltpu.VMEM((LAYERS, 1, lanes), F32),
        pltpu.VMEM(table.shape, BF),
        pltpu.VMEM((LAYERS, own, prompt_count, width), BF),
        pltpu.VMEM((half, images, width), BF),
        pltpu.VMEM((half, images, width), BF),
        pltpu.SemaphoreType.REGULAR,
        pltpu.VMEM((own, half, width), BF),
        pltpu.VMEM((own, half, width), BF),
        pltpu.VMEM((own, 8, width), F32),
        pltpu.SemaphoreType.DMA((4, LAYERS)),
        pltpu.SemaphoreType.DMA((8 + own,)),
    ]
    if reduce:
        steps = 6 * (LINE - 1) + 3
        count = 4 + own + RAIL + LAYERS * (RAIL - 1 + steps)
        outs += [
            shape((LAYERS, 2, LINE, LINE, pairs, EARLY, lanes), BF),
            shape((LAYERS, 2, LINE, LINE, pairs, share - EARLY, lanes), BF),
            shape((2, RAIL, 16, PAIR), BF),
        ]
        out_specs += [anywhere] * 3
        scratch += [
            pltpu.SemaphoreType.DMA((count,)),
            pltpu.SemaphoreType.DMA((count,)),
            pltpu.VMEM((LAYERS, width, lanes), BF),
            pltpu.VMEM((16, PAIR), BF),
            pltpu.VMEM((LAYERS, RAIL, share, lanes), BF),
            pltpu.VMEM((RAIL, 16, PAIR), BF),
            pltpu.VMEM((RAIL, 2, tasks // 2, PAIR), F32),
            pltpu.VMEM((2 * pairs, share, lanes), F32),
            pltpu.VMEM((LAYERS, pairs, share, lanes), F32),
            pltpu.VMEM((LAYERS, pairs, EARLY, lanes), BF),
            pltpu.VMEM((LAYERS, pairs, share - EARLY, lanes), BF),
            pltpu.SemaphoreType.DMA((2 * LAYERS,)),
        ]
    else:
        outs += [shape((LAYERS, width, lanes), BF), shape((16, PAIR), BF)]
        out_specs += [vmem] * 2
        scratch += [pltpu.SemaphoreType.DMA((4 + own,)), pltpu.SemaphoreType.DMA((4 + own,))]

    def kernel(*refs):
        encoder_kernel(own, 2 * half, prompt_count, classes, reduce, *refs)

    return pl.pallas_call(
        kernel,
        out_shape=outs,
        in_specs=[pl.BlockSpec(memory_space=pltpu.SMEM)] + [vmem] * 12 + [anywhere] * 8,
        out_specs=out_specs,
        scratch_shapes=scratch,
        compiler_params=pltpu.CompilerParams(vmem_limit_bytes=64 << 20, collective_id=0, has_side_effects=True),
        name="encoder",
    )(
        task_ids, cls_input, cls_cotangent, logit_cotangent, head_bias, attn_bias, out_bias, up_bias, down_bias,
        gains, shifts, final_gain, final_bias,
        patch_input.transpose(1, 0, 2), patch_cotangent.transpose(1, 0, 2), table, head_rows,
        attn_weight, out_weight, up_weight, down_weight,
    )


def finish_kernel(
    own, prompt_count, early_hbm, late_hbm, messages_hbm, small_hbm, y_hbm, dx_hbm,
    prompt_hbm, head_hbm, bias_hbm, y_cls_hbm, logits_hbm, dx_cls_hbm, y_patch_hbm, dx_patch_hbm,
    early, late, messages, small, y, dx, prompt_grad, head_grad, bias_grad, y_cls, logits, dx_cls, y_patch, dx_patch,
    rows_ref, left_ref, features_ref, sems,
):
    classes, tasks, width = head_grad.shape
    devices = 2 * RAIL
    count = own * devices
    pairs = early.shape[4]
    class_part = classes // FINISH_PARTS
    copies = []

    def copy(source, target):
        copies.append(pltpu.make_async_copy(source, target, sems.at[len(copies)]))
        copies[-1].start()
        return copies[-1]

    take_messages = copy(messages_hbm, messages)
    take_small = copy(small_hbm, small)
    take_dx, take_y = copy(dx_hbm, dx), copy(y_hbm, y)
    takes = []
    for side in range(2):
        for layer in range(LAYERS):
            takes.append(copy(early_hbm.at[layer, side], early.at[layer, side]))
            takes.append(copy(late_hbm.at[layer, side], late.at[layer, side]))
    gives = []

    def gather(k):
        return rows_ref[pl.ds(k, devices, stride=16)]

    take_messages.wait()
    rows_ref[...] = messages[...].astype(F32).reshape(rows_ref.shape)
    chunks = width // PAIR
    for i in range(own):
        for j in range(chunks):
            rows = slice(i * devices, (i + 1) * devices)
            features_ref[rows, j * PAIR : (j + 1) * PAIR] = gather(i * chunks + j).astype(BF)
    cots = jnp.concatenate([gather(own * chunks + i) for i in range(own)], 0)
    ids = gather(own * chunks + own).T
    ids = jnp.concatenate([ids[i * TAIL : i * TAIL + 1] for i in range(own)], 1)
    match = jnp.where(lax.broadcasted_iota(jnp.int32, (tasks, count), 0).astype(F32) == ids, 1.0, 0.0)
    cots_t = cots.T[:classes]
    left_ref[...] = (cots_t[:, None, :] * match[None]).astype(BF)
    for k in range(FINISH_PARTS):
        part = slice(k * class_part, (k + 1) * class_part)
        left = left_ref[part].reshape(class_part * tasks, count)
        head_grad[part] = dot(left, features_ref[...], NN).reshape(class_part, tasks, width)
        gives.append(copy(head_grad.at[part], head_hbm.at[part]))
    total = dot(match.astype(BF), cots.astype(BF), NN)
    bias_grad[...] = total[:, :classes]
    take_small.wait()
    y_cls[...] = small[:, 0, :].astype(BF)
    logits[...] = small[:, 1, : logits.shape[1]].astype(BF)
    dx_cls[...] = small[:, 2, :]
    for source, target in ((bias_grad, bias_hbm), (y_cls, y_cls_hbm), (logits, logits_hbm), (dx_cls, dx_cls_hbm)):
        gives.append(copy(source, target))

    take_dx.wait()
    take_y.wait()
    for i in range(y.shape[0]):
        dx_patch[:, i, :] = dx[i, : y.shape[1]]
        y_patch[:, i, :] = y[i]
    gives.append(copy(dx_patch, dx_patch_hbm))
    gives.append(copy(y_patch, y_patch_hbm))

    row = lax.broadcasted_iota(jnp.int32, (2 * TAIL, 2 * TAIL), 0)
    col = lax.broadcasted_iota(jnp.int32, (2 * TAIL, 2 * TAIL), 1)
    turn = jnp.where(row == col, 1.0, 0.0).astype(BF)
    start = PROMPT_AT - TAIL_AT
    for core in range(2):
        for take in takes[2 * LAYERS * core : 2 * LAYERS * (core + 1)]:
            take.wait()
        for k in range(pairs):
            task = 2 * (core * pairs + k)
            for layer in range(LAYERS):
                blocks = []
                for b in range(RAIL):
                    blocks.append(early[layer, core, b // LINE, b % LINE, k])
                    blocks.append(late[layer, core, b // LINE, b % LINE, k])
                both = dot(turn, jnp.concatenate(blocks, 0), NT)
                for side in range(2):
                    at = side * TAIL + start
                    prompt_grad[task + side, :, layer, :] = both[at : at + prompt_count]
            part = slice(task, task + 2)
            gives.append(copy(prompt_grad.at[part], prompt_hbm.at[part]))
    for give in gives:
        give.wait()


def run_finish(early, late, messages, small, y, dx, prompt_count, class_count, own):
    layers, cores, _, _, pairs, _, lanes = early.shape
    width = RAIL * (early.shape[5] + late.shape[5])
    tasks = 2 * cores * pairs
    images, half = y.shape[:2]
    shape = jax.ShapeDtypeStruct
    vmem = pl.BlockSpec(memory_space=pltpu.VMEM)
    anywhere = pl.BlockSpec(memory_space=pl.ANY)
    prompt_shape, head_shape = (tasks, prompt_count, layers, width), (class_count, tasks, width)
    patch_shape = (half, images, width)

    def kernel(*refs):
        finish_kernel(own, prompt_count, *refs)

    return pl.pallas_call(
        kernel,
        out_shape=(
            shape(prompt_shape, F32),
            shape(head_shape, F32),
            shape((tasks, class_count), F32),
            shape((images, width), BF),
            shape((images, class_count), BF),
            shape((images, width), F32),
            shape(patch_shape, BF),
            shape(patch_shape, F32),
        ),
        in_specs=[anywhere] * 6,
        out_specs=[anywhere] * 8,
        scratch_shapes=[
            pltpu.VMEM(early.shape, BF),
            pltpu.VMEM(late.shape, BF),
            pltpu.VMEM(messages.shape, BF),
            pltpu.VMEM(small.shape, F32),
            pltpu.VMEM(y.shape, BF),
            pltpu.VMEM(dx.shape, F32),
            pltpu.VMEM(prompt_shape, F32),
            pltpu.VMEM(head_shape, F32),
            pltpu.VMEM((tasks, class_count), F32),
            pltpu.VMEM((images, width), BF),
            pltpu.VMEM((images, class_count), BF),
            pltpu.VMEM((images, width), F32),
            pltpu.VMEM(patch_shape, BF),
            pltpu.VMEM(patch_shape, F32),
            pltpu.VMEM((2 * RAIL * 16, PAIR), F32),
            pltpu.VMEM((class_count, tasks, own * 2 * RAIL), BF),
            pltpu.VMEM((own * 2 * RAIL, width), BF),
            pltpu.SemaphoreType.DMA((8 + 4 * layers + FINISH_PARTS + 2 + cores * pairs,)),
        ],
        compiler_params=pltpu.CompilerParams(vmem_limit_bytes=62 << 20),
        name="finish",
    )(early, late, messages, small, y, dx)


def gathered_sums(grads, message, own_ids, task_ids, logit_cot, prompt_count, tasks):
    layers, width, lanes = grads.shape
    own = own_ids.shape[0]
    start = PROMPT_AT - TAIL_AT
    parts = grads.reshape(layers, width, own, TAIL)[..., start : start + prompt_count].astype(F32)
    names = jnp.arange(tasks, dtype=jnp.int32)[None, :]
    onehot = (own_ids[:, None] == names).astype(F32)
    dense = jnp.einsum("it,ldip->tlpd", onehot, parts, precision=lax.Precision.HIGHEST)
    prompt_grad = lax.psum(dense, ("batch", "seq"))
    features = message[: own * width // PAIR].reshape(own, width)
    features = lax.all_gather(features, ("batch", "seq"), axis=0, tiled=True)
    cots = lax.all_gather(logit_cot, "batch", axis=0, tiled=True)
    ids = lax.all_gather(task_ids.astype(F32), "batch", axis=0, tiled=True).astype(jnp.int32)
    match = (ids[:, None] == names).astype(BF)
    head_grad = jnp.einsum("id,it,ic->dtc", features, match, cots, preferred_element_type=F32)
    bias_grad = jnp.einsum("it,ic->tc", match, cots, preferred_element_type=F32)
    return prompt_grad, head_grad, bias_grad


def per_device(
    cls_input, patch_input, task_ids, prompts, attn_weight, attn_bias, out_weight, out_bias, up_weight, up_bias,
    down_weight, down_bias, norm_gain, norm_bias, final_gain, final_bias, head_weight, head_bias,
    cls_cotangent, patch_cotangent, logit_cotangent,
):
    cores = lax.axis_size("seq")
    core = lax.axis_index("seq")
    images, width = cls_input.shape
    own = images // cores
    tasks, class_count = head_bias.shape
    prompt_count = prompts.shape[2]
    reduce = lax.axis_size("batch") == RAIL
    y, dx, small, *sums = run_encoder(
        reduce, task_ids, patch_input, cls_input, patch_cotangent, cls_cotangent, logit_cotangent, prompts,
        head_weight, head_bias, attn_weight, attn_bias, out_weight, out_bias, up_weight, up_bias,
        down_weight, down_bias, norm_gain, norm_bias, final_gain, final_bias, own,
    )
    if reduce:
        prompt_grad, head_grad, bias_grad, y_cls, logits, dx_cls, y, dx = run_finish(
            *sums, small, y, dx, prompt_count, class_count, own
        )
        prompt_grad = prompt_grad.transpose(0, 2, 1, 3)
        head_grad = head_grad.transpose(2, 1, 0)
        y, dx = y.transpose(1, 0, 2), dx.transpose(1, 0, 2)
    else:
        own_ids = lax.dynamic_slice_in_dim(task_ids, core * own, own, 0)
        prompt_grad, head_grad, bias_grad = gathered_sums(
            *sums, own_ids, task_ids, logit_cotangent, prompt_count, tasks
        )
        y_cls, logits, dx_cls = small[:, 0].astype(BF), small[:, 1, :class_count].astype(BF), small[:, 2]
        dx = dx[:, : patch_input.shape[1]]
    return y_cls, y, logits, dx_cls, dx, prompt_grad, head_grad, bias_grad


def solution(mesh):
    rows, tokens, whole = P("batch", None), P("batch", "seq", None), P()
    return jax.shard_map(
        per_device,
        mesh=mesh,
        in_specs=(rows, tokens, P("batch")) + (whole,) * 15 + (rows, tokens, rows),
        out_specs=(rows, tokens, rows, rows, tokens, whole, whole, whole),
        check_vma=False,
    )
```

```python
from functools import partial

import jax
import jax.numpy as jnp
from jax import lax
from jax.experimental import pallas as pl
from jax.experimental.pallas import tpu as pltpu
from jax.sharding import PartitionSpec as P

HEADS = 12
HEAD_DIM = 64
LAYERS = 2
EPSILON = 1e-06
BF = jnp.bfloat16
F32 = jnp.float32

JOINT = 256
QUERY = 208
PROMPT_AT = 200
PAIR = 2 * HEAD_DIM
PAIRS = HEADS // 2
CHUNK = 32
HIDDEN_TILE = 512

TAIL = 64
TAIL_AT = JOINT - TAIL
RAIL = 16
LINE = 4
EARLY = 32
FINISH_PARTS = 4
FAR_FIRST = (8, 7, 9, 6, 10, 5, 11, 4, 12, 3, 13, 2, 14, 1, 15)
MESH = pl.DeviceIdType.MESH

NN = (((1,), (0,)), ((), ()))
NT = (((1,), (1,)), ((), ()))
TN = (((0,), (0,)), ((), ()))


def dot(left, right, dims):
    return lax.dot_general(left, right, dims, preferred_element_type=F32)


def gelu_and_slope(u):
    phi = 0.5 + 0.5 * lax.erf(u * 0.7071067811865476)
    return u * phi, phi + u * (0.3989422804014327 * jnp.exp(-0.5 * u * u))


def norm_parts(x):
    center = x - jnp.mean(x, -1, keepdims=True)
    inverse = lax.rsqrt(jnp.mean(center * center, -1, keepdims=True) + EPSILON)
    return center * inverse, inverse


def norm_back(grad, gain, unit, inverse):
    scaled = grad * gain
    first = jnp.mean(scaled, -1, keepdims=True)
    second = jnp.mean(scaled * unit, -1, keepdims=True)
    return inverse * (scaled - first - unit * second)


def pick_row(ref, index):
    values = ref[...].astype(F32)
    rows = lax.broadcasted_iota(jnp.int32, values.shape, 0)
    return jnp.sum(jnp.where(rows == index, values, 0.0), 0, keepdims=True)


def interleave(products, others):
    done = 0
    for k, product in enumerate(products):
        product()
        upto = len(others) * (k + 1) // len(products)
        for other in others[done:upto]:
            other()
        done = upto


class Copies:
    def __init__(self, send_sems, recv_sems):
        self.send_sems, self.recv_sems, self.made = send_sems, recv_sems, []

    def __call__(self, source, target, device):
        k = len(self.made)
        copy = pltpu.make_async_remote_copy(
            src_ref=source, dst_ref=target, send_sem=self.send_sems.at[k], recv_sem=self.recv_sems.at[k],
            device_id=device, device_id_type=MESH,
        )
        self.made.append(copy)
        return copy


class Reduction:
    def __init__(self, layer, tasks, remote, local_sems, refs):
        self.layer, self.tasks = layer, tasks
        self.grads, self.got, self.match, self.sums, self.got_sums, self.early, self.late, early_out, late_out = refs
        self.me, self.core = lax.axis_index("batch"), lax.axis_index("seq")
        core = self.core
        line, place = self.me // LINE, self.me % LINE
        partner = {"seq": 1 - core}
        pairs = self.early.shape[1]
        self.share = self.got.shape[2]
        self.pairs = pairs
        self.mine = pl.ds(core * pairs, pairs)
        targets = [(self.me + step) % RAIL for step in range(RAIL)]
        self.rows = [pl.ds(pl.multiple_of(target * self.share, 16), self.share) for target in targets]
        self.scattered = [
            remote(self.grads.at[layer, self.rows[k]], self.got.at[layer, self.me], {"batch": targets[k]})
            for k in FAR_FIRST
        ]
        theirs = self.sums.at[pl.ds((1 - core) * pairs, pairs)]
        self.swap = remote(theirs, self.got_sums.at[layer], partner)
        early_at, late_at = early_out.at[layer, core, line, place], late_out.at[layer, core, line, place]
        self.keeps = [
            pltpu.make_async_copy(self.early.at[layer], early_at, local_sems.at[2 * layer]),
            pltpu.make_async_copy(self.late.at[layer], late_at, local_sems.at[2 * layer + 1]),
        ]
        to_line = [{"batch": (line + step) % LINE * LINE + place} for step in range(LINE)]
        x, y = place % 2, place // 2
        places = [place, 2 * y + 1 - x, 2 * (1 - y) + x, 2 * (1 - y) + 1 - x]
        to_place = [{"batch": line * LINE + other} for other in places]
        self.spreads, self.relays = [], []
        for step in range(1, LINE):
            self.spreads.append(remote(self.early.at[layer], early_at, to_line[step]))
            self.spreads.append(remote(self.late.at[layer], late_at, to_place[step]))
        early_at, late_at = early_out.at[layer, core, :, place], late_out.at[layer, core, line]
        self.handed = [remote(at, at, partner) for at in (early_at, late_at)]
        for step in range(1, LINE):
            self.relays.append(remote(early_at, early_at, to_place[step]))
            self.relays.append(remote(late_at, late_at, to_line[step]))
        for step in range(1, LINE):
            for at in (
                early_out.at[layer, core, :, places[step]],
                late_out.at[layer, core, (line + LINE - step) % LINE],
            ):
                self.handed.append(remote(at, at, partner))

    def scatter(self):
        for copy in self.scattered:
            copy.start()
        self.got[self.layer, self.me] = self.grads[self.layer, self.rows[0]]

    def add(self):
        layer = self.layer
        for copy in self.scattered:
            copy.wait_recv()
        is_low = lax.broadcasted_iota(jnp.int32, (1, 2 * TAIL), 1) < TAIL
        for owner in (1 - self.core, self.core):
            for r in range(0, self.share, 16):

                def add_up(s, totals):
                    part = self.got[layer, s, r : r + 16].astype(F32)
                    match = self.match[s, owner]
                    return tuple(total + part * match[t : t + 1] for t, total in enumerate(totals))

                zero = jnp.zeros((16, 2 * TAIL), F32)
                totals = lax.fori_loop(0, RAIL, add_up, (zero,) * (2 * self.pairs), unroll=4)
                totals = [total + pltpu.roll(total, TAIL, 1) for total in totals]
                for k in range(self.pairs):
                    self.sums[owner * self.pairs + k, r : r + 16] = jnp.where(
                        is_low, totals[2 * k], totals[2 * k + 1]
                    )
            if owner is not self.core:
                self.swap.start()

    def spread(self):
        layer = self.layer
        self.swap.wait_recv()
        total = (self.sums[self.mine] + self.got_sums[layer]).astype(BF)
        self.early[layer] = total[:, :EARLY]
        self.late[layer] = total[:, EARLY:]
        for copy in self.spreads + self.keeps:
            copy.start()

    def relay(self):
        for copy in self.spreads:
            copy.wait_recv()
        for copy in self.keeps:
            copy.wait()
        for copy in self.relays + self.handed[:2]:
            copy.start()

    def hand_over(self):
        for k, copy in enumerate(self.relays):
            copy.wait_recv()
            self.handed[2 + k].start()

    def close(self):
        for copy in self.handed:
            copy.wait_recv()


def encoder_kernel(
    own, patches, prompt_count, classes, reduce,
    task_ids, cls_in, cls_cot, logit_cot, head_bias, attn_bias, out_bias, up_bias, down_bias, gains, shifts,
    final_gain, final_bias,
    patch_hbm, cot_hbm, prompts_hbm, head_hbm, attn_hbm, out_hbm, up_hbm, down_hbm,
    y_out, dx_out, small_out, *rest,
):
    if reduce:
        early_out, late_out, messages_out = rest[:3]
        rest = rest[3:]
    else:
        grads, message = rest[:2]
        rest = rest[2:]
    (
        attn_w, out_w, up_w, down_w, x_ref, t_ref, a_ref, o_ref, wide_ref,
        mixed, qkv, probs, slope, unit1, unit2, inv_ref, unit_t, inv_t, table, prompt_rows,
        patch_own, patch_other, free_sem, y_own, y_other, small,
        weight_sems, local_sems, send_sems, recv_sems,
    ) = rest[:30]
    if reduce:
        grads, message, got, got_messages, match_ref, sums, got_sums, early, late, keep_sems = rest[30:]
    half = patches // 2
    cls_at = patches
    width = x_ref.shape[1]
    hidden = up_w.shape[2]
    queries = own * QUERY
    tasks = head_bias.shape[0]
    core = lax.axis_index("seq")
    me = lax.axis_index("batch")
    first = core * own
    partner = {"seq": 1 - core}
    remote = Copies(send_sems, recv_sems)

    weights = ((attn_hbm, attn_w), (out_hbm, out_w), (up_hbm, up_w), (down_hbm, down_w))

    def weight_copy(k, layer):
        source, target = weights[k]
        return pltpu.make_async_copy(source.at[layer], target.at[layer], weight_sems.at[k, layer])

    def local_copy(k, source, target):
        return pltpu.make_async_copy(source, target, local_sems.at[k])

    dx_ref = x_ref
    head_rows = head_hbm.shape[0]
    take_patches = local_copy(0, patch_hbm, patch_own)
    take_cots = local_copy(1, cot_hbm, patch_own)
    take_table = local_copy(2, prompts_hbm, table)
    take_head = local_copy(3, head_hbm, down_w.at[0, pl.ds(0, head_rows)])
    put_back = local_copy(4, down_hbm.at[0, pl.ds(0, head_rows)], down_w.at[0, pl.ds(0, head_rows)])
    keep_y = local_copy(5, y_own, y_out.at[pl.ds(first, own)])
    keep_small = local_copy(6, small, small_out.at[pl.ds(first, own)])
    swap_patches = remote(patch_hbm, patch_other, partner)
    swap_cots = remote(cot_hbm, patch_other, partner)
    swap_y = remote(y_other, y_out.at[pl.ds(first, own)], partner)
    swap_small = remote(small, small_out.at[pl.ds(first, own)], partner)

    take_patches.start()
    take_table.start()
    weight_copy(0, 0).start()
    barrier = pltpu.get_barrier_semaphore()
    peers = [partner]
    if reduce:
        peers += [{"batch": (me + step) % RAIL} for step in range(1, RAIL)]
    for peer in peers:
        pl.semaphore_signal(barrier, inc=1, device_id=peer, device_id_type=MESH)

    lane = lax.broadcasted_iota(jnp.int32, (1, PAIR), 1)
    is_low = lane < HEAD_DIM
    column = lax.broadcasted_iota(jnp.int32, (1, JOINT), 1)
    is_key = (column <= cls_at) | ((column >= PROMPT_AT) & (column < PROMPT_AT + prompt_count))
    key_bias = jnp.where(is_key, 0.0, -1e30).astype(F32)

    def stack_pair(block):
        zero = jnp.zeros_like(block)
        return jnp.concatenate([jnp.where(is_low, block, zero), jnp.where(is_low, zero, block)], 0)

    def merge_pair(block):
        return jnp.where(is_low, block[:QUERY], block[QUERY:])

    def places(n):
        i, h = n // PAIRS, n % PAIRS
        lanes = [slice(k * width + h * PAIR, k * width + (h + 1) * PAIR) for k in range(3)]
        return slice(i * JOINT, (i + 1) * JOINT), slice(i * QUERY, (i + 1) * QUERY), lanes

    def tails(ref, lanes):
        return jnp.concatenate([ref[i * JOINT + TAIL_AT : (i + 1) * JOINT, lanes] for i in range(own)], 0)

    def own_rows(ref, i):
        values = ref[...].astype(F32)
        return jnp.where(core == 0, values[:, i, :], values[:, own + i, :])

    pl.semaphore_wait(barrier, len(peers))
    swap_patches.start()
    take_patches.wait()
    for i in range(own):
        at = i * JOINT
        x_ref[at + TAIL_AT : at + JOINT] = jnp.zeros((TAIL, width), F32)
        x_ref[at : at + half] = own_rows(patch_own, i)
        x_ref[at + cls_at : at + cls_at + 1] = pick_row(cls_in, first + i)
    take_table.wait()
    for i in range(own):
        entry = table[task_ids[first + i]].astype(F32)
        for layer in range(LAYERS):
            prompt_rows[layer, i] = entry[:, layer, :].astype(BF)
    swap_patches.wait_recv()
    for k in range(1, len(weights)):
        weight_copy(k, 0).start()
    for i in range(own):
        x_ref[i * JOINT + half : i * JOINT + patches] = own_rows(patch_other, i)
    pl.semaphore_signal(free_sem, inc=1, device_id=partner, device_id_type=MESH)

    def forward(layer, carry):
        for i in range(own):
            at = i * JOINT + PROMPT_AT
            x_ref[at : at + prompt_count] = prompt_rows[layer, i].astype(F32)
        gain, shift = gains[layer, 0:1], shifts[layer, 0:1]
        bias = pick_row(attn_bias, layer)

        def norm_first(i, r):
            at, to = i * JOINT + r, i * QUERY + r
            unit, inverse = norm_parts(x_ref[at : at + CHUNK])
            a_ref[at : at + CHUNK] = (unit * gain + shift).astype(BF)
            kept = min(CHUNK, QUERY - r)
            if kept > 0:
                unit1[layer, to : to + kept] = unit[:kept].astype(BF)
                inv_ref[layer, to : to + kept, 0:1] = inverse[:kept]

        def project(i, n):
            rows, part = slice(i * JOINT, (i + 1) * JOINT), slice(n * width, (n + 1) * width)
            qkv[layer, rows, part] = (dot(a_ref[rows], attn_w[layer, :, part], NN) + bias[:, part]).astype(BF)

        def norm_tails():
            turned = tails(x_ref, slice(None)).T
            center = turned - jnp.mean(turned, 0, keepdims=True)
            inverse = lax.rsqrt(jnp.mean(center * center, 0, keepdims=True) + EPSILON)
            unit_t[layer] = (center * inverse).astype(BF)
            inv_t[layer] = inverse

        for r in range(0, JOINT, CHUNK):
            norm_first(0, r)
        weight_copy(0, layer).wait()
        for i in range(own):
            others = [norm_tails]
            if i + 1 < own:
                others = [partial(norm_first, i + 1, r) for r in range(0, JOINT, CHUNK)]
            interleave([partial(project, i, n) for n in range(3)], others)

        def mix(n):
            rows, tokens, lanes = places(n)
            values = qkv[layer, rows, lanes[2]]
            mixed[layer, tokens, lanes[0]] = merge_pair(dot(probs[layer, n], values, NN)).astype(BF)

        gain, shift = gains[layer, 1:2], shifts[layer, 1:2]
        offset = pick_row(out_bias, layer)

        def join_branch(i):
            at, tokens = i * JOINT, slice(i * QUERY, (i + 1) * QUERY)
            t_ref[tokens] = x_ref[at : at + QUERY] + (dot(mixed[layer, tokens], out_w[layer], NN) + offset)

        def norm_second(i, r):
            part = slice(i * QUERY + r, i * QUERY + min(r + CHUNK, QUERY))
            unit, inverse = norm_parts(t_ref[part])
            unit2[layer, part] = unit.astype(BF)
            inv_ref[layer, part, 1:2] = inverse
            a_ref[part] = (unit * gain + shift).astype(BF)

        def norms_second(i):
            return [partial(norm_second, i, r) for r in range(0, QUERY, CHUNK)]

        weight_copy(1, layer).wait()
        for n in range(own * PAIRS):
            rows, _, lanes = places(n)
            query = stack_pair(qkv[layer, rows.start : rows.start + QUERY, lanes[0]])
            scores = dot(query, qkv[layer, rows, lanes[1]], NT) * HEAD_DIM**-0.5 + key_bias
            expo = jnp.exp(scores - jnp.max(scores, -1, keepdims=True))
            probs[layer, n] = (expo * (1.0 / jnp.sum(expo, -1, keepdims=True))).astype(BF)
            if n > 0:
                mix(n - 1)
            if n == PAIRS:
                join_branch(0)
            for other in norms_second(0)[2 * (n - PAIRS - 1) : 2 * (n - PAIRS)] if n > PAIRS else []:
                other()
        mix(own * PAIRS - 1)

        @pl.when(layer == 0)
        def fetch():
            for k in range(len(weights)):
                weight_copy(k, 1).start()
            pl.semaphore_wait(free_sem, 1)
            swap_cots.start()
            take_cots.start()

        def widen(i, c):
            tokens, part = slice(i * QUERY, (i + 1) * QUERY), slice(c, c + HIDDEN_TILE)
            act, act_slope = gelu_and_slope(dot(a_ref[tokens], up_w[layer, :, part], NN) + bias[:, part])
            wide_ref[tokens, part] = act.astype(BF)
            slope[layer, tokens, part] = act_slope.astype(BF)

        def narrow(i):
            at, tokens = i * JOINT, slice(i * QUERY, (i + 1) * QUERY)
            x_ref[at : at + QUERY] = t_ref[tokens] + (dot(wide_ref[tokens], down_w[layer], NN) + offset_down)

        bias = pick_row(up_bias, layer)
        offset_down = pick_row(down_bias, layer)
        join_branch(1)
        weight_copy(2, layer).wait()
        tiles = range(0, hidden, HIDDEN_TILE)
        interleave([partial(widen, 0, c) for c in tiles], norms_second(1))
        weight_copy(3, layer).wait()
        interleave([partial(widen, 1, c) for c in tiles], [partial(narrow, 0)])
        narrow(1)
        return carry

    lax.fori_loop(0, LAYERS, forward, 0)
    take_head.start()

    for i in range(own):
        at = i * JOINT
        y_own[i] = x_ref[at : at + half].astype(BF)
        y_other[i] = x_ref[at + half : at + patches].astype(BF)
    swap_y.start()
    keep_y.start()

    lasts = [x_ref[i * JOINT + cls_at : i * JOINT + cls_at + 1] for i in range(own)]
    swap_cots.wait_recv()
    take_cots.wait()
    for i in range(own):
        to = i * QUERY
        dx_ref[to + TAIL_AT : to + QUERY] = jnp.zeros((QUERY - TAIL_AT, width), F32)
        dx_ref[to : to + half] = own_rows(patch_own, i)
        dx_ref[to + half : to + patches] = own_rows(patch_other, i)
    rows = -(-classes // 8) * 8
    row = lax.broadcasted_iota(jnp.int32, (own * rows, tasks * classes), 0)
    col = lax.broadcasted_iota(jnp.int32, (own * rows, tasks * classes), 1)
    task = jnp.where(row < rows, task_ids[first], task_ids[first + 1])
    pick = jnp.where(row < rows, row, row - rows) * tasks + task == col
    pick = jnp.where(pick, 1.0, 0.0).astype(BF)
    take_head.wait()
    own_head = dot(pick, down_w[0, :head_rows], NN).astype(BF)
    parts = []
    ends = []
    for i in range(own):
        to = i * QUERY
        matrix = own_head[i * rows : (i + 1) * rows]
        unit, inverse = norm_parts(lasts[i])
        feature = (unit * final_gain[...].reshape(1, width) + final_bias[...].reshape(1, width)).astype(BF)
        task = lax.broadcasted_iota(jnp.int32, (tasks, classes), 0) == task_ids[first + i]
        offset = jnp.sum(jnp.where(task, head_bias[...].astype(F32), 0.0), 0, keepdims=True)
        offset = jnp.concatenate([offset, jnp.zeros((1, width - classes), F32)], 1)
        score = dot(jnp.broadcast_to(feature, (16, width)), matrix, NT)[:1]
        score = jnp.concatenate([score, jnp.zeros((1, width - rows), F32)], 1) + offset
        small[i, 0:1] = lasts[i]
        small[i, 1:2] = score
        small[i, 3:8] = jnp.zeros((5, width), F32)
        cot = pick_row(logit_cot, first + i)
        cot = jnp.concatenate([cot, jnp.zeros((1, PAIR - classes), F32)], 1)
        grad = dot(jnp.broadcast_to(cot[:, :rows].astype(BF), (16, rows)), matrix, NN)[:1]
        dx_ref[to + cls_at : to + cls_at + 1] = pick_row(cls_cot, first + i) + norm_back(
            grad, final_gain[...].reshape(1, width), unit, inverse
        )
        parts += [feature.astype(F32)[:, j : j + PAIR] for j in range(0, width, PAIR)]
        ends.append(cot)
    names = jnp.where(is_low, task_ids[first], task_ids[first + 1]).astype(F32)
    message[...] = jnp.concatenate(parts + ends + [names, jnp.zeros((1, PAIR), F32)], 0).astype(BF)
    put_back.start()
    if reduce:
        refs = (grads, got, match_ref, sums, got_sums, early, late, early_out, late_out)
        sums_of = [Reduction(layer, tasks, remote, keep_sems, refs) for layer in range(LAYERS)]
        give_messages = []
        for step in range(1, RAIL):
            give_messages.append(remote(message, got_messages.at[me], {"batch": (me + step) % RAIL}))
        for copy in give_messages:
            copy.start()
        got_messages[me] = message[...]

    def hook(step, at, action):
        if reduce:
            pl.when(step == at)(action)

    def add_last():
        for copy in give_messages:
            copy.wait_recv()
        order = lax.broadcasted_iota(jnp.int32, (tasks, PAIR), 0).astype(F32)
        for s in range(RAIL):
            match = jnp.where(got_messages[s, 14:15].astype(F32) == order, 1.0, 0.0)
            match_ref[s, 0], match_ref[s, 1] = match[: tasks // 2], match[tasks // 2 :]
        sums_of[1].add()

    def spread_last():
        sums_of[1].spread()

    scatter = [sums_of[k].scatter if reduce else None for k in range(LAYERS)]

    def backward(step, carry):
        layer = LAYERS - 1 - step
        pl.when(step == 1)(put_back.wait)
        gain = gains[layer, 1:2]

        def norm_second_back(i, r):
            part = slice(i * QUERY + r, i * QUERY + min(r + CHUNK, QUERY))
            inverse = inv_ref[layer, part, 1:2]
            total = dx_ref[part] + norm_back(t_ref[part], gain, unit2[layer, part].astype(F32), inverse)
            dx_ref[part] = total
            a_ref[part] = total.astype(BF)

        def norms_second_back(i):
            return [partial(norm_second_back, i, r) for r in range(0, QUERY, CHUNK)]

        def mix_back(i):
            tokens = slice(i * QUERY, (i + 1) * QUERY)
            o_ref[tokens] = dot(a_ref[tokens], out_w[layer], NT).astype(BF)

        a_ref[:queries] = dx_ref[:queries].astype(BF)
        for c in range(0, hidden, HIDDEN_TILE):
            part = slice(c, c + HIDDEN_TILE)
            grad = dot(a_ref[:queries], down_w[layer, part], NT)
            wide_ref[:queries, part] = (grad * slope[layer, :, part].astype(F32)).astype(BF)
        t_ref[...] = dot(wide_ref[:queries], up_w[layer], NT)
        hook(step, 1, add_last)
        for other in norms_second_back(0):
            other()
        mix_back(0)
        late_norms = norms_second_back(1)
        def scores_at(n):
            return slice(n * JOINT, (n + 1) * JOINT)

        def key_grad(n):
            rows, _, lanes = places(n)
            query = stack_pair(qkv[layer, rows.start : rows.start + QUERY, lanes[0]])
            grad_key = dot(query, slope[layer, :, scores_at(n)], TN) * HEAD_DIM**-0.5
            wide_ref[rows, lanes[1]] = grad_key.astype(BF).T

        def query_grad(n):
            rows, _, lanes = places(n)
            grad_query = dot(slope[layer, :, scores_at(n)], qkv[layer, rows, lanes[1]], NN) * HEAD_DIM**-0.5
            wide_ref[rows.start : rows.start + QUERY, lanes[0]] = merge_pair(grad_query).astype(BF)

        for n in range(own * PAIRS):
            rows, tokens, lanes = places(n)
            grad = stack_pair(o_ref[tokens, lanes[0]])
            twice = jnp.concatenate([mixed[layer, tokens, lanes[0]]] * 2, 0)
            center = jnp.sum(grad.astype(F32) * twice.astype(F32), -1, keepdims=True)
            grad_prob = dot(grad, qkv[layer, rows, lanes[2]], NT)
            prob = probs[layer, n]
            slope[layer, :, scores_at(n)] = (prob.astype(F32) * (grad_prob - center)).astype(BF)
            wide_ref[rows, lanes[2]] = dot(grad, prob, TN).astype(BF).T
            if n > 0:
                key_grad(n - 1)
            for other in late_norms[2 * n : 2 * n + 2]:
                other()
            if n == PAIRS - 1:
                mix_back(1)
                hook(step, 1, spread_last)
        key_grad(own * PAIRS - 1)
        gain = gains[layer, 0:1]
        gain_t = jnp.broadcast_to(gain, (PAIR, width)).T
        scaled = dot(attn_w[layer, :, width:], tails(wide_ref, slice(width, 3 * width)), NT) * gain_t
        unit = unit_t[layer].astype(F32)
        mean = jnp.mean(scaled, 0, keepdims=True)
        mean_unit = jnp.mean(scaled * unit, 0, keepdims=True)
        grads[layer] = (inv_t[layer] * (scaled - mean - unit * mean_unit)).astype(BF)
        for k in range(LAYERS):
            hook(step, LAYERS - 1 - k, scatter[k])

        def norm_first_back(i, r):
            part = slice(i * QUERY + r, i * QUERY + r + 16)
            inverse = inv_ref[layer, part, 0:1]
            grad = norm_back(t_ref[part], gain, unit1[layer, part].astype(F32), inverse)
            if r + 16 > cls_at:
                keep = lax.broadcasted_iota(jnp.int32, (16, 1), 0) + r <= cls_at
                grad = jnp.where(keep, grad, 0.0)
            dx_ref[part] += grad

        def norms_first_back(i):
            return [partial(norm_first_back, i, r) for r in range(0, QUERY, 16)]

        def project_back(i):
            rows = wide_ref[i * JOINT : i * JOINT + QUERY, : 3 * width]
            t_ref[i * QUERY : (i + 1) * QUERY] = dot(rows, attn_w[layer], NT)

        for n in range(PAIRS):
            query_grad(n)
        project_back(0)
        interleave([partial(query_grad, n) for n in range(PAIRS, own * PAIRS)], norms_first_back(0))
        project_back(1)
        for other in norms_first_back(1):
            other()
        return carry

    lax.fori_loop(0, LAYERS, backward, 0)

    gone = []

    def sent(copies):
        for copy in copies:
            copy.wait_send()
        gone.extend(copies)

    keep_dx, swap_dx = [], []
    padded = dx_out.shape[1]
    for i in range(own):
        to = i * QUERY
        t_ref[to : to + half] = dx_ref[to + half : to + patches]
        small[i, 2:3] = dx_ref[to + cls_at : to + cls_at + 1]
        keep_dx.append(local_copy(7 + i, dx_ref.at[pl.ds(to, padded)], dx_out.at[first + i]))
        swap_dx.append(remote(t_ref.at[pl.ds(to, padded)], dx_out.at[first + i], partner))
        swap_dx[i].start()
        keep_dx[i].start()
    swap_small.start()
    keep_small.start()
    if reduce:
        last, first_layer = sums_of[1], sums_of[0]
        last.relay()
        sent([last.swap])
        first_layer.add()
        swap_messages = remote(got_messages, messages_out.at[core], partner)
        keep_messages = local_copy(7 + own, got_messages, messages_out.at[core])
        swap_messages.start()
        keep_messages.start()
        first_layer.spread()
        last.hand_over()
        sent([swap_patches, swap_cots, swap_y] + give_messages)
        sent(last.scattered + last.spreads + first_layer.scattered + [first_layer.swap])
        first_layer.relay()
        sent([swap_small, swap_messages] + swap_dx + last.relays + last.handed + first_layer.spreads)
        first_layer.hand_over()
        last.close()
        first_layer.close()
        swap_messages.wait_recv()
        keep_messages.wait()
    for copy in [swap_y, swap_small] + swap_dx:
        copy.wait_recv()
    for copy in [keep_y, keep_small] + keep_dx:
        copy.wait()
    sent([copy for copy in remote.made if not any(copy is other for other in gone)])


def run_encoder(
    reduce, task_ids, patch_input, cls_input, patch_cotangent, cls_cotangent, logit_cotangent, prompts, head_weight,
    head_bias, attn_weight, attn_bias, out_weight, out_bias, up_weight, up_bias, down_weight, down_bias,
    gains, shifts, final_gain, final_bias, own,
):
    images, half, width = patch_input.shape
    tasks, classes = head_bias.shape
    prompt_count = prompts.shape[2]
    hidden = up_weight.shape[2]
    queries, joints = own * QUERY, own * JOINT
    lanes = own * TAIL
    pairs = tasks // 4
    share = width // RAIL
    shape = jax.ShapeDtypeStruct
    vmem = pl.BlockSpec(memory_space=pltpu.VMEM)
    anywhere = pl.BlockSpec(memory_space=pl.ANY)
    table = prompts.transpose(0, 2, 1, 3)
    head_rows = head_weight.transpose(2, 1, 0).reshape(-1, width)
    outs = [
        shape((images, half, width), BF),
        shape((images, -(-half // 8) * 8, width), F32),
        shape((images, 8, width), F32),
    ]
    out_specs = [anywhere] * 3
    scratch = [
        pltpu.VMEM(attn_weight.shape, BF),
        pltpu.VMEM(out_weight.shape, BF),
        pltpu.VMEM(up_weight.shape, BF),
        pltpu.VMEM(down_weight.shape, BF),
        pltpu.VMEM((joints, width), F32),
        pltpu.VMEM((queries, width), F32),
        pltpu.VMEM((joints, width), BF),
        pltpu.VMEM((queries, width), BF),
        pltpu.VMEM((joints, hidden), BF),
        pltpu.VMEM((LAYERS, queries, width), BF),
        pltpu.VMEM((LAYERS, joints, 3 * width), BF),
        pltpu.VMEM((LAYERS, own * PAIRS, 2 * QUERY, JOINT), BF),
        pltpu.VMEM((LAYERS, queries, hidden), BF),
        pltpu.VMEM((LAYERS, queries, width), BF),
        pltpu.VMEM((LAYERS, queries, width), BF),
        pltpu.VMEM((LAYERS, queries, 2), F32),
        pltpu.VMEM((LAYERS, width, lanes), BF),
        pltpu.VMEM((LAYERS, 1, lanes), F32),
        pltpu.VMEM(table.shape, BF),
        pltpu.VMEM((LAYERS, own, prompt_count, width), BF),
        pltpu.VMEM((half, images, width), BF),
        pltpu.VMEM((half, images, width), BF),
        pltpu.SemaphoreType.REGULAR,
        pltpu.VMEM((own, half, width), BF),
        pltpu.VMEM((own, half, width), BF),
        pltpu.VMEM((own, 8, width), F32),
        pltpu.SemaphoreType.DMA((4, LAYERS)),
        pltpu.SemaphoreType.DMA((8 + own,)),
    ]
    if reduce:
        steps = 6 * (LINE - 1) + 3
        count = 4 + own + RAIL + LAYERS * (RAIL - 1 + steps)
        outs += [
            shape((LAYERS, 2, LINE, LINE, pairs, EARLY, lanes), BF),
            shape((LAYERS, 2, LINE, LINE, pairs, share - EARLY, lanes), BF),
            shape((2, RAIL, 16, PAIR), BF),
        ]
        out_specs += [anywhere] * 3
        scratch += [
            pltpu.SemaphoreType.DMA((count,)),
            pltpu.SemaphoreType.DMA((count,)),
            pltpu.VMEM((LAYERS, width, lanes), BF),
            pltpu.VMEM((16, PAIR), BF),
            pltpu.VMEM((LAYERS, RAIL, share, lanes), BF),
            pltpu.VMEM((RAIL, 16, PAIR), BF),
            pltpu.VMEM((RAIL, 2, tasks // 2, PAIR), F32),
            pltpu.VMEM((2 * pairs, share, lanes), F32),
            pltpu.VMEM((LAYERS, pairs, share, lanes), F32),
            pltpu.VMEM((LAYERS, pairs, EARLY, lanes), BF),
            pltpu.VMEM((LAYERS, pairs, share - EARLY, lanes), BF),
            pltpu.SemaphoreType.DMA((2 * LAYERS,)),
        ]
    else:
        outs += [shape((LAYERS, width, lanes), BF), shape((16, PAIR), BF)]
        out_specs += [vmem] * 2
        scratch += [pltpu.SemaphoreType.DMA((4 + own,)), pltpu.SemaphoreType.DMA((4 + own,))]

    def kernel(*refs):
        encoder_kernel(own, 2 * half, prompt_count, classes, reduce, *refs)

    return pl.pallas_call(
        kernel,
        out_shape=outs,
        in_specs=[pl.BlockSpec(memory_space=pltpu.SMEM)] + [vmem] * 12 + [anywhere] * 8,
        out_specs=out_specs,
        scratch_shapes=scratch,
        compiler_params=pltpu.CompilerParams(vmem_limit_bytes=64 << 20, collective_id=0, has_side_effects=True),
        name="encoder",
    )(
        task_ids, cls_input, cls_cotangent, logit_cotangent, head_bias, attn_bias, out_bias, up_bias, down_bias,
        gains, shifts, final_gain, final_bias,
        patch_input.transpose(1, 0, 2), patch_cotangent.transpose(1, 0, 2), table, head_rows,
        attn_weight, out_weight, up_weight, down_weight,
    )


def finish_kernel(
    own, prompt_count, early_hbm, late_hbm, messages_hbm, small_hbm, y_hbm, dx_hbm,
    prompt_hbm, head_hbm, bias_hbm, y_cls_hbm, logits_hbm, dx_cls_hbm, y_patch_hbm, dx_patch_hbm,
    early, late, messages, small, y, dx, prompt_grad, head_grad, bias_grad, y_cls, logits, dx_cls, y_patch, dx_patch,
    rows_ref, left_ref, features_ref, sems,
):
    classes, tasks, width = head_grad.shape
    devices = 2 * RAIL
    count = own * devices
    pairs = early.shape[4]
    class_part = classes // FINISH_PARTS
    copies = []

    def copy(source, target):
        copies.append(pltpu.make_async_copy(source, target, sems.at[len(copies)]))
        copies[-1].start()
        return copies[-1]

    take_messages = copy(messages_hbm, messages)
    take_small = copy(small_hbm, small)
    take_dx, take_y = copy(dx_hbm, dx), copy(y_hbm, y)
    takes = []
    for side in range(2):
        for layer in range(LAYERS):
            takes.append(copy(early_hbm.at[layer, side], early.at[layer, side]))
            takes.append(copy(late_hbm.at[layer, side], late.at[layer, side]))
    gives = []

    def gather(k):
        return rows_ref[pl.ds(k, devices, stride=16)]

    take_messages.wait()
    rows_ref[...] = messages[...].astype(F32).reshape(rows_ref.shape)
    chunks = width // PAIR
    for i in range(own):
        for j in range(chunks):
            rows = slice(i * devices, (i + 1) * devices)
            features_ref[rows, j * PAIR : (j + 1) * PAIR] = gather(i * chunks + j).astype(BF)
    cots = jnp.concatenate([gather(own * chunks + i) for i in range(own)], 0)
    ids = gather(own * chunks + own).T
    ids = jnp.concatenate([ids[i * TAIL : i * TAIL + 1] for i in range(own)], 1)
    match = jnp.where(lax.broadcasted_iota(jnp.int32, (tasks, count), 0).astype(F32) == ids, 1.0, 0.0)
    cots_t = cots.T[:classes]
    left_ref[...] = (cots_t[:, None, :] * match[None]).astype(BF)
    for k in range(FINISH_PARTS):
        part = slice(k * class_part, (k + 1) * class_part)
        left = left_ref[part].reshape(class_part * tasks, count)
        head_grad[part] = dot(left, features_ref[...], NN).reshape(class_part, tasks, width)
        gives.append(copy(head_grad.at[part], head_hbm.at[part]))
    total = dot(match.astype(BF), cots.astype(BF), NN)
    bias_grad[...] = total[:, :classes]
    take_small.wait()
    y_cls[...] = small[:, 0, :].astype(BF)
    logits[...] = small[:, 1, : logits.shape[1]].astype(BF)
    dx_cls[...] = small[:, 2, :]
    for source, target in ((bias_grad, bias_hbm), (y_cls, y_cls_hbm), (logits, logits_hbm), (dx_cls, dx_cls_hbm)):
        gives.append(copy(source, target))

    take_dx.wait()
    take_y.wait()
    for i in range(y.shape[0]):
        dx_patch[:, i, :] = dx[i, : y.shape[1]]
        y_patch[:, i, :] = y[i]
    gives.append(copy(dx_patch, dx_patch_hbm))
    gives.append(copy(y_patch, y_patch_hbm))

    row = lax.broadcasted_iota(jnp.int32, (2 * TAIL, 2 * TAIL), 0)
    col = lax.broadcasted_iota(jnp.int32, (2 * TAIL, 2 * TAIL), 1)
    turn = jnp.where(row == col, 1.0, 0.0).astype(BF)
    start = PROMPT_AT - TAIL_AT
    for core in range(2):
        for take in takes[2 * LAYERS * core : 2 * LAYERS * (core + 1)]:
            take.wait()
        for k in range(pairs):
            task = 2 * (core * pairs + k)
            for layer in range(LAYERS):
                blocks = []
                for b in range(RAIL):
                    blocks.append(early[layer, core, b // LINE, b % LINE, k])
                    blocks.append(late[layer, core, b // LINE, b % LINE, k])
                both = dot(turn, jnp.concatenate(blocks, 0), NT)
                for side in range(2):
                    at = side * TAIL + start
                    prompt_grad[task + side, :, layer, :] = both[at : at + prompt_count]
            part = slice(task, task + 2)
            gives.append(copy(prompt_grad.at[part], prompt_hbm.at[part]))
    for give in gives:
        give.wait()


def run_finish(early, late, messages, small, y, dx, prompt_count, class_count, own):
    layers, cores, _, _, pairs, _, lanes = early.shape
    width = RAIL * (early.shape[5] + late.shape[5])
    tasks = 2 * cores * pairs
    images, half = y.shape[:2]
    shape = jax.ShapeDtypeStruct
    vmem = pl.BlockSpec(memory_space=pltpu.VMEM)
    anywhere = pl.BlockSpec(memory_space=pl.ANY)
    prompt_shape, head_shape = (tasks, prompt_count, layers, width), (class_count, tasks, width)
    patch_shape = (half, images, width)

    def kernel(*refs):
        finish_kernel(own, prompt_count, *refs)

    return pl.pallas_call(
        kernel,
        out_shape=(
            shape(prompt_shape, F32),
            shape(head_shape, F32),
            shape((tasks, class_count), F32),
            shape((images, width), BF),
            shape((images, class_count), BF),
            shape((images, width), F32),
            shape(patch_shape, BF),
            shape(patch_shape, F32),
        ),
        in_specs=[anywhere] * 6,
        out_specs=[anywhere] * 8,
        scratch_shapes=[
            pltpu.VMEM(early.shape, BF),
            pltpu.VMEM(late.shape, BF),
            pltpu.VMEM(messages.shape, BF),
            pltpu.VMEM(small.shape, F32),
            pltpu.VMEM(y.shape, BF),
            pltpu.VMEM(dx.shape, F32),
            pltpu.VMEM(prompt_shape, F32),
            pltpu.VMEM(head_shape, F32),
            pltpu.VMEM((tasks, class_count), F32),
            pltpu.VMEM((images, width), BF),
            pltpu.VMEM((images, class_count), BF),
            pltpu.VMEM((images, width), F32),
            pltpu.VMEM(patch_shape, BF),
            pltpu.VMEM(patch_shape, F32),
            pltpu.VMEM((2 * RAIL * 16, PAIR), F32),
            pltpu.VMEM((class_count, tasks, own * 2 * RAIL), BF),
            pltpu.VMEM((own * 2 * RAIL, width), BF),
            pltpu.SemaphoreType.DMA((8 + 4 * layers + FINISH_PARTS + 2 + cores * pairs,)),
        ],
        compiler_params=pltpu.CompilerParams(vmem_limit_bytes=62 << 20),
        name="finish",
    )(early, late, messages, small, y, dx)


def gathered_sums(grads, message, own_ids, task_ids, logit_cot, prompt_count, tasks):
    layers, width, lanes = grads.shape
    own = own_ids.shape[0]
    start = PROMPT_AT - TAIL_AT
    parts = grads.reshape(layers, width, own, TAIL)[..., start : start + prompt_count].astype(F32)
    names = jnp.arange(tasks, dtype=jnp.int32)[None, :]
    onehot = (own_ids[:, None] == names).astype(F32)
    dense = jnp.einsum("it,ldip->tlpd", onehot, parts, precision=lax.Precision.HIGHEST)
    prompt_grad = lax.psum(dense, ("batch", "seq"))
    features = message[: own * width // PAIR].reshape(own, width)
    features = lax.all_gather(features, ("batch", "seq"), axis=0, tiled=True)
    cots = lax.all_gather(logit_cot, "batch", axis=0, tiled=True)
    ids = lax.all_gather(task_ids.astype(F32), "batch", axis=0, tiled=True).astype(jnp.int32)
    match = (ids[:, None] == names).astype(BF)
    head_grad = jnp.einsum("id,it,ic->dtc", features, match, cots, preferred_element_type=F32)
    bias_grad = jnp.einsum("it,ic->tc", match, cots, preferred_element_type=F32)
    return prompt_grad, head_grad, bias_grad


def per_device(
    cls_input, patch_input, task_ids, prompts, attn_weight, attn_bias, out_weight, out_bias, up_weight, up_bias,
    down_weight, down_bias, norm_gain, norm_bias, final_gain, final_bias, head_weight, head_bias,
    cls_cotangent, patch_cotangent, logit_cotangent,
):
    cores = lax.axis_size("seq")
    core = lax.axis_index("seq")
    images, width = cls_input.shape
    own = images // cores
    tasks, class_count = head_bias.shape
    prompt_count = prompts.shape[2]
    reduce = lax.axis_size("batch") == RAIL
    y, dx, small, *sums = run_encoder(
        reduce, task_ids, patch_input, cls_input, patch_cotangent, cls_cotangent, logit_cotangent, prompts,
        head_weight, head_bias, attn_weight, attn_bias, out_weight, out_bias, up_weight, up_bias,
        down_weight, down_bias, norm_gain, norm_bias, final_gain, final_bias, own,
    )
    if reduce:
        prompt_grad, head_grad, bias_grad, y_cls, logits, dx_cls, y, dx = run_finish(
            *sums, small, y, dx, prompt_count, class_count, own
        )
        prompt_grad = prompt_grad.transpose(0, 2, 1, 3)
        head_grad = head_grad.transpose(2, 1, 0)
        y, dx = y.transpose(1, 0, 2), dx.transpose(1, 0, 2)
    else:
        own_ids = lax.dynamic_slice_in_dim(task_ids, core * own, own, 0)
        prompt_grad, head_grad, bias_grad = gathered_sums(
            *sums, own_ids, task_ids, logit_cotangent, prompt_count, tasks
        )
        y_cls, logits, dx_cls = small[:, 0].astype(BF), small[:, 1, :class_count].astype(BF), small[:, 2]
        dx = dx[:, : patch_input.shape[1]]
    return y_cls, y, logits, dx_cls, dx, prompt_grad, head_grad, bias_grad


def solution(mesh):
    rows, tokens, whole = P("batch", None), P("batch", "seq", None), P()
    return jax.shard_map(
        per_device,
        mesh=mesh,
        in_specs=(rows, tokens, P("batch")) + (whole,) * 15 + (rows, tokens, rows),
        out_specs=(rows, tokens, rows, rows, tokens, whole, whole, whole),
        check_vma=False,
    )
```
